128 devices in a mesh: row: 8 (over x, z_hi), col: 16 (over z_lo, y, core).
Axes of the slice: x: 4, y: 4, z: 4 (z_hi: 2, z_lo: 2; z = z_hi * 2 + z_lo), core: 2. Of those that a mesh axis runs over, the one named last changes fastest.
Arguments:
- tokens: bfloat16 [128, 384, 256], P('row', 'col'), may hold values from -6 to 6
- grad_fine: bfloat16 [128, 384, 256], P('row', 'col'), may hold values from -6 to 6
- grad_coarse: bfloat16 [32, 96, 1024], P('row', 'col'), may hold values from -6 to 6
- fine_gain: float32 [256], replicated, may hold values from 0.25 to 1.75
- fine_qkv: bfloat16 [256, 768], replicated, may hold values from -2 to 2
- fine_out: bfloat16 [256, 256], replicated, may hold values from -0.375 to 0.375
- merge_weight: bfloat16 [4096, 1024], replicated, may hold values from -0.09375 to 0.09375
- coarse_gain: float32 [1024], replicated, may hold values from 0.4 to 2.5
- coarse_qkv: bfloat16 [1024, 3072], replicated, may hold values from -1 to 1
- coarse_out: bfloat16 [1024, 1024], replicated, may hold values from -0.1875 to 0.1875
Outputs:
- grad_tokens: bfloat16 [128, 384, 256], P('row', 'col')
- grad_fine_qkv: float32 [256, 768], P('row', 'col')
- grad_fine_out: float32 [256, 256], P('row', 'col')
The draws below stay inside these ranges and needn't reach their ends.
All inputs are finite; a program needn't handle non-finite values.
Results may differ from the reference program's by a relative error of at most 0.04.
Values may be sent and summed in bfloat16 or wider, within the bound.
No kernel may reach another device: no remote copies, remote signals or barrier semaphores. Data moves between devices by JAX's collectives and lax.ppermute only.
A program may use at most 128 MiB of HBM per device.

```python
import math
import jax
import jax.numpy as jnp
from jax import lax

D0 = 256
H0 = 4
D1 = 1024
H1 = 16
HEAD = 64
RADIUS = 3
MERGE = 4
NR = 128
NC = 384


def draw_fine_qkv(key, part):
    key = jax.random.fold_in(key, 11)
    key_query, key_key, key_value = jax.random.split(key, 3)
    scaling = D0 ** (-0.5)
    query_part = jax.random.truncated_normal(key_query, -4.0, 4.0, (D0, D0), jnp.float32) * scaling
    value_part = jax.random.truncated_normal(key_value, -4.0, 4.0, (D0, D0), jnp.float32) * scaling
    key_part = jax.random.truncated_normal(key_key, -4.0, 4.0, (D0, D0), jnp.float32) * scaling
    return jnp.concatenate([query_part, key_part, value_part], axis=1).astype(jnp.bfloat16)


def draw_coarse_qkv(key, part):
    key = jax.random.fold_in(key, 12)
    key_query, key_key, key_value = jax.random.split(key, 3)
    scaling = D1 ** (-0.5)
    query_part = jax.random.truncated_normal(key_query, -4.0, 4.0, (D1, H1, HEAD), jnp.float32) * scaling
    value_part = jax.random.truncated_normal(key_value, -4.0, 4.0, (D1, H1, HEAD), jnp.float32) * scaling
    key_part = jax.random.truncated_normal(key_key, -4.0, 4.0, (D1, H1, HEAD), jnp.float32) * scaling
    return jnp.stack([query_part, key_part, value_part], axis=2).reshape(D1, 3 * D1).astype(jnp.bfloat16)


def block_scale(key, shape, shards, least, high):
    def one(position, blocks):
        heights = jax.random.uniform(jax.random.fold_in(jax.random.fold_in(key, 6), position), (blocks,), jnp.float32, least / len(shards), high / len(shards))
        return jnp.repeat(jnp.exp(heights), shape[position] // blocks).reshape((-1,) + (1,) * (len(shape) - position - 1))

    level = one(*shards[0])
    for cut in shards[1:]:
        level = level * one(*cut)
    return level


def normal_values(own_key, shape, scale, limit, cuts=(), held_as=jnp.bfloat16):
    loudness = block_scale(own_key, shape, cuts, -0.22, 0.18) if cuts else 1.0
    values = jax.random.normal(own_key, shape, jnp.float32) * scale * loudness
    return jnp.minimum(jnp.maximum(values, -limit), limit).astype(held_as)


def setup_inputs(seed: int = 0) -> dict:
    key_of = jax.random.split(jax.random.key(seed), 11)
    return {
        "tokens": normal_values(key_of[0], (NR, NC, D0), 1.0, 6.0, ((0, 8), (1, 16))),
        "grad_fine": normal_values(key_of[1], (NR, NC, D0), 1.0, 6.0, ((0, 8), (1, 16))),
        "grad_coarse": normal_values(key_of[2], (NR // 4, NC // 4, D1), 1.0, 6.0, ((0, 8), (1, 16))),
        "fine_gain": jnp.clip(1.0 + 0.15 * jax.random.normal(key_of[3], (D0,), jnp.float32), 0.25, 1.75),
        "fine_qkv": draw_fine_qkv(jax.random.fold_in(key_of[10], 71), 0),
        "fine_out": normal_values(key_of[5], (D0, D0), D0 ** -0.5, 0.375),
        "merge_weight": normal_values(key_of[6], (16 * D0, D1), (16 * D0) ** -0.5, 0.09375),
        "coarse_gain": jnp.clip(jnp.exp(jax.random.uniform(key_of[7], (D1,), jnp.float32, math.log(0.4), math.log(2.5))), 0.4, 2.5),
        "coarse_qkv": draw_coarse_qkv(jax.random.fold_in(key_of[10], 71), 0),
        "coarse_out": normal_values(key_of[9], (D1, D1), D1 ** -0.5, 0.1875),
    }


EPSILON = 1e-05

def norm_forward(values):
    values = values.astype(jnp.float32)
    center = values - lax.optimization_barrier(jnp.mean(values, axis=-1, keepdims=True))
    inverse = lax.rsqrt(lax.optimization_barrier(jnp.mean(center * center, axis=-1, keepdims=True)) + EPSILON)
    return (center * inverse, inverse)

def norm_backward(upstream, gain_vector, normed, inverse):
    scaled = upstream * gain_vector
    return inverse * (scaled - lax.optimization_barrier(jnp.mean(scaled, axis=-1, keepdims=True)) - normed * lax.optimization_barrier(jnp.mean(scaled * normed, axis=-1, keepdims=True)))

def head_sum(product, head_count):
    dims = product.shape
    return lax.optimization_barrier(jnp.sum(product.reshape(dims[:-1] + (head_count, dims[-1] // head_count)), axis=-1))

def merge_blocks(values):
    row_count, col_count, features = values.shape
    blocks = values.reshape(row_count // MERGE, MERGE, col_count // MERGE, MERGE, features)
    return blocks.transpose(0, 2, 1, 3, 4).reshape(row_count // MERGE * (col_count // MERGE), MERGE * MERGE * features)

def unmerge_blocks(flat_values, row_count, col_count):
    features = flat_values.shape[-1] // (MERGE * MERGE)
    blocks = flat_values.reshape(row_count // MERGE, col_count // MERGE, MERGE, MERGE, features)
    return blocks.transpose(0, 2, 1, 3, 4).reshape(row_count, col_count, features)

def window_mask(row_count, col_count, inside):
    ext_cols = col_count + 2 * RADIUS
    query_index = jnp.arange(row_count * col_count, dtype=jnp.int32)
    key_index = jnp.arange((row_count + 2 * RADIUS) * ext_cols, dtype=jnp.int32)
    row_gap = (key_index // ext_cols)[None, :] - (query_index // col_count)[:, None]
    col_gap = (key_index % ext_cols)[None, :] - (query_index % col_count)[:, None]
    near = (row_gap >= 0) & (row_gap <= 2 * RADIUS) & (col_gap >= 0) & (col_gap <= 2 * RADIUS)
    return near & inside.reshape(-1)[None, :]

def split_heads(values):
    return values.reshape(-1, H0, values.shape[-1] // H0).astype(jnp.float32)

def window_forward(queries, keyval, inside):
    row_count, col_count, features = queries.shape
    scaling = (features // H0) ** (-0.5)
    allowed = window_mask(row_count, col_count, inside)[None]
    query_heads = split_heads(queries)
    key_heads = split_heads(keyval[..., :features])
    value_heads = split_heads(keyval[..., features:])
    scores = jnp.where(allowed, jnp.einsum('qhe,khe->hqk', query_heads, key_heads) * scaling, -1e+30)
    maxima = lax.optimization_barrier(jnp.max(scores, axis=-1, keepdims=True))
    exponent = jnp.exp(scores - maxima)
    totals = lax.optimization_barrier(jnp.sum(exponent, axis=-1, keepdims=True))
    soft_weights = lax.optimization_barrier((exponent / totals).astype(jnp.bfloat16))
    output = jnp.einsum('hqk,khe->qhe', soft_weights.astype(jnp.float32), value_heads).reshape(row_count, col_count, features)
    return (output, jnp.transpose((maxima + jnp.log(totals))[..., 0]).reshape(row_count, col_count, H0))

def window_grad_query(queries, keyval, inside, log_total, grad_stat, grad_att):
    row_count, col_count, features = queries.shape
    scaling = (features // H0) ** (-0.5)
    allowed = window_mask(row_count, col_count, inside)[None]
    query_heads = split_heads(queries)
    key_heads = split_heads(keyval[..., :features])
    value_heads = split_heads(keyval[..., features:])
    grad_split = split_heads(grad_att)
    scores = jnp.einsum('qhe,khe->hqk', query_heads, key_heads) * scaling
    total_t = jnp.transpose(log_total.reshape(-1, H0))[..., None]
    stat_t = jnp.transpose(grad_stat.reshape(-1, H0))[..., None]
    soft_weights = jnp.exp(jnp.where(allowed, scores - total_t, -1e+30))
    grad_p = jnp.einsum('qhe,khe->hqk', grad_split, value_heads)
    slopes = lax.optimization_barrier((soft_weights * (grad_p - stat_t)).astype(jnp.bfloat16))
    result = jnp.einsum('hqk,khe->qhe', slopes.astype(jnp.float32), key_heads) * scaling
    return result.reshape(row_count, col_count, features)

def window_grad_keys(keyval, query_ext, stats_ext, inside):
    row_count, col_count, twice = keyval.shape
    features = twice // 2
    scaling = (features // H0) ** (-0.5)
    allowed = window_mask(row_count, col_count, inside)[None]
    key_heads = split_heads(keyval[..., :features])
    value_heads = split_heads(keyval[..., features:])
    query_heads = split_heads(query_ext[..., :features])
    grad_split = split_heads(query_ext[..., features:])
    total_t = jnp.transpose(stats_ext[..., :H0].reshape(-1, H0))[:, None, :]
    stat_t = jnp.transpose(stats_ext[..., H0:].reshape(-1, H0))[:, None, :]
    scores = jnp.einsum('khe,qhe->hkq', key_heads, query_heads) * scaling
    soft_weights = jnp.exp(jnp.where(allowed, scores - total_t, -1e+30))
    grad_p = jnp.einsum('khe,qhe->hkq', value_heads, grad_split)
    slopes = lax.optimization_barrier((soft_weights * (grad_p - stat_t)).astype(jnp.bfloat16))
    weights_low = lax.optimization_barrier(soft_weights.astype(jnp.bfloat16))
    key_grad = jnp.einsum('hkq,qhe->khe', slopes.astype(jnp.float32), query_heads) * scaling
    value_grad = jnp.einsum('hkq,qhe->khe', weights_low.astype(jnp.float32), grad_split)
    return (key_grad.reshape(row_count, col_count, features), value_grad.reshape(row_count, col_count, features))

def over_tiles(function, plain, extended):
    side = math.gcd(math.gcd(NR, NC), 8)
    rows = NR // side
    cols = NC // side

    def one_tile(index):
        index = index.astype(jnp.int32)
        row_start = (index // cols * side).astype(jnp.int32)
        col_start = (index % cols * side).astype(jnp.int32)
        zero_start = jnp.zeros((), jnp.int32)
        plain_parts = [lax.dynamic_slice(array, (row_start, col_start) + (zero_start,) * (array.ndim - 2), (side, side) + array.shape[2:]) for array in plain]
        ext_parts = [lax.dynamic_slice(array, (row_start, col_start) + (zero_start,) * (array.ndim - 2), (side + 2 * RADIUS, side + 2 * RADIUS) + array.shape[2:]) for array in extended]
        return function(*plain_parts, *ext_parts)
    results = lax.map(one_tile, jnp.arange(rows * cols, dtype=jnp.int32))
    return jax.tree.map(lambda piece: piece.reshape((rows, cols, side, side, piece.shape[-1])).transpose(0, 2, 1, 3, 4).reshape(NR, NC, piece.shape[-1]), results)

def block_size(row_total):
    return row_total if row_total <= 1024 else math.gcd(row_total, 1024)

def global_forward(queries, key_rows, value_rows):
    row_total, head_count, head_size = queries.shape
    block_rows = block_size(row_total)
    scaling = head_size ** (-0.5)
    key_f = key_rows.astype(jnp.float32)
    value_f = value_rows.astype(jnp.float32)

    def one_block(query_block):
        scores = jnp.einsum('qhe,khe->hqk', query_block.astype(jnp.float32), key_f) * scaling
        maxima = lax.optimization_barrier(jnp.max(scores, axis=-1, keepdims=True))
        exponent = jnp.exp(scores - maxima)
        totals = lax.optimization_barrier(jnp.sum(exponent, axis=-1, keepdims=True))
        soft_weights = lax.optimization_barrier((exponent / totals).astype(jnp.bfloat16))
        output = jnp.einsum('hqk,khe->qhe', soft_weights.astype(jnp.float32), value_f).astype(jnp.bfloat16)
        return (output, jnp.transpose((maxima + jnp.log(totals))[..., 0]))
    outputs, log_total = lax.map(one_block, queries.reshape(row_total // block_rows, block_rows, head_count, head_size))
    return (outputs.reshape(row_total, head_count, head_size), log_total.reshape(row_total, head_count))

def global_grad_query(queries, grad_att, log_total, grad_stat, key_rows, value_rows):
    row_total, head_count, head_size = queries.shape
    block_rows = block_size(row_total)
    scaling = head_size ** (-0.5)
    key_f = key_rows.astype(jnp.float32)
    value_f = value_rows.astype(jnp.float32)

    def one_block(pieces):
        query_block, grad_block, total_block, stat_block = pieces
        scores = jnp.einsum('qhe,khe->hqk', query_block.astype(jnp.float32), key_f) * scaling
        soft_weights = jnp.exp(scores - jnp.transpose(total_block)[..., None])
        grad_p = jnp.einsum('qhe,khe->hqk', grad_block.astype(jnp.float32), value_f)
        slopes = lax.optimization_barrier((soft_weights * (grad_p - jnp.transpose(stat_block)[..., None])).astype(jnp.bfloat16))
        return jnp.einsum('hqk,khe->qhe', slopes.astype(jnp.float32), key_f) * scaling
    split = row_total // block_rows
    result = lax.map(one_block, (queries.reshape(split, block_rows, head_count, head_size), grad_att.reshape(split, block_rows, head_count, head_size), log_total.reshape(split, block_rows, head_count), grad_stat.reshape(split, block_rows, head_count)))
    return result.reshape(row_total, head_count, head_size)

def global_grad_keys(key_rows, value_rows, queries, grad_att, log_total, grad_stat):
    row_total, head_count, head_size = queries.shape
    block_rows = block_size(row_total)
    scaling = head_size ** (-0.5)
    key_f = key_rows.astype(jnp.float32)
    value_f = value_rows.astype(jnp.float32)

    def one_block(running, pieces):
        query_block, grad_block, total_block, stat_block = pieces
        query_f = query_block.astype(jnp.float32)
        grad_f = grad_block.astype(jnp.float32)
        scores = jnp.einsum('qhe,khe->hqk', query_f, key_f) * scaling
        soft_weights = jnp.exp(scores - jnp.transpose(total_block)[..., None])
        grad_p = jnp.einsum('qhe,khe->hqk', grad_f, value_f)
        slopes = lax.optimization_barrier((soft_weights * (grad_p - jnp.transpose(stat_block)[..., None])).astype(jnp.bfloat16))
        weights_low = lax.optimization_barrier(soft_weights.astype(jnp.bfloat16))
        key_grad = jnp.einsum('hqk,qhe->khe', slopes.astype(jnp.float32), query_f)
        value_grad = jnp.einsum('hqk,qhe->khe', weights_low.astype(jnp.float32), grad_f)
        return ((running[0] + key_grad, running[1] + value_grad), None)
    split = row_total // block_rows
    zero_grads = jnp.zeros(key_rows.shape, jnp.float32)
    pieces = (queries.reshape(split, block_rows, head_count, head_size), grad_att.reshape(split, block_rows, head_count, head_size), log_total.reshape(split, block_rows, head_count), grad_stat.reshape(split, block_rows, head_count))
    (key_grad, value_grad), _ = lax.scan(one_block, (zero_grads, zero_grads), pieces)
    return (key_grad * scaling, value_grad)

def reference(tokens, grad_fine, grad_coarse, fine_gain, fine_qkv, fine_out, merge_weight, coarse_gain, coarse_qkv, coarse_out):
    normed_f, inverse_f = norm_forward(tokens)
    normed_fine = (normed_f * fine_gain).astype(jnp.bfloat16)
    qkv_fine = jnp.dot(normed_fine.reshape(-1, D0), fine_qkv, preferred_element_type=jnp.float32).astype(jnp.bfloat16).reshape(NR, NC, 3 * D0)
    query_fine = qkv_fine[..., :D0]
    keyval_fine = qkv_fine[..., D0:]
    padding = ((RADIUS, RADIUS), (RADIUS, RADIUS), (0, 0))
    keyval_ext = jnp.pad(keyval_fine, padding)
    inside = jnp.pad(jnp.ones((NR, NC), jnp.bool_), RADIUS)
    attended_f, lse_fine = over_tiles(window_forward, [query_fine], [keyval_ext, inside])
    attended_fine = attended_f.astype(jnp.bfloat16)
    projected = jnp.dot(attended_fine.reshape(-1, D0), fine_out, preferred_element_type=jnp.float32).reshape(NR, NC, D0)
    hidden = (tokens.astype(jnp.float32) + projected).astype(jnp.bfloat16)
    merged = merge_blocks(hidden)
    coarse = jnp.dot(merged, merge_weight, preferred_element_type=jnp.float32).astype(jnp.bfloat16)
    normed_c, inverse_c = norm_forward(coarse)
    normed_coarse = (normed_c * coarse_gain).astype(jnp.bfloat16)
    qkv_coarse = jnp.dot(normed_coarse, coarse_qkv, preferred_element_type=jnp.float32).astype(jnp.bfloat16).reshape(-1, H1, 3, HEAD)
    query_c = qkv_coarse[:, :, 0]
    key_c = qkv_coarse[:, :, 1]
    value_c = qkv_coarse[:, :, 2]
    attended_coarse, lse_coarse = global_forward(query_c, key_c, value_c)
    grad_flat = grad_coarse.reshape(-1, D1)
    grad_att_c = jnp.dot(grad_flat, coarse_out.T, preferred_element_type=jnp.float32).astype(jnp.bfloat16).reshape(-1, H1, HEAD)
    stat_coarse = lax.optimization_barrier(jnp.sum(grad_att_c.astype(jnp.float32) * attended_coarse.astype(jnp.float32), axis=-1))
    query_grad = global_grad_query(query_c, grad_att_c, lse_coarse, stat_coarse, key_c, value_c)
    token_total = query_c.shape[0]
    block_rows = block_size(token_total)

    def key_block(pieces):
        return global_grad_keys(pieces[0], pieces[1], query_c, grad_att_c, lse_coarse, stat_coarse)
    key_grad, value_grad = lax.map(key_block, (key_c.reshape(token_total // block_rows, block_rows, H1, HEAD), value_c.reshape(token_total // block_rows, block_rows, H1, HEAD)))
    key_grad = key_grad.reshape(token_total, H1, HEAD)
    value_grad = value_grad.reshape(token_total, H1, HEAD)
    qkv_grad_c = jnp.stack([query_grad, key_grad, value_grad], axis=2).astype(jnp.bfloat16).reshape(token_total, 3 * D1)
    upstream_c = jnp.dot(qkv_grad_c, coarse_qkv.T, preferred_element_type=jnp.float32)
    coarse_total = (grad_flat.astype(jnp.float32) + norm_backward(upstream_c, coarse_gain, normed_c, inverse_c)).astype(jnp.bfloat16)
    spread_back = unmerge_blocks(jnp.dot(coarse_total, merge_weight.T, preferred_element_type=jnp.float32), NR, NC)
    grad_hidden = (grad_fine.astype(jnp.float32) + spread_back).astype(jnp.bfloat16)
    flat_hidden = grad_hidden.reshape(-1, D0)
    grad_fine_out = jnp.dot(attended_fine.reshape(-1, D0).T, flat_hidden, preferred_element_type=jnp.float32)
    grad_att_f = jnp.dot(flat_hidden, fine_out.T, preferred_element_type=jnp.float32).astype(jnp.bfloat16).reshape(NR, NC, D0)
    stat_fine = head_sum(grad_att_f.astype(jnp.float32) * attended_fine.astype(jnp.float32), H0)

    def query_side(queries, log_total, grad_stat, grad_att, keyval, mask_part):
        return window_grad_query(queries, keyval, mask_part, log_total, grad_stat, grad_att)
    query_grad_f = over_tiles(query_side, [query_fine, lse_fine, stat_fine, grad_att_f], [keyval_ext, inside])
    query_ext = jnp.pad(jnp.concatenate([query_fine, grad_att_f], axis=-1), padding)
    stats_ext = jnp.pad(jnp.concatenate([lse_fine, stat_fine], axis=-1), padding)
    key_grad_f, value_grad_f = over_tiles(window_grad_keys, [keyval_fine], [query_ext, stats_ext, inside])
    qkv_grad_f = jnp.concatenate([query_grad_f, key_grad_f, value_grad_f], axis=-1).astype(jnp.bfloat16).reshape(-1, 3 * D0)
    grad_fine_qkv = jnp.dot(normed_fine.reshape(-1, D0).T, qkv_grad_f, preferred_element_type=jnp.float32)
    upstream_f = jnp.dot(qkv_grad_f, fine_qkv.T, preferred_element_type=jnp.float32).reshape(NR, NC, D0)
    grad_tokens = (grad_hidden.astype(jnp.float32) + norm_backward(upstream_f, fine_gain, normed_f, inverse_f)).astype(jnp.bfloat16)
    return (grad_tokens, grad_fine_qkv, grad_fine_out)
```

```python
import math

import jax
import jax.numpy as jnp
from jax import lax
from jax.sharding import PartitionSpec as P

H0 = 4
D1 = 1024
H1 = 16
HEAD = 64
RADIUS = 3
MERGE = 4


EPSILON = 1e-05


def with_halo(array, sides, width):
    for axis, dim in sides:
        devices, length = (lax.axis_size(axis), array.shape[dim])
        up = [(i, (i + 1) % devices) for i in range(devices - 1)]
        down = [(j, i) for i, j in up]
        last = lax.slice_in_dim(array, length - width, length, axis=dim)
        first = lax.slice_in_dim(array, 0, width, axis=dim)
        before = lax.ppermute(last, axis, up)
        after = lax.ppermute(first, axis, down)
        array = jnp.concatenate([before, array, after], axis=dim)
    return array


def norm_forward(values):
    values = values.astype(jnp.float32)
    center = values - jnp.mean(values, axis=-1, keepdims=True)
    inverse = lax.rsqrt(jnp.mean(center * center, axis=-1, keepdims=True) + EPSILON)
    return (center * inverse, inverse)


def norm_backward(upstream, gain_vector, normed, inverse):
    scaled = upstream * gain_vector
    return inverse * (
        scaled
        - jnp.mean(scaled, axis=-1, keepdims=True)
        - normed * jnp.mean(scaled * normed, axis=-1, keepdims=True)
    )


def head_sum(product, head_count):
    dims = product.shape
    return jnp.sum(product.reshape(dims[:-1] + (head_count, dims[-1] // head_count)), axis=-1)


def merge_blocks(values):
    row_count, col_count, features = values.shape
    blocks = values.reshape(row_count // MERGE, MERGE, col_count // MERGE, MERGE, features)
    return blocks.transpose(0, 2, 1, 3, 4).reshape(
        row_count // MERGE * (col_count // MERGE), MERGE * MERGE * features
    )


def unmerge_blocks(flat_values, row_count, col_count):
    features = flat_values.shape[-1] // (MERGE * MERGE)
    blocks = flat_values.reshape(row_count // MERGE, col_count // MERGE, MERGE, MERGE, features)
    return blocks.transpose(0, 2, 1, 3, 4).reshape(row_count, col_count, features)


def device_blocks(matrix, row_devices, col_devices):
    row_total, col_total = matrix.shape
    blocks = matrix.reshape(
        row_devices, row_total // row_devices, col_devices, col_total // col_devices
    )
    return blocks.transpose(0, 2, 1, 3).reshape(row_devices * col_devices, -1, 128)


def window_mask(row_count, col_count, inside):
    ext_cols = col_count + 2 * RADIUS
    query_index = jnp.arange(row_count * col_count, dtype=jnp.int32)
    key_index = jnp.arange((row_count + 2 * RADIUS) * ext_cols, dtype=jnp.int32)
    row_gap = (key_index // ext_cols)[None, :] - (query_index // col_count)[:, None]
    col_gap = (key_index % ext_cols)[None, :] - (query_index % col_count)[:, None]
    near = (row_gap >= 0) & (row_gap <= 2 * RADIUS) & (col_gap >= 0) & (col_gap <= 2 * RADIUS)
    return near & inside.reshape(-1)[None, :]


def split_heads(values):
    return values.reshape(-1, H0, values.shape[-1] // H0)


def window_forward(queries, keyval, inside):
    row_count, col_count, features = queries.shape
    scaling = (features // H0) ** (-0.5)
    allowed = window_mask(row_count, col_count, inside)[None]
    query_heads = split_heads(queries)
    key_heads = split_heads(keyval[..., :features])
    value_heads = split_heads(keyval[..., features:])
    scores = jnp.where(
        allowed,
        jnp.einsum("qhe,khe->hqk", query_heads, key_heads, preferred_element_type=jnp.float32)
        * scaling,
        -1e30,
    )
    maxima = jnp.max(scores, axis=-1, keepdims=True)
    exponent = jnp.exp(scores - maxima)
    totals = jnp.sum(exponent, axis=-1, keepdims=True)
    soft_weights = (exponent / totals).astype(jnp.bfloat16)
    output = jnp.einsum(
        "hqk,khe->qhe", soft_weights, value_heads, preferred_element_type=jnp.float32
    ).reshape(row_count, col_count, features)
    return (
        output,
        jnp.transpose((maxima + jnp.log(totals))[..., 0]).reshape(row_count, col_count, H0),
    )


def window_grad_query(queries, keyval, inside, log_total, grad_stat, grad_att):
    row_count, col_count, features = queries.shape
    scaling = (features // H0) ** (-0.5)
    allowed = window_mask(row_count, col_count, inside)[None]
    query_heads = split_heads(queries)
    key_heads = split_heads(keyval[..., :features])
    value_heads = split_heads(keyval[..., features:])
    grad_split = split_heads(grad_att)
    scores = (
        jnp.einsum("qhe,khe->hqk", query_heads, key_heads, preferred_element_type=jnp.float32)
        * scaling
    )
    total_t = jnp.transpose(log_total.reshape(-1, H0))[..., None]
    stat_t = jnp.transpose(grad_stat.reshape(-1, H0))[..., None]
    soft_weights = jnp.exp(jnp.where(allowed, scores - total_t, -1e30))
    grad_p = jnp.einsum("qhe,khe->hqk", grad_split, value_heads, preferred_element_type=jnp.float32)
    slopes = (soft_weights * (grad_p - stat_t)).astype(jnp.bfloat16)
    result = (
        jnp.einsum("hqk,khe->qhe", slopes, key_heads, preferred_element_type=jnp.float32) * scaling
    )
    return result.reshape(row_count, col_count, features)


def window_grad_keys(keyval, query_ext, stats_ext, inside):
    row_count, col_count, twice = keyval.shape
    features = twice // 2
    scaling = (features // H0) ** (-0.5)
    allowed = window_mask(row_count, col_count, inside)[None]
    key_heads = split_heads(keyval[..., :features])
    value_heads = split_heads(keyval[..., features:])
    query_heads = split_heads(query_ext[..., :features])
    grad_split = split_heads(query_ext[..., features:])
    total_t = jnp.transpose(stats_ext[..., :H0].reshape(-1, H0))[:, None, :]
    stat_t = jnp.transpose(stats_ext[..., H0:].reshape(-1, H0))[:, None, :]
    scores = (
        jnp.einsum("khe,qhe->hkq", key_heads, query_heads, preferred_element_type=jnp.float32)
        * scaling
    )
    soft_weights = jnp.exp(jnp.where(allowed, scores - total_t, -1e30))
    grad_p = jnp.einsum("khe,qhe->hkq", value_heads, grad_split, preferred_element_type=jnp.float32)
    slopes = (soft_weights * (grad_p - stat_t)).astype(jnp.bfloat16)
    weights_low = soft_weights.astype(jnp.bfloat16)
    key_grad = (
        jnp.einsum("hkq,qhe->khe", slopes, query_heads, preferred_element_type=jnp.float32)
        * scaling
    )
    value_grad = jnp.einsum(
        "hkq,qhe->khe", weights_low, grad_split, preferred_element_type=jnp.float32
    )
    return (
        key_grad.reshape(row_count, col_count, features),
        value_grad.reshape(row_count, col_count, features),
    )


def block_size(row_total):
    return row_total if row_total <= 1024 else math.gcd(row_total, 1024)


def global_forward(queries, key_rows, value_rows):
    row_total, head_count, head_size = queries.shape
    block_rows = block_size(row_total)
    scaling = head_size ** (-0.5)

    def one_block(query_block):
        scores = (
            jnp.einsum("qhe,khe->hqk", query_block, key_rows, preferred_element_type=jnp.float32)
            * scaling
        )
        maxima = jnp.max(scores, axis=-1, keepdims=True)
        exponent = jnp.exp(scores - maxima)
        totals = jnp.sum(exponent, axis=-1, keepdims=True)
        soft_weights = (exponent / totals).astype(jnp.bfloat16)
        output = jnp.einsum(
            "hqk,khe->qhe", soft_weights, value_rows, preferred_element_type=jnp.float32
        ).astype(jnp.bfloat16)
        return (output, jnp.transpose((maxima + jnp.log(totals))[..., 0]))

    outputs, log_total = lax.map(
        one_block, queries.reshape(row_total // block_rows, block_rows, head_count, head_size)
    )
    return (
        outputs.reshape(row_total, head_count, head_size),
        log_total.reshape(row_total, head_count),
    )


def global_grad_query(queries, grad_att, log_total, grad_stat, key_rows, value_rows):
    row_total, head_count, head_size = queries.shape
    block_rows = block_size(row_total)
    scaling = head_size ** (-0.5)

    def one_block(pieces):
        query_block, grad_block, total_block, stat_block = pieces
        scores = (
            jnp.einsum("qhe,khe->hqk", query_block, key_rows, preferred_element_type=jnp.float32)
            * scaling
        )
        soft_weights = jnp.exp(scores - jnp.transpose(total_block)[..., None])
        grad_p = jnp.einsum(
            "qhe,khe->hqk", grad_block, value_rows, preferred_element_type=jnp.float32
        )
        slopes = (soft_weights * (grad_p - jnp.transpose(stat_block)[..., None])).astype(
            jnp.bfloat16
        )
        return (
            jnp.einsum("hqk,khe->qhe", slopes, key_rows, preferred_element_type=jnp.float32)
            * scaling
        )

    split = row_total // block_rows
    result = lax.map(
        one_block,
        (
            queries.reshape(split, block_rows, head_count, head_size),
            grad_att.reshape(split, block_rows, head_count, head_size),
            log_total.reshape(split, block_rows, head_count),
            grad_stat.reshape(split, block_rows, head_count),
        ),
    )
    return result.reshape(row_total, head_count, head_size)


def global_grad_keys(key_rows, value_rows, queries, grad_att, log_total, grad_stat):
    row_total, head_count, head_size = queries.shape
    block_rows = block_size(row_total)
    scaling = head_size ** (-0.5)

    def one_block(running, pieces):
        query_block, grad_block, total_block, stat_block = pieces
        scores = (
            jnp.einsum("qhe,khe->hqk", query_block, key_rows, preferred_element_type=jnp.float32)
            * scaling
        )
        soft_weights = jnp.exp(scores - jnp.transpose(total_block)[..., None])
        grad_p = jnp.einsum(
            "qhe,khe->hqk", grad_block, value_rows, preferred_element_type=jnp.float32
        )
        slopes = (soft_weights * (grad_p - jnp.transpose(stat_block)[..., None])).astype(
            jnp.bfloat16
        )
        weights_low = soft_weights.astype(jnp.bfloat16)
        key_grad = jnp.einsum(
            "hqk,qhe->khe", slopes, query_block, preferred_element_type=jnp.float32
        )
        value_grad = jnp.einsum(
            "hqk,qhe->khe", weights_low, grad_block, preferred_element_type=jnp.float32
        )
        return ((running[0] + key_grad, running[1] + value_grad), None)

    split = row_total // block_rows
    zero_grads = jnp.zeros(key_rows.shape, jnp.float32)
    pieces = (
        queries.reshape(split, block_rows, head_count, head_size),
        grad_att.reshape(split, block_rows, head_count, head_size),
        log_total.reshape(split, block_rows, head_count),
        grad_stat.reshape(split, block_rows, head_count),
    )
    (key_grad, value_grad), _ = lax.scan(one_block, (zero_grads, zero_grads), pieces)
    return (key_grad * scaling, value_grad)


def on_device(
    tokens,
    grad_fine,
    grad_coarse,
    fine_gain,
    fine_qkv,
    fine_out,
    merge_weight,
    coarse_gain,
    coarse_qkv,
    coarse_out,
):
    row_count, col_count, features = tokens.shape
    row_devices = lax.axis_size("row")
    col_devices = lax.axis_size("col")
    grid_row = lax.axis_index("row") * row_count - RADIUS + jnp.arange(row_count + 2 * RADIUS)
    grid_col = lax.axis_index("col") * col_count - RADIUS + jnp.arange(col_count + 2 * RADIUS)
    inside = ((grid_row >= 0) & (grid_row < row_count * row_devices))[:, None] & (
        (grid_col >= 0) & (grid_col < col_count * col_devices)
    )[None, :]
    normed_f, inverse_f = norm_forward(tokens)
    normed_fine = (normed_f * fine_gain).astype(jnp.bfloat16)
    qkv_fine = (
        jnp.dot(normed_fine.reshape(-1, features), fine_qkv, preferred_element_type=jnp.float32)
        .astype(jnp.bfloat16)
        .reshape(row_count, col_count, 3 * features)
    )
    query_fine = qkv_fine[..., :features]
    keyval_fine = qkv_fine[..., features:]
    keyval_ext = with_halo(keyval_fine, (("row", 0), ("col", 1)), RADIUS)
    attended_f, lse_fine = window_forward(query_fine, keyval_ext, inside)
    attended_fine = attended_f.astype(jnp.bfloat16)
    projected = jnp.dot(
        attended_fine.reshape(-1, features), fine_out, preferred_element_type=jnp.float32
    ).reshape(row_count, col_count, features)
    hidden = (tokens.astype(jnp.float32) + projected).astype(jnp.bfloat16)
    merged = merge_blocks(hidden)
    coarse = jnp.dot(merged, merge_weight, preferred_element_type=jnp.float32).astype(jnp.bfloat16)
    normed_c, inverse_c = norm_forward(coarse)
    normed_coarse = (normed_c * coarse_gain).astype(jnp.bfloat16)
    qkv_coarse = jnp.dot(normed_coarse, coarse_qkv, preferred_element_type=jnp.float32).astype(
        jnp.bfloat16
    )
    grouped = lax.all_to_all(qkv_coarse, "row", split_axis=1, concat_axis=0, tiled=True)
    head_count = H1 // row_devices
    query_count = grouped.shape[0]
    grouped = grouped.reshape(query_count, head_count, 3, HEAD)
    query_c = grouped[:, :, 0]
    own_keyval = grouped[:, :, 1:].reshape(query_count, head_count * 2 * HEAD)
    gathered = lax.all_gather(own_keyval, "col", axis=0, tiled=True)
    all_keyval = gathered.reshape(-1, head_count, 2, HEAD)
    key_all = all_keyval[:, :, 0]
    value_all = all_keyval[:, :, 1]
    attended_coarse, lse_coarse = global_forward(query_c, key_all, value_all)
    grad_flat = grad_coarse.reshape(-1, D1)
    grad_heads = jnp.dot(grad_flat, coarse_out.T, preferred_element_type=jnp.float32).astype(
        jnp.bfloat16
    )
    grad_moved = lax.all_to_all(grad_heads, "row", split_axis=1, concat_axis=0, tiled=True)
    grad_att_c = grad_moved.reshape(query_count, head_count, HEAD)
    stat_coarse = jnp.sum(
        grad_att_c.astype(jnp.float32) * attended_coarse.astype(jnp.float32), axis=-1
    )
    query_grad = global_grad_query(query_c, grad_att_c, lse_coarse, stat_coarse, key_all, value_all)
    row_total = query_count * lax.axis_size("col")
    block_rows = block_size(row_total)

    def one_block(pieces):
        return global_grad_keys(pieces[0], pieces[1], query_c, grad_att_c, lse_coarse, stat_coarse)

    split = row_total // block_rows
    key_blocks, value_blocks = lax.map(
        one_block,
        (
            key_all.reshape(split, block_rows, head_count, HEAD),
            value_all.reshape(split, block_rows, head_count, HEAD),
        ),
    )
    stacked = jnp.stack(
        [
            key_blocks.reshape(row_total, head_count, HEAD),
            value_blocks.reshape(row_total, head_count, HEAD),
        ],
        axis=2,
    )
    partial = stacked.reshape(col_devices, query_count, head_count * 2 * HEAD).astype(jnp.bfloat16)
    swapped = lax.all_to_all(partial, "col", split_axis=0, concat_axis=0, tiled=True)
    summed = jnp.sum(swapped.astype(jnp.float32), axis=0)
    summed = summed.reshape(query_count, head_count, 2, HEAD)
    key_grad = summed[:, :, 0]
    value_grad = summed[:, :, 1]
    qkv_grad_heads = (
        jnp.stack([query_grad, key_grad, value_grad], axis=2)
        .astype(jnp.bfloat16)
        .reshape(query_count, head_count * 3 * HEAD)
    )
    qkv_grad_c = lax.all_to_all(qkv_grad_heads, "row", split_axis=0, concat_axis=1, tiled=True)
    upstream_c = jnp.dot(qkv_grad_c, coarse_qkv.T, preferred_element_type=jnp.float32)
    coarse_total = (
        grad_flat.astype(jnp.float32) + norm_backward(upstream_c, coarse_gain, normed_c, inverse_c)
    ).astype(jnp.bfloat16)
    spread_back = unmerge_blocks(
        jnp.dot(coarse_total, merge_weight.T, preferred_element_type=jnp.float32),
        row_count,
        col_count,
    )
    grad_hidden = (grad_fine.astype(jnp.float32) + spread_back).astype(jnp.bfloat16)
    flat_hidden = grad_hidden.reshape(-1, features)
    out_term = jnp.dot(
        attended_fine.reshape(-1, features).T, flat_hidden, preferred_element_type=jnp.float32
    )
    grad_att_f = (
        jnp.dot(flat_hidden, fine_out.T, preferred_element_type=jnp.float32)
        .astype(jnp.bfloat16)
        .reshape(row_count, col_count, features)
    )
    stat_fine = head_sum(grad_att_f.astype(jnp.float32) * attended_fine.astype(jnp.float32), H0)
    query_grad_f = window_grad_query(
        query_fine, keyval_ext, inside, lse_fine, stat_fine, grad_att_f
    )
    query_ext = with_halo(
        jnp.concatenate([query_fine, grad_att_f], axis=-1), (("row", 0), ("col", 1)), RADIUS
    )
    stats_ext = with_halo(
        jnp.concatenate([lse_fine, stat_fine], axis=-1), (("row", 0), ("col", 1)), RADIUS
    )
    key_grad_f, value_grad_f = window_grad_keys(keyval_fine, query_ext, stats_ext, inside)
    qkv_grad_f = (
        jnp.concatenate([query_grad_f, key_grad_f, value_grad_f], axis=-1)
        .astype(jnp.bfloat16)
        .reshape(-1, 3 * features)
    )
    qkv_term = jnp.dot(
        normed_fine.reshape(-1, features).T, qkv_grad_f, preferred_element_type=jnp.float32
    )
    qkv_blocks = device_blocks(qkv_term, row_devices, col_devices)
    out_blocks = device_blocks(out_term, row_devices, col_devices)
    packed = jnp.concatenate([qkv_blocks, out_blocks], axis=1).astype(jnp.bfloat16)
    terms = lax.all_to_all(packed, ("row", "col"), split_axis=0, concat_axis=0, tiled=True)
    total = jnp.sum(terms.astype(jnp.float32), axis=0).reshape(-1)
    qkv_size = qkv_blocks.shape[1] * 128
    grad_fine_qkv = total[:qkv_size].reshape(
        qkv_term.shape[0] // row_devices, qkv_term.shape[1] // col_devices
    )
    grad_fine_out = total[qkv_size:].reshape(
        out_term.shape[0] // row_devices, out_term.shape[1] // col_devices
    )
    upstream_f = jnp.dot(qkv_grad_f, fine_qkv.T, preferred_element_type=jnp.float32).reshape(
        row_count, col_count, features
    )
    grad_tokens = (
        grad_hidden.astype(jnp.float32) + norm_backward(upstream_f, fine_gain, normed_f, inverse_f)
    ).astype(jnp.bfloat16)
    return (grad_tokens, grad_fine_qkv, grad_fine_out)


def solution(mesh):
    return jax.shard_map(
        on_device,
        mesh=mesh,
        in_specs=(
            P("row", "col", None),
            P("row", "col", None),
            P("row", "col", None),
            P(),
            P(),
            P(),
            P(),
            P(),
            P(),
            P(),
        ),
        out_specs=(P("row", "col", None), P("row", "col"), P("row", "col")),
        check_vma=False,
    )
```

```python
import functools

import jax
import jax.numpy as jnp
from jax import lax
from jax.experimental import pallas as pl
from jax.experimental.pallas import tpu as pltpu
from jax.sharding import PartitionSpec as P

H0 = 4
H1 = 16
HEAD = 64
MERGE = 4
EPSILON = 1e-05
FAR = 1e30
D0 = 256
D1 = 1024

ROWS, COLS = 16, 24
CROWS, CCOLS = 4, 6
R8, C8 = ROWS + 16, COLS + 16
R4, C4 = ROWS + 8, COLS + 8
N4 = R4 * C4
BLOCK = 4 * C4
BLOCKS = R4 // 4
WROWS = R4 + 6
OWN = ROWS * C4
EXT = (CROWS + 2) * (CCOLS + 2)

F32 = jnp.float32
BF16 = jnp.bfloat16


def vmem_params(mib):
    return pltpu.CompilerParams(vmem_limit_bytes=mib * 1024 * 1024)


def whole():
    return pl.BlockSpec(memory_space=pltpu.VMEM)


def dot(a, b, ca, cb):
    return lax.dot_general(a, b, (((ca,), (cb,)), ((), ())), preferred_element_type=F32)


def norm_forward(values):
    center = values - jnp.mean(values, axis=-1, keepdims=True)
    inverse = lax.rsqrt(jnp.mean(center * center, axis=-1, keepdims=True) + EPSILON)
    return center * inverse, inverse


def norm_backward(scaled, normed, inverse):
    return inverse * (
        scaled
        - jnp.mean(scaled, axis=-1, keepdims=True)
        - normed * jnp.mean(scaled * normed, axis=-1, keepdims=True)
    )


def head_lanes(rows):
    return lax.broadcasted_iota(jnp.int32, (rows, D0), 1) // HEAD


def stack_heads(values):
    lanes = head_lanes(values.shape[0])
    zero = jnp.zeros_like(values)
    return jnp.concatenate([jnp.where(lanes == h, values, zero) for h in range(H0)], axis=0)


def unstack_heads(stacked):
    rows = stacked.shape[0] // H0
    lanes = head_lanes(rows)
    result = stacked[:rows]
    for h in range(1, H0):
        result = jnp.where(lanes == h, stacked[h * rows : (h + 1) * rows], result)
    return result


def window_bias(key_cols, col_shift, key_row, key_col):
    shape = (10, key_cols, BLOCK)
    kr = lax.broadcasted_iota(jnp.int32, shape, 0)
    kc = lax.broadcasted_iota(jnp.int32, shape, 1)
    lane = lax.broadcasted_iota(jnp.int32, shape, 2)
    row_gap = kr - lane // C4
    col_gap = kc - lane % C4 - col_shift
    rows_ok = (row_gap >= 0) & (row_gap <= 6) & (col_gap >= 0) & (col_gap <= 6)
    grid_row = key_row + kr
    grid_col = key_col + kc
    inside = (grid_row >= 0) & (grid_row < 128) & (grid_col >= 0) & (grid_col < 384)
    return jnp.where(rows_ok & inside, 0.0, -FAR).reshape(10 * key_cols, BLOCK)


def fine_forward(
    place,
    tokens,
    gain,
    w_qkv,
    w_out,
    merged,
    queries,
    keys_w,
    values_w,
    attended,
    lse,
    tokens_own,
    x32,
    q32,
    k32,
    v32,
    hid32,
):
    row0 = place[0]
    col0 = place[1]
    x = tokens[...].astype(F32)
    x32[...] = x
    normed, _ = norm_forward(x)
    normed = (normed * gain[...]).astype(BF16)
    q32[...] = dot(normed, w_qkv[:, :D0], 1, 0).astype(BF16).astype(F32) * (HEAD**-0.5)
    k32[...] = dot(normed, w_qkv[:, D0 : 2 * D0], 1, 0).astype(BF16).astype(F32)
    v32[...] = dot(normed, w_qkv[:, 2 * D0 :], 1, 0).astype(BF16).astype(F32)
    for i in range(R4):
        queries[C4 * i : C4 * (i + 1)] = q32[pl.ds((i + 4) * C8 + 4, C4), :].astype(BF16)
    for i in range(WROWS):
        keys_w[C4 * i : C4 * (i + 1)] = k32[pl.ds((i + 1) * C8 + 4, C4), :].astype(BF16)
        values_w[C4 * i : C4 * (i + 1)] = v32[pl.ds((i + 1) * C8 + 4, C4), :].astype(BF16)
    for i in range(ROWS):
        tokens_own[C4 * i : C4 * (i + 1)] = x32[pl.ds((i + 8) * C8 + 4, C4), :].astype(BF16)
    lse[...] = jnp.full(lse.shape, FAR, F32)
    for b in range(BLOCKS):
        start = (4 * b + 1) * C8
        key_block = k32[start : start + 10 * C8].astype(BF16)
        value_block = v32[start : start + 10 * C8].astype(BF16)
        stacked = stack_heads(queries[BLOCK * b : BLOCK * (b + 1)].astype(F32)).astype(BF16)
        bias = window_bias(C8, 1, row0 - 7 + 4 * b, col0 - 8)
        scores = dot(key_block, stacked, 1, 1) + jnp.concatenate([bias] * H0, axis=1)
        maxima = jnp.max(scores, axis=0, keepdims=True)
        exponent = jnp.exp(scores - maxima)
        totals = jnp.sum(exponent, axis=0, keepdims=True)
        weights = (exponent * (1.0 / totals)).astype(BF16)
        result = unstack_heads(dot(weights, value_block, 0, 0)).astype(BF16)
        attended[BLOCK * b : BLOCK * (b + 1)] = result
        lane = lax.broadcasted_iota(jnp.int32, (1, H0 * BLOCK), 1) % BLOCK
        q_row = row0 - 4 + 4 * b + lane // C4
        q_col = col0 - 4 + lane % C4
        q_in = (q_row >= 0) & (q_row < 128) & (q_col >= 0) & (q_col < 384)
        lse[b : b + 1] = jnp.where(q_in, maxima + jnp.log(totals), FAR)
        projected = dot(result, w_out[...], 1, 0)
        for a in range(4):
            own = x32[pl.ds((4 * b + a + 4) * C8 + 4, C4), :]
            total = own + projected[C4 * a : C4 * (a + 1)]
            at = BLOCK * b + C4 * a
            total = total.astype(BF16).astype(F32)
            hid32[0, at : at + C4] = total[:, :128]
            hid32[1, at : at + C4] = total[:, 128:]
    for pair in range((CROWS + 2) // 2):
        for a in range(MERGE):
            for c in range(MERGE):
                for half in range(2):
                    parts = [
                        hid32[half, pl.ds((4 * i + a) * C4 + c, CCOLS + 2, stride=MERGE), :]
                        for i in (2 * pair, 2 * pair + 1)
                    ]
                    at = (a * MERGE + c) * D0 + half * 128
                    merged[16 * pair : 16 * (pair + 1), at : at + 128] = jnp.concatenate(
                        parts, axis=0
                    ).astype(BF16)


def run_fine_forward(place, tokens8, gain, w_qkv, w_out):
    flat = R8 * C8
    shapes = [
        ((EXT, MERGE * MERGE * D0), BF16),
        ((N4, D0), BF16),
        ((WROWS * C4, D0), BF16),
        ((WROWS * C4, D0), BF16),
        ((N4, D0), BF16),
        ((8, H0 * BLOCK), F32),
        ((OWN, D0), BF16),
    ]
    return pl.pallas_call(
        fine_forward,
        out_shape=[jax.ShapeDtypeStruct(s, d) for s, d in shapes],
        in_specs=[pl.BlockSpec(memory_space=pltpu.SMEM)] + [whole()] * 4,
        out_specs=[whole()] * len(shapes),
        scratch_shapes=[pltpu.VMEM((flat, D0), F32)] * 4 + [pltpu.VMEM((2, N4, 128), F32)],
        compiler_params=vmem_params(32),
        cost_estimate=pl.CostEstimate(flops=2 * 10**9, bytes_accessed=4 * 10**6, transcendentals=10**6),
        name="fine_forward",
    )(place, tokens8.reshape(flat, D0), gain.reshape(1, D0), w_qkv, w_out)


def coarse_project(coarse, gain, weight, grads, out, normed_ref):
    @pl.when(pl.program_id(0) == 0)
    def _():
        normed, _ = norm_forward(coarse[...].astype(F32))
        normed = normed * gain[...]
        wide = CCOLS + 2
        parts = [normed[wide * i + 1 : wide * i + 1 + CCOLS] for i in range(1, CROWS + 1)]
        normed_ref[...] = jnp.concatenate(parts, axis=0).astype(BF16)

    result = dot(normed_ref[...], weight[...], 1, 0)
    grad = grads[...].astype(F32)
    for h in range(2):
        q = result[:, 192 * h : 192 * h + 64]
        k = result[:, 192 * h + 64 : 192 * h + 128]
        v = result[:, 192 * h + 128 : 192 * h + 192]
        g = grad[:, 64 * h : 64 * h + 64]
        packed = jnp.concatenate([k, v, q, g], axis=1).astype(BF16)
        for r in range(8):
            out[r, h] = packed


def run_coarse_project(coarse, gain, weight, grads):
    own = CROWS * CCOLS
    return pl.pallas_call(
        coarse_project,
        grid=(8,),
        out_shape=jax.ShapeDtypeStruct((8, H1, own, 256), BF16),
        in_specs=[
            pl.BlockSpec((EXT, D1), lambda n: (0, 0)),
            pl.BlockSpec((1, D1), lambda n: (0, 0)),
            pl.BlockSpec((D1, 384), lambda n: (0, n)),
            pl.BlockSpec((own, 128), lambda n: (0, n)),
        ],
        out_specs=pl.BlockSpec((8, 2, own, 256), lambda n: (0, n, 0, 0)),
        scratch_shapes=[pltpu.VMEM((own, D1), BF16)],
        compiler_params=vmem_params(32),
        cost_estimate=pl.CostEstimate(flops=2 * 10**8, bytes_accessed=8 * 10**6, transcendentals=0),
        name="coarse_project",
    )(coarse, gain.reshape(1, D1), weight, grads)


def lane_half(values, low):
    lanes = lax.broadcasted_iota(jnp.int32, values.shape, 1)
    keep = lanes < HEAD if low else lanes >= HEAD
    return jnp.where(keep, values, jnp.zeros_like(values))


def coarse_forward(every, own, stats, scores_ref):
    keyval = every[:, :128]
    keys = lane_half(keyval.astype(F32) * (HEAD**-0.5), True).astype(BF16)
    row = lax.broadcasted_iota(jnp.int32, (8, 128), 0)
    for b in range(3):
        part = own[128 * b : 128 * (b + 1), 128:]
        scores_ref[...] = dot(keys, part, 1, 1)
        maxima = jnp.max(scores_ref[...], axis=0, keepdims=True)
        exponent = jnp.exp(scores_ref[...] - maxima)
        totals = jnp.sum(exponent, axis=0, keepdims=True)
        weights = (exponent * (1.0 / totals)).astype(BF16)
        attended = dot(keyval, weights, 0, 0).astype(BF16).astype(F32)
        grads = part.astype(F32).T
        stat = jnp.sum(grads[HEAD:] * attended[HEAD:], axis=0, keepdims=True)
        log_total = maxima + jnp.log(totals)
        stats[:, 128 * b : 128 * (b + 1)] = jnp.where(
            row == 0, log_total, jnp.where(row == 1, stat, 0.0)
        )


def run_coarse_forward(every, own):
    return pl.pallas_call(
        coarse_forward,
        out_shape=jax.ShapeDtypeStruct((8, 384), F32),
        in_specs=[whole()] * 2,
        out_specs=whole(),
        scratch_shapes=[pltpu.VMEM((3072, 128), F32)],
        compiler_params=vmem_params(32),
        cost_estimate=pl.CostEstimate(flops=10**9, bytes_accessed=2 * 10**6, transcendentals=10**6),
        name="coarse_forward",
    )(every, own)


CHUNK = 512
EDGE = 576


def coarse_backward(every, edge, stats, edge_stats, out, dq_ref, dk_ref, dv_ref):
    edge_kv = edge[:, :128]
    edge_qg = edge[:, 128:]
    edge_k = lane_half(edge_kv.astype(F32) * (HEAD**-0.5), True).astype(BF16)
    edge_v = lane_half(edge_kv.astype(F32), False).astype(BF16)
    dq_ref[...] = jnp.zeros_like(dq_ref)
    dk_ref[...] = jnp.zeros_like(dk_ref)
    dv_ref[...] = jnp.zeros_like(dv_ref)
    lse_edge = edge_stats[0:1]
    stat_edge = edge_stats[1:2]
    for n in range(3072 // CHUNK):
        rows = slice(n * CHUNK, (n + 1) * CHUNK)
        keyval = every[rows, :128]
        wide = keyval.astype(F32)
        keys = lane_half(wide * (HEAD**-0.5), True).astype(BF16)
        values = lane_half(wide, False).astype(BF16)
        probs = jnp.exp(dot(keys, edge_qg, 1, 1) - lse_edge)
        slopes = (probs * (dot(values, edge_qg, 1, 1) - stat_edge)).astype(BF16)
        dq_ref[...] += dot(keyval, slopes, 0, 0)
        query = every[rows, 128:]
        probs = jnp.exp(dot(edge_k, query, 1, 1) - stats[0:1, rows])
        slopes = (probs * (dot(edge_v, query, 1, 1) - stats[1:2, rows])).astype(BF16)
        dk_ref[...] += dot(slopes, query, 1, 0)
        dv_ref[...] += dot(probs.astype(BF16), query, 1, 0)
    lanes = lax.broadcasted_iota(jnp.int32, (EDGE, 128), 1)
    out[:, :128] = jnp.where(lanes < HEAD, dk_ref[...] * (HEAD**-0.5), dv_ref[...]).astype(BF16)
    out[:, 128:] = (dq_ref[...].T * (HEAD**-0.5)).astype(BF16)


def run_coarse_backward(every, edge, stats, edge_stats):
    return pl.pallas_call(
        coarse_backward,
        out_shape=jax.ShapeDtypeStruct((EDGE, 256), BF16),
        in_specs=[whole()] * 4,
        out_specs=whole(),
        scratch_shapes=[
            pltpu.VMEM((128, EDGE), F32),
            pltpu.VMEM((EDGE, 128), F32),
            pltpu.VMEM((EDGE, 128), F32),
        ],
        compiler_params=vmem_params(40),
        cost_estimate=pl.CostEstimate(flops=3 * 10**9, bytes_accessed=2 * 10**6, transcendentals=4 * 10**6),
        name="coarse_backward",
    )(every, edge, stats, edge_stats)


def coarse_upstream(terms, weight, coarse, gain, grads, out, total):
    n = pl.program_id(0)

    @pl.when(n == 0)
    def _():
        total[...] = jnp.zeros_like(total)

    parts = []
    for h in range(2):
        block = terms[h].astype(F32)
        parts += [block[:, 128:192], block[:, :128]]
    total[...] += dot(jnp.concatenate(parts, axis=1).astype(BF16), weight[...], 1, 1)

    @pl.when(n == pl.num_programs(0) - 1)
    def _():
        normed, inverse = norm_forward(coarse[...].astype(F32))
        change = norm_backward(total[...] * gain[...], normed, inverse)
        out[...] = (grads[...].astype(F32) + change).astype(BF16)


def run_coarse_upstream(terms, weight, coarse, gain, grads):
    return pl.pallas_call(
        coarse_upstream,
        grid=(8,),
        out_shape=jax.ShapeDtypeStruct((EXT, D1), BF16),
        in_specs=[
            pl.BlockSpec((2, EXT, 256), lambda n: (n, 0, 0)),
            pl.BlockSpec((D1, 384), lambda n: (0, n)),
            pl.BlockSpec((EXT, D1), lambda n: (0, 0)),
            pl.BlockSpec((1, D1), lambda n: (0, 0)),
            pl.BlockSpec((EXT, D1), lambda n: (0, 0)),
        ],
        out_specs=pl.BlockSpec((EXT, D1), lambda n: (0, 0)),
        scratch_shapes=[pltpu.VMEM((EXT, D1), F32)],
        compiler_params=vmem_params(32),
        cost_estimate=pl.CostEstimate(flops=3 * 10**8, bytes_accessed=8 * 10**6, transcendentals=0),
        name="coarse_upstream",
    )(terms, weight, coarse, gain.reshape(1, D1), grads)


def fine_backward(
    place,
    spread,
    grad_fine,
    queries,
    keys_w,
    values_w,
    attended,
    lse,
    tokens_own,
    gain,
    w_qkv,
    w_out,
    grad_tokens,
    term_qkv,
    term_out,
    sp32,
    gh_ref,
    ga_ref,
    dq_ref,
    dk_ref,
    dv_ref,
    gt_ref,
):
    row0 = place[0]
    col0 = place[1]
    wide = CCOLS + 2
    for i in range(CROWS + 2):
        for a in range(MERGE):
            for c in range(MERGE):
                for half in range(2):
                    at = (a * MERGE + c) * D0 + half * 128
                    sp32[half, pl.ds((4 * i + a) * C4 + c, wide, stride=MERGE), :] = spread[
                        wide * i : wide * (i + 1), at : at + 128
                    ]
    for half in range(2):
        at = slice(half * 128, (half + 1) * 128)
        gh_ref[:, at] = (grad_fine[:, at].astype(F32) + sp32[half]).astype(BF16)
    ga_ref[...] = dot(gh_ref[...], w_out[...], 1, 1).astype(BF16)
    dk_ref[...] = jnp.zeros_like(dk_ref)
    dv_ref[...] = jnp.zeros_like(dv_ref)
    pick = (
        lax.broadcasted_iota(jnp.int32, (8, D0), 1) // HEAD
        == lax.broadcasted_iota(jnp.int32, (8, D0), 0)
    ).astype(F32)
    for b in range(BLOCKS):
        at = slice(BLOCK * b, BLOCK * (b + 1))
        keep = slice(BLOCK * b, BLOCK * b + 10 * C4)
        grad = ga_ref[at].astype(F32)
        product = grad * attended[at].astype(F32)
        sums = lax.dot_general(
            pick,
            product,
            (((1,), (1,)), ((), ())),
            precision=lax.Precision.HIGHEST,
            preferred_element_type=F32,
        )
        stat = jnp.concatenate([sums[h : h + 1] for h in range(H0)], axis=1)
        stack_q = stack_heads(queries[at].astype(F32)).astype(BF16)
        stack_g = stack_heads(grad).astype(BF16)
        key_block = keys_w[keep]
        bias = window_bias(C4, -3, row0 - 7 + 4 * b, col0 - 4)
        scores = dot(key_block, stack_q, 1, 1) + jnp.concatenate([bias] * H0, axis=1)
        probs = jnp.exp(scores - lse[b : b + 1])
        slopes = (probs * (dot(values_w[keep], stack_g, 1, 1) - stat)).astype(BF16)
        dk_ref[keep] += dot(slopes, stack_q, 1, 0)
        dv_ref[keep] += dot(probs.astype(BF16), stack_g, 1, 0)
        if 1 <= b <= 4:
            dq = unstack_heads(dot(slopes, key_block, 0, 0)) * (HEAD**-0.5)
            dq_ref[BLOCK * (b - 1) : BLOCK * b] = dq.astype(BF16)
    own = slice(7 * C4, 7 * C4 + OWN)
    grads = jnp.concatenate(
        [dq_ref[...], dk_ref[own].astype(BF16), dv_ref[own].astype(BF16)], axis=1
    )
    column = lax.broadcasted_iota(jnp.int32, (ROWS, C4, D0), 1).reshape(OWN, D0)
    in_tile = (column >= 4) & (column < 4 + COLS)
    normed, inverse = norm_forward(tokens_own[...].astype(F32))
    rounded = jnp.where(in_tile, normed * gain[...], 0.0).astype(BF16)
    term_qkv[...] = dot(rounded, grads, 0, 0).astype(BF16)
    inner = slice(BLOCK, BLOCK + OWN)
    att = jnp.where(in_tile, attended[inner].astype(F32), 0.0).astype(BF16)
    term_out[...] = dot(att, gh_ref[inner], 0, 0).astype(BF16)
    upstream = dot(grads, w_qkv[...], 1, 1) * gain[...]
    gt_ref[...] = gh_ref[inner].astype(F32) + norm_backward(upstream, normed, inverse)
    for pair in range(ROWS // 2):
        parts = [gt_ref[pl.ds(i * C4 + 4, COLS), :] for i in (2 * pair, 2 * pair + 1)]
        grad_tokens[2 * COLS * pair : 2 * COLS * (pair + 1)] = jnp.concatenate(
            parts, axis=0
        ).astype(BF16)


def run_fine_backward(*operands):
    shapes = [((ROWS * COLS, D0), BF16), ((D0, 3 * D0), BF16), ((D0, D0), BF16)]
    return pl.pallas_call(
        fine_backward,
        out_shape=[jax.ShapeDtypeStruct(s, d) for s, d in shapes],
        in_specs=[pl.BlockSpec(memory_space=pltpu.SMEM)] + [whole()] * 11,
        out_specs=[whole()] * 3,
        scratch_shapes=[
            pltpu.VMEM((2, N4, 128), F32),
            pltpu.VMEM((N4, D0), BF16),
            pltpu.VMEM((N4, D0), BF16),
            pltpu.VMEM((OWN, D0), BF16),
            pltpu.VMEM((WROWS * C4, D0), F32),
            pltpu.VMEM((WROWS * C4, D0), F32),
            pltpu.VMEM((OWN, D0), F32),
        ],
        compiler_params=vmem_params(40),
        cost_estimate=pl.CostEstimate(flops=4 * 10**9, bytes_accessed=6 * 10**6, transcendentals=10**6),
        name="fine_backward",
    )(*operands)


def ring(axis, step):
    devices = lax.axis_size(axis)
    return [(i, (i + step) % devices) for i in range(devices)]


def swap_edges(first, last, axis):
    before = lax.ppermute(last, axis, ring(axis, 1))
    after = lax.ppermute(first, axis, ring(axis, -1))
    return before, after


def token_halo(tokens, width):
    for axis, dim in (("row", 0), ("col", 1)):
        length = tokens.shape[dim]
        first = lax.slice_in_dim(tokens, 0, width, axis=dim)
        last = lax.slice_in_dim(tokens, length - width, length, axis=dim)
        before, after = swap_edges(first, last, axis)
        tokens = jnp.concatenate([before, tokens, after], axis=dim)
    return tokens


def grad_halo(grad_fine, grad_coarse):
    folded = grad_coarse.reshape(CROWS, CCOLS, 4, D0).transpose(0, 2, 1, 3)
    both = jnp.concatenate([grad_fine, folded.reshape(ROWS, CCOLS, D0)], axis=1)
    before, after = swap_edges(both[:4], both[-4:], "row")
    both = jnp.concatenate([before, both, after], axis=0)
    first = jnp.concatenate([both[:, :4], both[:, COLS : COLS + 1]], axis=1)
    last = jnp.concatenate([both[:, COLS - 4 : COLS], both[:, -1:]], axis=1)
    before, after = swap_edges(first, last, "col")
    fine = jnp.concatenate([before[:, :4], both[:, :COLS], after[:, :4]], axis=1)
    coarse = jnp.concatenate([before[:, 4:], both[:, COLS:], after[:, 4:]], axis=1)
    coarse = coarse.reshape(CROWS + 2, 4, CCOLS + 2, D0).transpose(0, 2, 1, 3)
    return fine, coarse.reshape(EXT, D1)


def on_device(
    tokens,
    grad_fine,
    grad_coarse,
    fine_gain,
    fine_qkv,
    fine_out,
    merge_weight,
    coarse_gain,
    coarse_qkv,
    coarse_out,
):
    row = lax.axis_index("row")
    col = lax.axis_index("col")
    place = jnp.stack([row * ROWS, col * COLS]).astype(jnp.int32)
    tokens8 = token_halo(tokens, 8)
    grad_heads = jnp.dot(
        grad_coarse.reshape(-1, D1), coarse_out.T, preferred_element_type=F32
    ).astype(BF16)
    merged, queries, keys_w, values_w, attended, lse, tokens_own = run_fine_forward(
        place, tokens8, fine_gain, fine_qkv, fine_out
    )
    coarse = jnp.dot(merged, merge_weight, preferred_element_type=F32).astype(BF16)
    packed = run_coarse_project(coarse, coarse_gain, coarse_qkv, grad_heads)
    every = lax.all_to_all(
        packed.reshape(8 * H1, CROWS * CCOLS, 256),
        ("row", "col"),
        split_axis=0,
        concat_axis=0,
        tiled=True,
    )
    slabs = every.reshape(8, H1, CROWS, CCOLS, 256)
    own = lax.dynamic_index_in_dim(slabs, row, 0, keepdims=False).reshape(384, 256)
    above = lax.dynamic_index_in_dim(slabs[:, :, CROWS - 1], (row + 7) % 8, 0, keepdims=False)
    below = lax.dynamic_index_in_dim(slabs[:, :, 0], (row + 1) % 8, 0, keepdims=False)
    edge = jnp.concatenate([own, above.reshape(96, 256), below.reshape(96, 256)], axis=0)
    every = every.reshape(3072, 256)
    stats = run_coarse_forward(every, own)
    copies = jnp.broadcast_to(stats[None], (8, 8, 384))
    stats = lax.all_to_all(copies, "row", split_axis=0, concat_axis=0, tiled=True)
    stat_slabs = stats[:, :2].reshape(8, 2, H1, CROWS, CCOLS)
    own_s = lax.dynamic_index_in_dim(stats[:, :2], row, 0, keepdims=False)
    above_s = lax.dynamic_index_in_dim(
        stat_slabs[:, :, :, CROWS - 1], (row + 7) % 8, 0, keepdims=False
    )
    below_s = lax.dynamic_index_in_dim(stat_slabs[:, :, :, 0], (row + 1) % 8, 0, keepdims=False)
    edge_stats = jnp.concatenate([own_s, above_s.reshape(2, 96), below_s.reshape(2, 96)], axis=1)
    all_stats = stats[:, :2].transpose(1, 0, 2).reshape(2, 3072)
    grads = run_coarse_backward(every, edge, all_stats, edge_stats)
    main = grads[:384].reshape(H1, CROWS, CCOLS, 256)
    tiles = jnp.concatenate(
        [
            grads[384:480].reshape(H1, 1, CCOLS, 256),
            main,
            grads[480:].reshape(H1, 1, CCOLS, 256),
        ],
        axis=1,
    )
    left = jnp.roll(tiles[:, :, -1:], 1, axis=0)
    right = jnp.roll(tiles[:, :, :1], -1, axis=0)
    tiles = jnp.concatenate([left, tiles, right], axis=2).reshape(H1, EXT, 256)
    terms = lax.all_to_all(tiles, "col", split_axis=0, concat_axis=0, tiled=True)
    fine_ext, coarse_ext = grad_halo(grad_fine, grad_coarse)
    coarse_total = run_coarse_upstream(terms, coarse_qkv, coarse, coarse_gain, coarse_ext)
    spread = jnp.dot(coarse_total, merge_weight.T, preferred_element_type=F32)
    grad_tokens, term_qkv, term_out = run_fine_backward(
        place,
        spread,
        fine_ext.reshape(N4, D0),
        queries,
        keys_w,
        values_w,
        attended,
        lse,
        tokens_own,
        fine_gain.reshape(1, D0),
        fine_qkv,
        fine_out,
    )
    qkv_blocks = term_qkv.reshape(8, 32, H1, 48).transpose(0, 2, 1, 3).reshape(128, 12, 128)
    out_blocks = term_out.reshape(8, 32, H1, 16).transpose(0, 2, 1, 3).reshape(128, 4, 128)
    blocks = jnp.concatenate([qkv_blocks, out_blocks], axis=1)
    blocks = lax.all_to_all(blocks, ("row", "col"), split_axis=0, concat_axis=0, tiled=True)
    total = jnp.sum(blocks.astype(F32), axis=0)
    return (
        grad_tokens.reshape(ROWS, COLS, D0),
        total[:12].reshape(32, 48),
        total[12:].reshape(32, 16),
    )


def solution(mesh):
    return jax.shard_map(
        on_device,
        mesh=mesh,
        in_specs=(P("row", "col", None),) * 3 + (P(),) * 7,
        out_specs=(P("row", "col", None), P("row", "col"), P("row", "col")),
        check_vma=False,
    )
```

```python
import jax
import jax.numpy as jnp
import numpy as np
from jax import lax
from jax.experimental import pallas as pl
from jax.experimental.pallas import tpu as pltpu
from jax.sharding import PartitionSpec as P

H0 = 4
H1 = 16
HEAD = 64
MERGE = 4
EPSILON = 1e-05
FAR = 1e30
D0 = 256
D1 = 1024

ROWS, COLS = 16, 24
CROWS, CCOLS = 4, 6
R8, C8 = ROWS + 16, COLS + 16
R4, C4 = ROWS + 8, COLS + 8
N4 = R4 * C4
BLOCK = 4 * C4
BLOCKS = R4 // 4
WROWS = R4 + 6
OWN = ROWS * C4
EXT = (CROWS + 2) * (CCOLS + 2)

F32 = jnp.float32
BF16 = jnp.bfloat16


def vmem_params(mib):
    return pltpu.CompilerParams(vmem_limit_bytes=mib * 1024 * 1024)


def whole():
    return pl.BlockSpec(memory_space=pltpu.VMEM)


def far():
    return pl.BlockSpec(memory_space=pltpu.HBM)


def fetch(source, target, sems, pieces):
    rows = source.shape[0] // pieces
    return [
        pltpu.make_async_copy(
            source.at[pl.ds(n * rows, rows)], target.at[pl.ds(n * rows, rows)], sems.at[n]
        )
        for n in range(pieces)
    ]


def dot(a, b, ca, cb):
    return lax.dot_general(a, b, (((ca,), (cb,)), ((), ())), preferred_element_type=F32)


def norm_forward(values):
    center = values - jnp.mean(values, axis=-1, keepdims=True)
    inverse = lax.rsqrt(jnp.mean(center * center, axis=-1, keepdims=True) + EPSILON)
    return center * inverse, inverse


def norm_backward(scaled, normed, inverse):
    return inverse * (
        scaled
        - jnp.mean(scaled, axis=-1, keepdims=True)
        - normed * jnp.mean(scaled * normed, axis=-1, keepdims=True)
    )


def head_lanes(rows):
    return lax.broadcasted_iota(jnp.int32, (rows, D0), 1) // HEAD


def stack_heads(values):
    lanes = head_lanes(values.shape[0])
    zero = jnp.zeros_like(values)
    return jnp.concatenate([jnp.where(lanes == h, values, zero) for h in range(H0)], axis=0)


def unstack_heads(stacked):
    rows = stacked.shape[0] // H0
    lanes = head_lanes(rows)
    result = stacked[:rows]
    for h in range(1, H0):
        result = jnp.where(lanes == h, stacked[h * rows : (h + 1) * rows], result)
    return result


AT_Q = 0
AT_ATT = N4
AT_K = 2 * N4
AT_V = AT_K + WROWS * C4
AT_X = AT_V + WROWS * C4
STASH = AT_X + OWN


def window_bias(key_cols, col_shift, key_row, key_col):
    shape = (10, key_cols, BLOCK)
    kr = lax.broadcasted_iota(jnp.int32, shape, 0)
    kc = lax.broadcasted_iota(jnp.int32, shape, 1)
    lane = lax.broadcasted_iota(jnp.int32, shape, 2)
    row_gap = kr - lane // C4
    col_gap = kc - lane % C4 - col_shift
    rows_ok = (row_gap >= 0) & (row_gap <= 6) & (col_gap >= 0) & (col_gap <= 6)
    grid_row = key_row + kr
    grid_col = key_col + kc
    inside = (grid_row >= 0) & (grid_row < 128) & (grid_col >= 0) & (grid_col < 384)
    return jnp.where(rows_ok & inside, 0.0, -FAR).reshape(10 * key_cols, BLOCK)


def forward_kernel(
    place,
    tokens,
    above,
    below,
    left,
    right,
    gain,
    w_qkv,
    w_out,
    w_merge_far,
    gain_coarse,
    w_coarse_far,
    grads,
    stash_far,
    lse,
    coarse_out,
    packed_far,
    x32,
    q32,
    k32,
    v32,
    hid32,
    stash,
    merged,
    w_merge,
    w_coarse,
    packed,
    merge_sems,
    coarse_sems,
    stash_sem,
    packed_sems,
):
    merge_copies = fetch(w_merge_far, w_merge, merge_sems, 4)
    coarse_copies = fetch(w_coarse_far, w_coarse, coarse_sems, 2)
    for copy in merge_copies + coarse_copies:
        copy.start()
    queries = stash.at[pl.ds(AT_Q, N4)]
    attended = stash.at[pl.ds(AT_ATT, N4)]
    keys_w = stash.at[pl.ds(AT_K, WROWS * C4)]
    values_w = stash.at[pl.ds(AT_V, WROWS * C4)]
    tokens_own = stash.at[pl.ds(AT_X, OWN)]
    row0 = place[0]
    col0 = place[1]
    middle = [above[...].astype(F32), tokens[...].astype(F32), below[...].astype(F32)]
    sides = [left[...].astype(F32), right[...].astype(F32)]
    for i in range(R8):
        part, at = (0, i) if i < 8 else (1, i - 8) if i < 8 + ROWS else (2, i - 8 - ROWS)
        x32[C8 * i : C8 * i + 8] = sides[0][8 * i : 8 * i + 8]
        x32[C8 * i + 8 : C8 * i + 8 + COLS] = middle[part][COLS * at : COLS * (at + 1)]
        x32[C8 * i + 8 + COLS : C8 * (i + 1)] = sides[1][8 * i : 8 * i + 8]
    normed, _ = norm_forward(x32[...])
    normed = (normed * gain[...]).astype(BF16)
    q32[...] = dot(normed, w_qkv[:, :D0], 1, 0).astype(BF16).astype(F32) * (HEAD**-0.5)
    k32[...] = dot(normed, w_qkv[:, D0 : 2 * D0], 1, 0).astype(BF16).astype(F32)
    v32[...] = dot(normed, w_qkv[:, 2 * D0 :], 1, 0).astype(BF16).astype(F32)
    for i in range(R4):
        queries[C4 * i : C4 * (i + 1)] = q32[pl.ds((i + 4) * C8 + 4, C4), :].astype(BF16)
    for i in range(WROWS):
        keys_w[C4 * i : C4 * (i + 1)] = k32[pl.ds((i + 1) * C8 + 4, C4), :].astype(BF16)
        values_w[C4 * i : C4 * (i + 1)] = v32[pl.ds((i + 1) * C8 + 4, C4), :].astype(BF16)
    for i in range(ROWS):
        tokens_own[C4 * i : C4 * (i + 1)] = x32[pl.ds((i + 8) * C8 + 4, C4), :].astype(BF16)
    lse[...] = jnp.full(lse.shape, FAR, F32)
    for b in range(BLOCKS):
        start = (4 * b + 1) * C8
        key_block = k32[start : start + 10 * C8].astype(BF16)
        value_block = v32[start : start + 10 * C8].astype(BF16)
        stacked = stack_heads(queries[BLOCK * b : BLOCK * (b + 1)].astype(F32)).astype(BF16)
        bias = window_bias(C8, 1, row0 - 7 + 4 * b, col0 - 8)
        scores = dot(key_block, stacked, 1, 1) + jnp.concatenate([bias] * H0, axis=1)
        maxima = jnp.max(scores, axis=0, keepdims=True)
        exponent = jnp.exp(scores - maxima)
        totals = jnp.sum(exponent, axis=0, keepdims=True)
        weights = (exponent * (1.0 / totals)).astype(BF16)
        result = unstack_heads(dot(weights, value_block, 0, 0)).astype(BF16)
        attended[BLOCK * b : BLOCK * (b + 1)] = result
        lane = lax.broadcasted_iota(jnp.int32, (1, H0 * BLOCK), 1) % BLOCK
        q_row = row0 - 4 + 4 * b + lane // C4
        q_col = col0 - 4 + lane % C4
        q_in = (q_row >= 0) & (q_row < 128) & (q_col >= 0) & (q_col < 384)
        lse[b : b + 1] = jnp.where(q_in, maxima + jnp.log(totals), FAR)
        projected = dot(result, w_out[...], 1, 0)
        for a in range(4):
            own = x32[pl.ds((4 * b + a + 4) * C8 + 4, C4), :]
            total = own + projected[C4 * a : C4 * (a + 1)]
            at = BLOCK * b + C4 * a
            total = total.astype(BF16).astype(F32)
            hid32[0, at : at + C4] = total[:, :128]
            hid32[1, at : at + C4] = total[:, 128:]
    for pair in range((CROWS + 2) // 2):
        for a in range(MERGE):
            for c in range(MERGE):
                for half in range(2):
                    parts = [
                        hid32[half, pl.ds((4 * i + a) * C4 + c, CCOLS + 2, stride=MERGE), :]
                        for i in (2 * pair, 2 * pair + 1)
                    ]
                    at = (a * MERGE + c) * D0 + half * 128
                    merged[16 * pair : 16 * (pair + 1), at : at + 128] = jnp.concatenate(
                        parts, axis=0
                    ).astype(BF16)
    stash_copy = pltpu.make_async_copy(stash, stash_far, stash_sem)
    stash_copy.start()
    total = None
    for n, copy in enumerate(merge_copies):
        copy.wait()
        part = dot(merged[:, D1 * n : D1 * (n + 1)], w_merge[D1 * n : D1 * (n + 1)], 1, 0)
        total = part if total is None else total + part
    coarse = total.astype(BF16)
    coarse_out[...] = coarse
    normed, _ = norm_forward(coarse.astype(F32))
    normed = normed * gain_coarse[...]
    wide = CCOLS + 2
    parts = [normed[wide * i + 1 : wide * i + 1 + CCOLS] for i in range(1, CROWS + 1)]
    normed = jnp.concatenate(parts, axis=0).astype(BF16)
    for copy in coarse_copies:
        copy.wait()
    packed_copies = []
    for n in range(8):
        result = dot(normed, w_coarse[:, 384 * n : 384 * (n + 1)], 1, 0)
        grad = grads[:, 128 * n : 128 * (n + 1)].astype(F32)
        parts = []
        for h in range(2):
            q = result[:, 192 * h : 192 * h + 64]
            k = result[:, 192 * h + 64 : 192 * h + 128]
            v = result[:, 192 * h + 128 : 192 * h + 192]
            g = grad[:, 64 * h : 64 * h + 64]
            parts.append(jnp.concatenate([k, v, q, g], axis=1))
        packed[n] = jnp.concatenate(parts, axis=0).astype(BF16)
        if n % 4 == 3:
            at = pl.ds(n - 3, 4)
            for r in range(8):
                packed_copies.append(
                    pltpu.make_async_copy(
                        packed.at[at], packed_far.at[r, at], packed_sems.at[n // 4, r]
                    )
                )
                packed_copies[-1].start()
    for copy in packed_copies + [stash_copy]:
        copy.wait()


def run_forward(place, pieces, gain, w_qkv, w_out, w_merge, gain_coarse, w_coarse, grads):
    flat = R8 * C8
    own = CROWS * CCOLS
    shapes = [
        ((STASH, D0), BF16),
        ((8, H0 * BLOCK), F32),
        ((EXT, D1), BF16),
        ((8, 8, 2 * own, 256), BF16),
    ]
    return pl.pallas_call(
        forward_kernel,
        out_shape=[
            pltpu.HBM(s, d) if n in (0, 3) else jax.ShapeDtypeStruct(s, d)
            for n, (s, d) in enumerate(shapes)
        ],
        in_specs=[pl.BlockSpec(memory_space=pltpu.SMEM)]
        + [whole()] * 8
        + [far(), whole(), far(), whole()],
        out_specs=[far(), whole(), whole(), far()],
        scratch_shapes=[pltpu.VMEM((flat, D0), F32)] * 4
        + [
            pltpu.VMEM((2, N4, 128), F32),
            pltpu.VMEM((STASH, D0), BF16),
            pltpu.VMEM((EXT, MERGE * MERGE * D0), BF16),
            pltpu.VMEM(w_merge.shape, BF16),
            pltpu.VMEM(w_coarse.shape, BF16),
            pltpu.VMEM((8, 2 * own, 256), BF16),
            pltpu.SemaphoreType.DMA((4,)),
            pltpu.SemaphoreType.DMA((2,)),
            pltpu.SemaphoreType.DMA(()),
            pltpu.SemaphoreType.DMA((2, 8)),
        ],
        compiler_params=vmem_params(48),
        cost_estimate=pl.CostEstimate(flops=3 * 10**9, bytes_accessed=2 * 10**7, transcendentals=10**6),
        name="forward_kernel",
    )(
        place,
        *[piece.reshape(-1, D0) for piece in pieces],
        gain.reshape(1, D0),
        w_qkv,
        w_out,
        w_merge,
        gain_coarse.reshape(1, D1),
        w_coarse,
        grads,
    )


def lane_half(values, low):
    lanes = lax.broadcasted_iota(jnp.int32, values.shape, 1)
    keep = lanes < HEAD if low else lanes >= HEAD
    return jnp.where(keep, values, jnp.zeros_like(values))


SLAB = 384
SLABS = 8
STRIP = 96
EDGE = SLAB + 2 * STRIP


def strip_pick():
    tile, j = np.divmod(np.arange(STRIP), CCOLS)
    pick = np.zeros((2, STRIP, SLAB), np.float32)
    last = (CROWS - 1) * CCOLS
    pick[0, np.arange(STRIP), tile * CROWS * CCOLS + last + j] = 1
    pick[1, np.arange(STRIP), tile * CROWS * CCOLS + j] = 1
    return pick


def tile_pick():
    c, i, j = np.meshgrid(np.arange(H1), np.arange(6), np.arange(8), indexing="ij")
    tile = (c + (j == 7) - (j == 0)) % H1
    jj = np.where(j == 0, 5, np.where(j == 7, 0, j - 1))
    middle = tile * 24 + (i - 1) * 6 + jj
    source = np.where(i == 0, SLAB + tile * 6 + jj, np.where(i == 5, SLAB + STRIP + tile * 6 + jj, middle))
    pick = np.zeros((H1 * EXT, EDGE), np.float32)
    pick[np.arange(H1 * EXT), source.reshape(-1)] = 1
    return pick


def coarse_forward(place, every, stats, scores_ref):
    keyval = every[:, :128]
    keys = lane_half(keyval.astype(F32) * (HEAD**-0.5), True).astype(BF16)
    own = every[pl.ds(pl.multiple_of(place[2] * SLAB, SLAB), SLAB), 128:]
    logs = []
    sums = []
    for b in range(3):
        part = own[128 * b : 128 * (b + 1)]
        scores_ref[...] = dot(keys, part, 1, 1)
        maxima = jnp.max(scores_ref[...], axis=0, keepdims=True)
        exponent = jnp.exp(scores_ref[...] - maxima)
        totals = jnp.sum(exponent, axis=0, keepdims=True)
        weights = (exponent * (1.0 / totals)).astype(BF16)
        attended = dot(keyval, weights, 0, 0).astype(BF16).astype(F32)
        grads = part.astype(F32).T
        sums.append(jnp.sum(grads[HEAD:] * attended[HEAD:], axis=0, keepdims=True))
        logs.append(maxima + jnp.log(totals))
    result = jnp.concatenate(logs + sums + [jnp.zeros((2, 128), F32)], axis=0)
    for r in range(SLABS):
        stats[r] = result


def run_coarse_forward(place, every):
    return pl.pallas_call(
        coarse_forward,
        out_shape=jax.ShapeDtypeStruct((SLABS, 8, 128), F32),
        in_specs=[pl.BlockSpec(memory_space=pltpu.SMEM), whole()],
        out_specs=whole(),
        scratch_shapes=[pltpu.VMEM((SLAB * SLABS, 128), F32)],
        compiler_params=vmem_params(16),
        cost_estimate=pl.CostEstimate(flops=10**9, bytes_accessed=2 * 10**6, transcendentals=10**6),
        name="coarse_forward",
    )(place, every)


def stat_rows(stats):
    lse = jnp.concatenate([stats[k : k + 1] for k in range(3)], axis=1)
    stat = jnp.concatenate([stats[k : k + 1] for k in range(3, 6)], axis=1)
    return lse, stat


def coarse_backward(place, every, stats, strips, tiles, out, edge, dq_ref, dk_ref, dv_ref):
    row = place[2]
    above = lax.rem(row + SLABS - 1, SLABS)
    below = lax.rem(row + 1, SLABS)

    def slab(index):
        return pl.ds(pl.multiple_of(index * SLAB, SLAB), SLAB)

    edge[:SLAB] = every[slab(row)]
    edge_lse, edge_stat = stat_rows(stats[row])
    for k, other in enumerate((above, below)):
        at = SLAB + STRIP * k
        edge[at : at + STRIP] = dot(strips[k], every[slab(other)], 1, 0).astype(BF16)
        both = jnp.concatenate(stat_rows(stats[other]) + (jnp.zeros((6, SLAB), F32),), axis=0)
        taken = lax.dot_general(
            both,
            strips[k].astype(F32),
            (((1,), (1,)), ((), ())),
            precision=lax.Precision.HIGHEST,
            preferred_element_type=F32,
        )
        edge_lse = jnp.concatenate([edge_lse, taken[0:1]], axis=1)
        edge_stat = jnp.concatenate([edge_stat, taken[1:2]], axis=1)
    edge_kv = edge[:, :128]
    edge_qg = edge[:, 128:]
    edge_k = lane_half(edge_kv.astype(F32) * (HEAD**-0.5), True).astype(BF16)
    edge_v = lane_half(edge_kv.astype(F32), False).astype(BF16)
    for n in range(SLABS):
        rows = slice(n * SLAB, (n + 1) * SLAB)
        keyval = every[rows, :128]
        wide = keyval.astype(F32)
        keys = lane_half(wide * (HEAD**-0.5), True).astype(BF16)
        values = lane_half(wide, False).astype(BF16)
        probs = jnp.exp(dot(keys, edge_qg, 1, 1) - edge_lse)
        slopes = (probs * (dot(values, edge_qg, 1, 1) - edge_stat)).astype(BF16)
        dq = dot(keyval, slopes, 0, 0)
        query = every[rows, 128:]
        lse, stat = stat_rows(stats[n])
        probs = jnp.exp(dot(edge_k, query, 1, 1) - lse)
        slopes = (probs * (dot(edge_v, query, 1, 1) - stat)).astype(BF16)
        dk = dot(slopes, query, 1, 0)
        dv = dot(probs.astype(BF16), query, 1, 0)
        if n == 0:
            dq_ref[...] = dq
            dk_ref[...] = dk
            dv_ref[...] = dv
        else:
            dq_ref[...] += dq
            dk_ref[...] += dk
            dv_ref[...] += dv
    lanes = lax.broadcasted_iota(jnp.int32, (EDGE, 128), 1)
    keyval = jnp.where(lanes < HEAD, dk_ref[...] * (HEAD**-0.5), dv_ref[...]).astype(BF16)
    query = (dq_ref[...].T * (HEAD**-0.5)).astype(BF16)
    out[:, :128] = dot(tiles[...], keyval, 1, 0).astype(BF16)
    out[:, 128:] = dot(tiles[...], query, 1, 0).astype(BF16)


def run_coarse_backward(place, every, stats):
    strips = jnp.asarray(strip_pick(), BF16)
    tiles = jnp.asarray(tile_pick(), BF16)
    return pl.pallas_call(
        coarse_backward,
        out_shape=jax.ShapeDtypeStruct((H1 * EXT, 256), BF16),
        in_specs=[pl.BlockSpec(memory_space=pltpu.SMEM)] + [whole()] * 4,
        out_specs=whole(),
        scratch_shapes=[
            pltpu.VMEM((EDGE, 256), BF16),
            pltpu.VMEM((128, EDGE), F32),
            pltpu.VMEM((EDGE, 128), F32),
            pltpu.VMEM((EDGE, 128), F32),
        ],
        compiler_params=vmem_params(20),
        cost_estimate=pl.CostEstimate(flops=3 * 10**9, bytes_accessed=2 * 10**6, transcendentals=4 * 10**6),
        name="coarse_backward",
    )(place, every, stats, strips, tiles)


def block_pick():
    c, b = np.meshgrid(np.arange(H1), np.arange(64), indexing="ij")
    source = np.where(b < 48, 48 * c + b, 3 * D0 + 16 * c + b - 48).reshape(-1)
    pick = np.zeros((4 * D0, 4 * D0), np.float32)
    pick[source, np.arange(4 * D0)] = 1
    return pick


def backward_kernel(
    place,
    terms_coarse,
    grads,
    grads_left,
    grads_right,
    coarse,
    lse,
    gain_coarse,
    gain,
    w_qkv,
    w_out,
    pick_block,
    w_merge_far,
    w_coarse_far,
    stash_far,
    grad_tokens,
    terms,
    grad_fine,
    sp32,
    gh_ref,
    ga_ref,
    dq_ref,
    dk_ref,
    dv_ref,
    gt_ref,
    stash,
    w_merge,
    w_coarse,
    merge_sems,
    coarse_sems,
    stash_sem,
):
    merge_copies = fetch(w_merge_far, w_merge, merge_sems, 4)
    coarse_copies = fetch(w_coarse_far, w_coarse, coarse_sems, 4)
    stash_copy = pltpu.make_async_copy(stash_far, stash, stash_sem)
    for copy in coarse_copies + merge_copies + [stash_copy]:
        copy.start()
    queries = stash.at[pl.ds(AT_Q, N4)]
    attended = stash.at[pl.ds(AT_ATT, N4)]
    keys_w = stash.at[pl.ds(AT_K, WROWS * C4)]
    values_w = stash.at[pl.ds(AT_V, WROWS * C4)]
    tokens_own = stash.at[pl.ds(AT_X, OWN)]
    row0 = place[0]
    col0 = place[1]
    wide = CCOLS + 2
    grad_coarse = []
    for i in range(CROWS + 2):
        parts = []
        for a in range(4):
            own = grads[4 * i + a].astype(F32)
            left = grads_left[4 * i + a].astype(F32)
            right = grads_right[4 * i + a].astype(F32)
            at = C4 * (4 * i + a)
            grad_fine[at : at + C4] = jnp.concatenate([left[:4], own[:COLS], right[:4]], axis=0)
            parts.append(jnp.concatenate([left[4:], own[COLS:], right[4:]], axis=0))
        grad_coarse.append(jnp.concatenate(parts, axis=1))
    grad_coarse = jnp.concatenate(grad_coarse, axis=0)
    parts = []
    for h in range(H1):
        block = terms_coarse[h].astype(F32)
        parts += [block[:, 128:192], block[:, :128]]
    heads = jnp.concatenate(parts, axis=1).astype(BF16)
    parts = []
    for n, copy in enumerate(coarse_copies):
        copy.wait()
        parts.append(dot(heads, w_coarse[256 * n : 256 * (n + 1)], 1, 1))
    upstream = jnp.concatenate(parts, axis=1) * gain_coarse[...]
    normed, inverse = norm_forward(coarse[...].astype(F32))
    back = norm_backward(upstream, normed, inverse)
    change = (grad_coarse + back).astype(BF16)
    for a, copy in enumerate(merge_copies):
        copy.wait()
        spread = dot(change, w_merge[D1 * a : D1 * (a + 1)], 1, 1)
        for i in range(CROWS + 2):
            for c in range(MERGE):
                for half in range(2):
                    at = c * D0 + half * 128
                    sp32[half, pl.ds((4 * i + a) * C4 + c, wide, stride=MERGE), :] = spread[
                        wide * i : wide * (i + 1), at : at + 128
                    ]
    for half in range(2):
        at = slice(half * 128, (half + 1) * 128)
        gh_ref[:, at] = (grad_fine[:, at] + sp32[half]).astype(BF16)
    ga_ref[...] = dot(gh_ref[...], w_out[...], 1, 1).astype(BF16)
    stash_copy.wait()
    dk_ref[...] = jnp.zeros_like(dk_ref)
    dv_ref[...] = jnp.zeros_like(dv_ref)
    pick = (
        lax.broadcasted_iota(jnp.int32, (8, D0), 1) // HEAD
        == lax.broadcasted_iota(jnp.int32, (8, D0), 0)
    ).astype(F32)
    for b in range(BLOCKS):
        at = slice(BLOCK * b, BLOCK * (b + 1))
        keep = slice(BLOCK * b, BLOCK * b + 10 * C4)
        grad = ga_ref[at].astype(F32)
        product = grad * attended[at].astype(F32)
        sums = lax.dot_general(
            pick,
            product,
            (((1,), (1,)), ((), ())),
            precision=lax.Precision.HIGHEST,
            preferred_element_type=F32,
        )
        stat = jnp.concatenate([sums[h : h + 1] for h in range(H0)], axis=1)
        stack_q = stack_heads(queries[at].astype(F32)).astype(BF16)
        stack_g = stack_heads(grad).astype(BF16)
        key_block = keys_w[keep]
        bias = window_bias(C4, -3, row0 - 7 + 4 * b, col0 - 4)
        scores = dot(key_block, stack_q, 1, 1) + jnp.concatenate([bias] * H0, axis=1)
        probs = jnp.exp(scores - lse[b : b + 1])
        slopes = (probs * (dot(values_w[keep], stack_g, 1, 1) - stat)).astype(BF16)
        dk_ref[keep] += dot(slopes, stack_q, 1, 0)
        dv_ref[keep] += dot(probs.astype(BF16), stack_g, 1, 0)
        if 1 <= b <= 4:
            dq = unstack_heads(dot(slopes, key_block, 0, 0)) * (HEAD**-0.5)
            dq_ref[BLOCK * (b - 1) : BLOCK * b] = dq.astype(BF16)
    own = slice(7 * C4, 7 * C4 + OWN)
    grads = jnp.concatenate(
        [dq_ref[...], dk_ref[own].astype(BF16), dv_ref[own].astype(BF16)], axis=1
    )
    column = lax.broadcasted_iota(jnp.int32, (ROWS, C4, D0), 1).reshape(OWN, D0)
    in_tile = (column >= 4) & (column < 4 + COLS)
    normed, inverse = norm_forward(tokens_own[...].astype(F32))
    rounded = jnp.where(in_tile, normed * gain[...], 0.0).astype(BF16)
    term_qkv = dot(rounded, grads, 0, 0).astype(BF16)
    inner = slice(BLOCK, BLOCK + OWN)
    att = jnp.where(in_tile, attended[inner].astype(F32), 0.0).astype(BF16)
    term_out = dot(att, gh_ref[inner], 0, 0).astype(BF16)
    both = dot(jnp.concatenate([term_qkv, term_out], axis=1), pick_block[...], 1, 0)
    low = lax.broadcasted_iota(jnp.int32, (16, 128), 1) < 64
    for r in range(8):
        for m in range(8):
            first = both[32 * r : 32 * r + 16, 128 * m : 128 * (m + 1)]
            last = both[32 * r + 16 : 32 * (r + 1), 128 * m : 128 * (m + 1)]
            terms[16 * r + 2 * m] = jnp.where(low, first, pltpu.roll(last, 64, 1)).astype(BF16)
            terms[16 * r + 2 * m + 1] = jnp.where(low, pltpu.roll(first, 64, 1), last).astype(BF16)
    upstream = dot(grads, w_qkv[...], 1, 1) * gain[...]
    gt_ref[...] = gh_ref[inner].astype(F32) + norm_backward(upstream, normed, inverse)
    for pair in range(ROWS // 2):
        parts = [gt_ref[pl.ds(i * C4 + 4, COLS), :] for i in (2 * pair, 2 * pair + 1)]
        grad_tokens[2 * COLS * pair : 2 * COLS * (pair + 1)] = jnp.concatenate(
            parts, axis=0
        ).astype(BF16)


def run_backward(place, *operands):
    shapes = [((ROWS * COLS, D0), BF16), ((128, 16, 128), BF16)]
    return pl.pallas_call(
        backward_kernel,
        out_shape=[jax.ShapeDtypeStruct(s, d) for s, d in shapes],
        in_specs=[pl.BlockSpec(memory_space=pltpu.SMEM)] + [whole()] * 11 + [far()] * 3,
        out_specs=[whole()] * 2,
        scratch_shapes=[
            pltpu.VMEM((N4, D0), F32),
            pltpu.VMEM((2, N4, 128), F32),
            pltpu.VMEM((N4, D0), BF16),
            pltpu.VMEM((N4, D0), BF16),
            pltpu.VMEM((OWN, D0), BF16),
            pltpu.VMEM((WROWS * C4, D0), F32),
            pltpu.VMEM((WROWS * C4, D0), F32),
            pltpu.VMEM((OWN, D0), F32),
            pltpu.VMEM((STASH, D0), BF16),
            pltpu.VMEM((MERGE * MERGE * D0, D1), BF16),
            pltpu.VMEM((D1, 3 * D1), BF16),
            pltpu.SemaphoreType.DMA((4,)),
            pltpu.SemaphoreType.DMA((4,)),
            pltpu.SemaphoreType.DMA(()),
        ],
        compiler_params=vmem_params(48),
        cost_estimate=pl.CostEstimate(flops=5 * 10**9, bytes_accessed=2 * 10**7, transcendentals=10**6),
        name="backward_kernel",
    )(place, *operands)


def sum_terms(terms, out_qkv, out_out):
    total = jnp.sum(terms[...].astype(F32), axis=0)
    total = jnp.concatenate([total[:, :64], total[:, 64:]], axis=0)
    out_qkv[...] = total[:, :48]
    out_out[...] = total[:, 48:].T


def run_sum_terms(terms):
    return pl.pallas_call(
        sum_terms,
        out_shape=[jax.ShapeDtypeStruct((32, 48), F32), jax.ShapeDtypeStruct((16, 32), F32)],
        in_specs=[whole()],
        out_specs=[whole()] * 2,
        compiler_params=vmem_params(8),
        name="sum_terms",
    )(terms)


def ring(axis, step):
    devices = lax.axis_size(axis)
    return [(i, (i + step) % devices) for i in range(devices)]


def swap_edges(first, last, axis):
    before = lax.ppermute(last, axis, ring(axis, 1))
    after = lax.ppermute(first, axis, ring(axis, -1))
    return before, after


def token_halo(tokens, width):
    above, below = swap_edges(tokens[:width], tokens[-width:], "row")
    first = jnp.concatenate([above[:, :width], tokens[:, :width], below[:, :width]], axis=0)
    last = jnp.concatenate([above[:, -width:], tokens[:, -width:], below[:, -width:]], axis=0)
    left, right = swap_edges(first, last, "col")
    return tokens, above, below, left, right


def grad_rows(grad_fine, grad_coarse):
    folded = grad_coarse.reshape(CROWS, CCOLS, 4, D0).transpose(0, 2, 1, 3)
    both = jnp.concatenate([grad_fine, folded.reshape(ROWS, CCOLS, D0)], axis=1)
    above, below = swap_edges(both[:4], both[-4:], "row")
    return jnp.concatenate([above, both, below], axis=0)


def grad_sides(both):
    first = jnp.concatenate([both[:, :4], both[:, COLS : COLS + 1]], axis=1)
    last = jnp.concatenate([both[:, COLS - 4 : COLS], both[:, -1:]], axis=1)
    return first, last


def on_device(
    tokens,
    grad_fine,
    grad_coarse,
    fine_gain,
    fine_qkv,
    fine_out,
    merge_weight,
    coarse_gain,
    coarse_qkv,
    coarse_out,
):
    row = lax.axis_index("row")
    col = lax.axis_index("col")
    place = jnp.stack([row * ROWS, col * COLS, row]).astype(jnp.int32)
    pieces = token_halo(tokens, 8)
    grad_heads = jnp.dot(
        grad_coarse.reshape(-1, D1), coarse_out.T, preferred_element_type=F32
    ).astype(BF16)
    stash, lse, coarse, packed = run_forward(
        place,
        pieces,
        fine_gain,
        fine_qkv,
        fine_out,
        merge_weight,
        coarse_gain,
        coarse_qkv,
        grad_heads,
    )
    every = lax.all_to_all(
        packed.reshape(8 * H1, CROWS * CCOLS, 256),
        ("row", "col"),
        split_axis=0,
        concat_axis=0,
        tiled=True,
    )
    coarse, grad_fine, grad_coarse = lax.optimization_barrier((coarse, grad_fine, grad_coarse))
    both = grad_rows(grad_fine, grad_coarse)
    every, both = lax.optimization_barrier((every, both))
    every = every.reshape(SLAB * SLABS, 256)
    stats = run_coarse_forward(place, every)
    stats, both = lax.optimization_barrier((stats, both))
    stats = lax.all_to_all(stats, "row", split_axis=0, concat_axis=0, tiled=True)
    left, right = swap_edges(*grad_sides(both), "col")
    stats, left, right = lax.optimization_barrier((stats, left, right))
    tiles = run_coarse_backward(place, every, stats).reshape(H1, EXT, 256)
    terms = lax.all_to_all(tiles, "col", split_axis=0, concat_axis=0, tiled=True)
    grad_tokens, blocks = run_backward(
        place,
        terms,
        both,
        left,
        right,
        coarse,
        lse,
        coarse_gain.reshape(1, D1),
        fine_gain.reshape(1, D0),
        fine_qkv,
        fine_out,
        jnp.asarray(block_pick(), BF16),
        merge_weight,
        coarse_qkv,
        stash,
    )
    blocks = lax.all_to_all(blocks, ("row", "col"), split_axis=0, concat_axis=0, tiled=True)
    grad_qkv, grad_out = run_sum_terms(blocks)
    return grad_tokens.reshape(ROWS, COLS, D0), grad_qkv, grad_out.T


def solution(mesh):
    return jax.shard_map(
        on_device,
        mesh=mesh,
        in_specs=(P("row", "col", None),) * 3 + (P(),) * 7,
        out_specs=(P("row", "col", None), P("row", "col"), P("row", "col")),
        check_vma=False,
    )
```

```python
import jax
import jax.numpy as jnp
import numpy as np
from jax import lax
from jax.experimental import pallas as pl
from jax.experimental.pallas import tpu as pltpu
from jax.sharding import PartitionSpec as P

H0 = 4
H1 = 16
HEAD = 64
MERGE = 4
EPSILON = 1e-05
FAR = 1e30
D0 = 256
D1 = 1024

ROWS, COLS = 16, 24
CROWS, CCOLS = 4, 6
R8, C8 = ROWS + 16, COLS + 16
R4, C4 = ROWS + 8, COLS + 8
N4 = R4 * C4
BLOCK = 4 * C4
BLOCKS = R4 // 4
WROWS = R4 + 6
OWN = ROWS * C4
EXT = (CROWS + 2) * (CCOLS + 2)

F32 = jnp.float32
BF16 = jnp.bfloat16


def vmem_params(mib):
    return pltpu.CompilerParams(vmem_limit_bytes=mib * 1024 * 1024)


def whole():
    return pl.BlockSpec(memory_space=pltpu.VMEM)


def far():
    return pl.BlockSpec(memory_space=pltpu.HBM)


def fetch(source, target, sems, pieces):
    rows = source.shape[0] // pieces
    return [
        pltpu.make_async_copy(
            source.at[pl.ds(n * rows, rows)], target.at[pl.ds(n * rows, rows)], sems.at[n]
        )
        for n in range(pieces)
    ]


def dot(a, b, ca, cb):
    return lax.dot_general(a, b, (((ca,), (cb,)), ((), ())), preferred_element_type=F32)


def norm_forward(values):
    center = values - jnp.mean(values, axis=-1, keepdims=True)
    inverse = lax.rsqrt(jnp.mean(center * center, axis=-1, keepdims=True) + EPSILON)
    return center * inverse, inverse


def norm_backward(scaled, normed, inverse):
    return inverse * (
        scaled
        - jnp.mean(scaled, axis=-1, keepdims=True)
        - normed * jnp.mean(scaled * normed, axis=-1, keepdims=True)
    )


def head_lanes(rows):
    return lax.broadcasted_iota(jnp.int32, (rows, D0), 1) // HEAD


def stack_heads(values):
    lanes = head_lanes(values.shape[0])
    zero = jnp.zeros_like(values)
    return jnp.concatenate([jnp.where(lanes == h, values, zero) for h in range(H0)], axis=0)


def unstack_heads(stacked):
    rows = stacked.shape[0] // H0
    lanes = head_lanes(rows)
    result = stacked[:rows]
    for h in range(1, H0):
        result = jnp.where(lanes == h, stacked[h * rows : (h + 1) * rows], result)
    return result


AT_Q = 0
AT_ATT = N4
AT_K = 2 * N4
AT_V = AT_K + WROWS * C4
AT_X = AT_V + WROWS * C4
STASH = AT_X + OWN


def window_bias(key_cols, col_shift):
    shape = (10, key_cols, BLOCK)
    kr = lax.broadcasted_iota(jnp.int32, shape, 0)
    kc = lax.broadcasted_iota(jnp.int32, shape, 1)
    lane = lax.broadcasted_iota(jnp.int32, shape, 2)
    row_gap = kr - lane // C4
    col_gap = kc - lane % C4 - col_shift
    near = (row_gap >= 0) & (row_gap <= 6) & (col_gap >= 0) & (col_gap <= 6)
    return jnp.where(near, 0.0, -FAR).reshape(10 * key_cols, BLOCK)


def key_bias(key_cols, key_row, key_col):
    shape = (10, key_cols, 1)
    grid_row = key_row + lax.broadcasted_iota(jnp.int32, shape, 0)
    grid_col = key_col + lax.broadcasted_iota(jnp.int32, shape, 1)
    inside = (grid_row >= 0) & (grid_row < 128) & (grid_col >= 0) & (grid_col < 384)
    return jnp.where(inside, 0.0, -FAR).reshape(10 * key_cols, 1)


def all_heads(bias):
    return jnp.concatenate([bias] * H0, axis=1)


def near_kernel(
    place,
    tokens,
    above,
    below,
    left,
    right,
    gain,
    w_qkv,
    w_out,
    w_merge_far,
    gain_coarse,
    w_coarse_far,
    grads,
    packed_far,
    x32,
    keys,
    values,
    hid32,
    merged,
    w_merge,
    w_coarse,
    packed,
    merge_sems,
    coarse_sems,
    packed_sems,
):
    merge_copies = fetch(w_merge_far, w_merge, merge_sems, 4)
    coarse_copies = fetch(w_coarse_far, w_coarse, coarse_sems, 2)
    for copy in merge_copies + coarse_copies:
        copy.start()
    row0 = place[0]
    col0 = place[1]
    middle = [part[: 8 * COLS].astype(F32) for part in (above, below)]
    middle.insert(1, tokens[...].astype(F32))
    sides = [left[...].astype(F32), right[...].astype(F32)]
    for t in range(ROWS + 6):
        e = t + 5
        part, at = (0, e) if e < 8 else (1, e - 8) if e < 8 + ROWS else (2, e - 8 - ROWS)
        x32[C4 * t : C4 * (t + 1)] = jnp.concatenate(
            [
                sides[0][8 * e + 4 : 8 * e + 8],
                middle[part][COLS * at : COLS * (at + 1)],
                sides[1][8 * e : 8 * e + 4],
            ],
            axis=0,
        )
    normed, _ = norm_forward(x32[...])
    normed = (normed * gain[...]).astype(BF16)
    inner = slice(3 * C4, 3 * C4 + OWN)
    queries = dot(normed[inner], w_qkv[:, :D0], 1, 0).astype(BF16).astype(F32) * (HEAD**-0.5)
    keys[...] = dot(normed, w_qkv[:, D0 : 2 * D0], 1, 0).astype(BF16)
    values[...] = dot(normed, w_qkv[:, 2 * D0 :], 1, 0).astype(BF16)
    window = window_bias(C4, -3)
    for b in range(ROWS // 4):
        block = slice(BLOCK * b, BLOCK * b + 10 * C4)
        stacked = stack_heads(queries[BLOCK * b : BLOCK * (b + 1)]).astype(BF16)
        bias = all_heads(window + key_bias(C4, row0 - 3 + 4 * b, col0 - 4))
        scores = dot(keys[block], stacked, 1, 1) + bias
        maxima = jnp.max(scores, axis=0, keepdims=True)
        exponent = jnp.exp(scores - maxima)
        totals = jnp.sum(exponent, axis=0, keepdims=True)
        weights = (exponent * (1.0 / totals)).astype(BF16)
        attended = unstack_heads(dot(weights, values[block], 0, 0)).astype(BF16)
        at = BLOCK * b
        own = x32[3 * C4 + at : 3 * C4 + at + BLOCK]
        total = (own + dot(attended, w_out[...], 1, 0)).astype(BF16).astype(F32)
        hid32[0, at : at + BLOCK] = total[:, :128]
        hid32[1, at : at + BLOCK] = total[:, 128:]
    wide = CCOLS + 2
    merge_rows(hid32, merged, CROWS)
    total = None
    for n, copy in enumerate(merge_copies):
        copy.wait()
        part = dot(merged[:, D1 * n : D1 * (n + 1)], w_merge[D1 * n : D1 * (n + 1)], 1, 0)
        total = part if total is None else total + part
    normed, _ = norm_forward(total.astype(BF16).astype(F32))
    normed = normed * gain_coarse[...]
    parts = [normed[wide * i + 1 : wide * i + 1 + CCOLS] for i in range(CROWS)]
    normed = jnp.concatenate(parts, axis=0).astype(BF16)
    for copy in coarse_copies:
        copy.wait()
    packed_copies = []
    for n in range(4):
        result = dot(normed, w_coarse[:, 768 * n : 768 * (n + 1)], 1, 0)
        grad = grads[:, 256 * n : 256 * (n + 1)].astype(F32)
        parts = []
        for h in range(4):
            q = result[:, 192 * h : 192 * h + 64]
            k = result[:, 192 * h + 64 : 192 * h + 128]
            v = result[:, 192 * h + 128 : 192 * h + 192]
            g = grad[:, 64 * h : 64 * h + 64]
            parts.append(jnp.concatenate([k, v, q, g], axis=1))
        packed[2 * n] = jnp.concatenate(parts[:2], axis=0).astype(BF16)
        packed[2 * n + 1] = jnp.concatenate(parts[2:], axis=0).astype(BF16)
        at = pl.ds(2 * n, 2)
        for r in range(8):
            packed_copies.append(
                pltpu.make_async_copy(packed.at[at], packed_far.at[r, at], packed_sems.at[n, r])
            )
            packed_copies[-1].start()
    for copy in packed_copies:
        copy.wait()


def merge_rows(hid32, merged, count):
    for pair in range(count // 2):
        for a in range(MERGE):
            for c in range(MERGE):
                for half in range(2):
                    parts = [
                        hid32[half, pl.ds((4 * i + a) * C4 + c, CCOLS + 2, stride=MERGE), :]
                        for i in (2 * pair, 2 * pair + 1)
                    ]
                    at = (a * MERGE + c) * D0 + half * 128
                    merged[16 * pair : 16 * (pair + 1), at : at + 128] = jnp.concatenate(
                        parts, axis=0
                    ).astype(BF16)


def run_near(place, pieces, gain, w_qkv, w_out, w_merge, gain_coarse, w_coarse, grads):
    own = CROWS * CCOLS
    return pl.pallas_call(
        near_kernel,
        out_shape=pltpu.HBM((8, 8, 2 * own, 256), BF16),
        in_specs=[pl.BlockSpec(memory_space=pltpu.SMEM)]
        + [whole()] * 8
        + [far(), whole(), far(), whole()],
        out_specs=far(),
        scratch_shapes=[
            pltpu.VMEM(((ROWS + 6) * C4, D0), F32),
            pltpu.VMEM(((ROWS + 6) * C4, D0), BF16),
            pltpu.VMEM(((ROWS + 6) * C4, D0), BF16),
            pltpu.VMEM((2, OWN, 128), F32),
            pltpu.VMEM((CROWS * (CCOLS + 2), MERGE * MERGE * D0), BF16),
            pltpu.VMEM(w_merge.shape, BF16),
            pltpu.VMEM(w_coarse.shape, BF16),
            pltpu.VMEM((8, 2 * own, 256), BF16),
            pltpu.SemaphoreType.DMA((4,)),
            pltpu.SemaphoreType.DMA((2,)),
            pltpu.SemaphoreType.DMA((4, 8)),
        ],
        compiler_params=vmem_params(48),
        cost_estimate=pl.CostEstimate(flops=3 * 10**9, bytes_accessed=2 * 10**7, transcendentals=10**6),
        name="near_kernel",
    )(
        place,
        *[piece.reshape(-1, D0) for piece in pieces],
        gain.reshape(1, D0),
        w_qkv,
        w_out,
        in_hbm(w_merge),
        gain_coarse.reshape(1, D1),
        in_hbm(w_coarse),
        grads,
    )


def in_hbm(array):
    return pltpu.with_memory_space_constraint(array, pltpu.HBM)


def wide_kernel(
    place,
    tokens,
    above,
    below,
    left,
    right,
    gain,
    w_qkv,
    w_out,
    w_merge_far,
    stash_far,
    lse,
    coarse_out,
    x32,
    q32,
    k32,
    v32,
    hid32,
    stash,
    merged,
    w_merge,
    merge_sems,
    stash_sem,
):
    merge_copies = fetch(w_merge_far, w_merge, merge_sems, 4)
    for copy in merge_copies:
        copy.start()
    queries = stash.at[pl.ds(AT_Q, N4)]
    attended = stash.at[pl.ds(AT_ATT, N4)]
    keys_w = stash.at[pl.ds(AT_K, WROWS * C4)]
    values_w = stash.at[pl.ds(AT_V, WROWS * C4)]
    tokens_own = stash.at[pl.ds(AT_X, OWN)]
    row0 = place[0]
    col0 = place[1]
    middle = [part[: 8 * COLS].astype(F32) for part in (above, below)]
    middle.insert(1, tokens[...].astype(F32))
    sides = [left[...].astype(F32), right[...].astype(F32)]
    for i in range(R8):
        part, at = (0, i) if i < 8 else (1, i - 8) if i < 8 + ROWS else (2, i - 8 - ROWS)
        x32[C8 * i : C8 * i + 8] = sides[0][8 * i : 8 * i + 8]
        x32[C8 * i + 8 : C8 * i + 8 + COLS] = middle[part][COLS * at : COLS * (at + 1)]
        x32[C8 * i + 8 + COLS : C8 * (i + 1)] = sides[1][8 * i : 8 * i + 8]
    normed, _ = norm_forward(x32[...])
    normed = (normed * gain[...]).astype(BF16)
    q32[...] = dot(normed, w_qkv[:, :D0], 1, 0).astype(BF16).astype(F32) * (HEAD**-0.5)
    k32[...] = dot(normed, w_qkv[:, D0 : 2 * D0], 1, 0).astype(BF16).astype(F32)
    v32[...] = dot(normed, w_qkv[:, 2 * D0 :], 1, 0).astype(BF16).astype(F32)
    for i in range(R4):
        queries[C4 * i : C4 * (i + 1)] = q32[pl.ds((i + 4) * C8 + 4, C4), :].astype(BF16)
    for i in range(WROWS):
        keys_w[C4 * i : C4 * (i + 1)] = k32[pl.ds((i + 1) * C8 + 4, C4), :].astype(BF16)
        values_w[C4 * i : C4 * (i + 1)] = v32[pl.ds((i + 1) * C8 + 4, C4), :].astype(BF16)
    for i in range(ROWS):
        tokens_own[C4 * i : C4 * (i + 1)] = x32[pl.ds((i + 8) * C8 + 4, C4), :].astype(BF16)
    lse[...] = jnp.full(lse.shape, FAR, F32)
    window = window_bias(C8, 1)
    for b in range(BLOCKS):
        start = (4 * b + 1) * C8
        key_block = k32[start : start + 10 * C8].astype(BF16)
        value_block = v32[start : start + 10 * C8].astype(BF16)
        stacked = stack_heads(queries[BLOCK * b : BLOCK * (b + 1)].astype(F32)).astype(BF16)
        bias = all_heads(window + key_bias(C8, row0 - 7 + 4 * b, col0 - 8))
        scores = dot(key_block, stacked, 1, 1) + bias
        maxima = jnp.max(scores, axis=0, keepdims=True)
        exponent = jnp.exp(scores - maxima)
        totals = jnp.sum(exponent, axis=0, keepdims=True)
        weights = (exponent * (1.0 / totals)).astype(BF16)
        result = unstack_heads(dot(weights, value_block, 0, 0)).astype(BF16)
        attended[BLOCK * b : BLOCK * (b + 1)] = result
        lane = lax.broadcasted_iota(jnp.int32, (1, H0 * BLOCK), 1) % BLOCK
        q_row = row0 - 4 + 4 * b + lane // C4
        q_col = col0 - 4 + lane % C4
        q_in = (q_row >= 0) & (q_row < 128) & (q_col >= 0) & (q_col < 384)
        lse[b : b + 1] = jnp.where(q_in, maxima + jnp.log(totals), FAR)
        projected = dot(result, w_out[...], 1, 0)
        for a in range(4):
            own = x32[pl.ds((4 * b + a + 4) * C8 + 4, C4), :]
            total = own + projected[C4 * a : C4 * (a + 1)]
            at = BLOCK * b + C4 * a
            total = total.astype(BF16).astype(F32)
            hid32[0, at : at + C4] = total[:, :128]
            hid32[1, at : at + C4] = total[:, 128:]
    merge_rows(hid32, merged, CROWS + 2)
    stash_copy = pltpu.make_async_copy(stash, stash_far, stash_sem)
    stash_copy.start()
    total = None
    for n, copy in enumerate(merge_copies):
        copy.wait()
        part = dot(merged[:, D1 * n : D1 * (n + 1)], w_merge[D1 * n : D1 * (n + 1)], 1, 0)
        total = part if total is None else total + part
    coarse_out[...] = total.astype(BF16)
    stash_copy.wait()


def run_wide(place, pieces, gain, w_qkv, w_out, w_merge):
    flat = R8 * C8
    return pl.pallas_call(
        wide_kernel,
        out_shape=[
            pltpu.HBM((STASH, D0), BF16),
            pltpu.HBM((8, H0 * BLOCK), F32),
            pltpu.HBM((EXT, D1), BF16),
        ],
        in_specs=[pl.BlockSpec(memory_space=pltpu.SMEM)] + [whole()] * 8 + [far()],
        out_specs=[far(), whole(), whole()],
        scratch_shapes=[pltpu.VMEM((flat, D0), F32)] * 4
        + [
            pltpu.VMEM((2, N4, 128), F32),
            pltpu.VMEM((STASH, D0), BF16),
            pltpu.VMEM((EXT, MERGE * MERGE * D0), BF16),
            pltpu.VMEM(w_merge.shape, BF16),
            pltpu.SemaphoreType.DMA((4,)),
            pltpu.SemaphoreType.DMA(()),
        ],
        compiler_params=vmem_params(40),
        cost_estimate=pl.CostEstimate(flops=3 * 10**9, bytes_accessed=10**7, transcendentals=10**6),
        name="wide_kernel",
    )(
        place,
        *[piece.reshape(-1, D0) for piece in pieces],
        gain.reshape(1, D0),
        w_qkv,
        w_out,
        in_hbm(w_merge),
    )


def lane_half(values, low):
    lanes = lax.broadcasted_iota(jnp.int32, values.shape, 1)
    keep = lanes < HEAD if low else lanes >= HEAD
    return jnp.where(keep, values, jnp.zeros_like(values))


SLAB = 384
SLABS = 8
STRIP = 96
EDGE = SLAB + 2 * STRIP


def strip_pick():
    tile, j = np.divmod(np.arange(STRIP), CCOLS)
    pick = np.zeros((2, STRIP, SLAB), np.float32)
    last = (CROWS - 1) * CCOLS
    pick[0, np.arange(STRIP), tile * CROWS * CCOLS + last + j] = 1
    pick[1, np.arange(STRIP), tile * CROWS * CCOLS + j] = 1
    return pick


def tile_pick():
    c, i, j = np.meshgrid(np.arange(H1), np.arange(6), np.arange(8), indexing="ij")
    tile = (c + (j == 7) - (j == 0)) % H1
    jj = np.where(j == 0, 5, np.where(j == 7, 0, j - 1))
    middle = tile * 24 + (i - 1) * 6 + jj
    source = np.where(i == 0, SLAB + tile * 6 + jj, np.where(i == 5, SLAB + STRIP + tile * 6 + jj, middle))
    pick = np.zeros((H1 * EXT, EDGE), np.float32)
    pick[np.arange(H1 * EXT), source.reshape(-1)] = 1
    return pick


def coarse_forward(place, every, stats, scores_ref):
    keyval = every[:, :128]
    own = every[pl.ds(pl.multiple_of(place[2] * SLAB, SLAB), SLAB), 128:]
    queries = lane_half(own.astype(F32) * (HEAD**-0.5), True).astype(BF16)
    columns = []
    for b in range(3):
        rows = slice(128 * b, 128 * (b + 1))
        scores_ref[b] = dot(queries[rows], keyval, 1, 1)
        maxima = jnp.max(scores_ref[b], axis=1, keepdims=True)
        exponent = jnp.exp(scores_ref[b] - maxima)
        totals = jnp.sum(exponent, axis=1, keepdims=True)
        weights = (exponent * (1.0 / totals)).astype(BF16)
        attended = dot(weights, keyval, 1, 0).astype(BF16).astype(F32)
        product = lane_half(own[rows].astype(F32) * attended, False)
        columns.append((maxima + jnp.log(totals), jnp.sum(product, axis=1, keepdims=True)))
    lane = lax.broadcasted_iota(jnp.int32, (128, 128), 1)
    turned = [
        jnp.where(lane == 0, log, jnp.where(lane == 1, stat, 0.0)).T for log, stat in columns
    ]
    result = jnp.concatenate(
        [t[0:1] for t in turned] + [t[1:2] for t in turned] + [jnp.zeros((2, 128), F32)], axis=0
    )
    for r in range(SLABS):
        stats[r] = result


def run_coarse_forward(place, every):
    return pl.pallas_call(
        coarse_forward,
        out_shape=jax.ShapeDtypeStruct((SLABS, 8, 128), F32),
        in_specs=[pl.BlockSpec(memory_space=pltpu.SMEM), whole()],
        out_specs=whole(),
        scratch_shapes=[pltpu.VMEM((3, 128, SLAB * SLABS), F32)],
        compiler_params=vmem_params(16),
        cost_estimate=pl.CostEstimate(flops=10**9, bytes_accessed=2 * 10**6, transcendentals=10**6),
        name="coarse_forward",
    )(place, every)


def stat_rows(stats):
    lse = jnp.concatenate([stats[k : k + 1] for k in range(3)], axis=1)
    stat = jnp.concatenate([stats[k : k + 1] for k in range(3, 6)], axis=1)
    return lse, stat


def slab_rows(index):
    return pl.ds(pl.multiple_of(index * SLAB, SLAB), SLAB)


def turn(lse, stat):
    filler = jnp.zeros((128 - 2, lse.shape[1]), F32)
    turned = jnp.concatenate([lse, stat, filler], axis=0).T
    return turned[:, 0:1], turned[:, 1:2]


def query_side(every, rows, queries, grads, lse, stat):
    keyval = every[rows, :128]
    probs = jnp.exp(dot(queries, keyval, 1, 1) - lse)
    slopes = (probs * (dot(grads, keyval, 1, 1) - stat)).astype(BF16)
    return dot(slopes, keyval, 1, 0)


def halves(pair):
    wide = pair.astype(F32)
    return lane_half(wide * (HEAD**-0.5), True).astype(BF16), lane_half(wide, False).astype(BF16)


def coarse_own(place, every, stats, strips, edge, dq_out, dq_ref):
    row = place[2]
    edge[:SLAB] = every[slab_rows(row)]
    others = (lax.rem(row + SLABS - 1, SLABS), lax.rem(row + 1, SLABS))
    for k, other in enumerate(others):
        at = SLAB + STRIP * k
        edge[at : at + STRIP] = dot(strips[k], every[slab_rows(other)], 1, 0).astype(BF16)
    lse, stat = turn(*stat_rows(stats[0]))
    queries, grads = halves(edge[:SLAB, 128:])
    for n in range(SLABS // 2):
        rows = slice(2 * n * SLAB, 2 * (n + 1) * SLAB)
        term = query_side(every, rows, queries, grads, lse, stat)
        dq_ref[...] = term if n == 0 else dq_ref[...] + term
    dq_out[...] = (dq_ref[...] * (HEAD**-0.5)).astype(BF16)


def run_coarse_own(place, every, stats, strips):
    return pl.pallas_call(
        coarse_own,
        out_shape=[
            pltpu.HBM((EDGE, 256), BF16),
            pltpu.HBM((SLAB, 128), BF16),
        ],
        in_specs=[pl.BlockSpec(memory_space=pltpu.SMEM)] + [whole()] * 3,
        out_specs=[whole()] * 2,
        scratch_shapes=[pltpu.VMEM((SLAB, 128), F32)],
        compiler_params=vmem_params(24),
        cost_estimate=pl.CostEstimate(flops=10**9, bytes_accessed=2 * 10**6, transcendentals=10**6),
        name="coarse_own",
    )(place, every, stats, strips)


def coarse_backward(
    place,
    every,
    stats,
    strips,
    edge,
    dq_own,
    tiles_far,
    coarse_far,
    stash_far,
    out,
    w_coarse,
    stash,
    dq_ref,
    dk_ref,
    dv_ref,
    tiles,
    sems,
):
    pairs = (
        (tiles_far, tiles),
        (coarse_far, w_coarse),
        (stash_far, stash),
    )
    copies = [pltpu.make_async_copy(a, b, sems.at[n]) for n, (a, b) in enumerate(pairs)]
    for copy in copies:
        copy.start()
    row = place[2]
    others = (lax.rem(row + SLABS - 1, SLABS), lax.rem(row + 1, SLABS))
    taken = []
    for k, other in enumerate(others):
        both = jnp.concatenate(stat_rows(stats[other]) + (jnp.zeros((6, SLAB), F32),), axis=0)
        taken.append(
            lax.dot_general(
                both,
                strips[k].astype(F32),
                (((1,), (1,)), ((), ())),
                precision=lax.Precision.HIGHEST,
                preferred_element_type=F32,
            )
        )
    strip_lse, strip_stat = turn(
        jnp.concatenate([t[0:1] for t in taken], axis=1),
        jnp.concatenate([t[1:2] for t in taken], axis=1),
    )
    edge_k, edge_v = halves(edge[:, :128])
    edge_q, edge_g = halves(edge[SLAB:, 128:])
    for n in range(SLABS // 2):
        rows = slice(2 * n * SLAB, 2 * (n + 1) * SLAB)
        dq = query_side(every, rows, edge_q, edge_g, strip_lse, strip_stat)
        query = every[rows, 128:]
        both = [stat_rows(stats[2 * n + k]) for k in range(2)]
        lse = jnp.concatenate([pair[0] for pair in both], axis=1)
        stat = jnp.concatenate([pair[1] for pair in both], axis=1)
        probs = jnp.exp(dot(edge_k, query, 1, 1) - lse)
        slopes = (probs * (dot(edge_v, query, 1, 1) - stat)).astype(BF16)
        dk = dot(slopes, query, 1, 0)
        dv = dot(probs.astype(BF16), query, 1, 0)
        if n == 0:
            dq_ref[...] = dq
            dk_ref[...] = dk
            dv_ref[...] = dv
        else:
            dq_ref[...] += dq
            dk_ref[...] += dk
            dv_ref[...] += dv
    lanes = lax.broadcasted_iota(jnp.int32, (EDGE, 128), 1)
    keyval = jnp.where(lanes < HEAD, dk_ref[...] * (HEAD**-0.5), dv_ref[...]).astype(BF16)
    query = jnp.concatenate(
        [dq_own[...], (dq_ref[...] * (HEAD**-0.5)).astype(BF16)], axis=0
    )
    copies[0].wait()
    out[...] = dot(tiles[...], jnp.concatenate([keyval, query], axis=1), 1, 0).astype(BF16)
    for copy in copies[1:]:
        copy.wait()


def run_coarse_backward(place, every, stats, strips, edge, dq_own, *later):
    tiles = jnp.asarray(tile_pick(), BF16)
    return pl.pallas_call(
        coarse_backward,
        out_shape=[pltpu.HBM((H1 * EXT, 256), BF16)]
        + [pltpu.VMEM(array.shape, array.dtype) for array in later],
        in_specs=[pl.BlockSpec(memory_space=pltpu.SMEM)] + [whole()] * 5 + [far()] * 3,
        out_specs=[whole()] * 3,
        scratch_shapes=[
            pltpu.VMEM((2 * STRIP, 128), F32),
            pltpu.VMEM((EDGE, 128), F32),
            pltpu.VMEM((EDGE, 128), F32),
            pltpu.VMEM(tiles.shape, BF16),
            pltpu.SemaphoreType.DMA((3,)),
        ],
        compiler_params=vmem_params(24),
        cost_estimate=pl.CostEstimate(flops=3 * 10**9, bytes_accessed=2 * 10**6, transcendentals=4 * 10**6),
        name="coarse_backward",
    )(
        place,
        every,
        stats,
        strips,
        in_hbm(edge),
        in_hbm(dq_own),
        *[in_hbm(array) for array in (tiles,) + later],
    )


def block_pick():
    c, b = np.meshgrid(np.arange(H1), np.arange(64), indexing="ij")
    source = np.where(b < 48, 48 * c + b, 3 * D0 + 16 * c + b - 48).reshape(-1)
    pick = np.zeros((4 * D0, 4 * D0), np.float32)
    pick[source, np.arange(4 * D0)] = 1
    return pick


def merged_order(back):
    rows = lax.broadcasted_iota(jnp.int32, (BLOCK, BLOCK), 0)
    cols = lax.broadcasted_iota(jnp.int32, (BLOCK, BLOCK), 1)
    merged, grid = (cols, rows) if back else (rows, cols)
    a = merged // C4
    c = merged // 8 % MERGE
    j = merged % 8
    return (grid == a * C4 + j * MERGE + c).astype(F32).astype(BF16)


def backward_kernel(
    place,
    terms_coarse,
    own_fine,
    own_coarse,
    above,
    below,
    grads_left,
    grads_right,
    coarse,
    lse,
    gain_coarse,
    gain,
    w_qkv,
    w_out,
    w_coarse,
    stash,
    pick_far,
    w_merge_far,
    grad_tokens,
    terms,
    grad_fine,
    sp32,
    gh_ref,
    ga_ref,
    dq_ref,
    dk_ref,
    dv_ref,
    gt_ref,
    pick_block,
    w_merge,
    stack_ref,
    probs_ref,
    merge_sems,
    pick_sem,
):
    merge_copies = fetch(w_merge_far, w_merge, merge_sems, 4)
    pick_copy = pltpu.make_async_copy(pick_far, pick_block, pick_sem)
    for copy in merge_copies + [pick_copy]:
        copy.start()
    queries = stash.at[pl.ds(AT_Q, N4)]
    attended = stash.at[pl.ds(AT_ATT, N4)]
    keys_w = stash.at[pl.ds(AT_K, WROWS * C4)]
    values_w = stash.at[pl.ds(AT_V, WROWS * C4)]
    tokens_own = stash.at[pl.ds(AT_X, OWN)]
    row0 = place[0]
    col0 = place[1]
    wide = CCOLS + 2
    fine_rows, coarse_rows = grads_of(own_fine, own_coarse, above, below)
    side = [part[...].astype(F32) for part in (grads_left, grads_right)]
    for i, row in enumerate(fine_rows):
        outer = [part[4 * i : 4 * (i + 1)] for part in side]
        grad_fine[C4 * i : C4 * (i + 1)] = jnp.concatenate([outer[0], row, outer[1]], axis=0)
    grad_coarse = []
    for i, row in enumerate(coarse_rows):
        parts = []
        for g, piece in enumerate(row):
            at = 4 * R4 + 4 * i + g
            outer = [part[at : at + 1] for part in side]
            parts.append(jnp.concatenate([outer[0], piece, outer[1]], axis=0))
        grad_coarse.append(jnp.concatenate(parts, axis=1))
    grad_coarse = jnp.concatenate(grad_coarse, axis=0)
    parts = []
    for h in range(H1):
        block = terms_coarse[h].astype(F32)
        parts += [block[:, 128:192], block[:, :128]]
    heads = jnp.concatenate(parts, axis=1).astype(BF16)
    upstream = dot(heads, w_coarse[...], 1, 1) * gain_coarse[...]
    normed, inverse = norm_forward(coarse[...].astype(F32))
    back = norm_backward(upstream, normed, inverse)
    change = (grad_coarse + back).astype(BF16)
    for a, copy in enumerate(merge_copies):
        copy.wait()
        sp32[a] = dot(change, w_merge[D1 * a : D1 * (a + 1)], 1, 1)
    window = window_bias(C4, -3)
    for b in range(BLOCKS):
        stacked = stack_heads(queries[BLOCK * b : BLOCK * (b + 1)].astype(F32)).astype(BF16)
        stack_ref[b] = stacked
        bias = all_heads(window + key_bias(C4, row0 - 7 + 4 * b, col0 - 4))
        scores = dot(keys_w[BLOCK * b : BLOCK * b + 10 * C4], stacked, 1, 1) + bias
        probs_ref[b] = jnp.exp(scores - lse[b : b + 1])
    to_merged = merged_order(False)
    to_grid = merged_order(True)
    for i in range(CROWS + 2):
        block = slice(BLOCK * i, BLOCK * (i + 1))
        rows = slice(wide * i, wide * (i + 1))
        spread = [
            sp32[a, rows, D0 * c : D0 * (c + 1)] for a in range(MERGE) for c in range(MERGE)
        ]
        total = dot(to_merged, grad_fine[block].astype(BF16), 1, 0) + jnp.concatenate(spread, axis=0)
        gh_ref[block] = dot(to_grid, total.astype(BF16), 1, 0).astype(BF16)
    ga_ref[...] = dot(gh_ref[...], w_out[...], 1, 1).astype(BF16)
    dk_ref[...] = jnp.zeros_like(dk_ref)
    dv_ref[...] = jnp.zeros_like(dv_ref)
    pick = (
        lax.broadcasted_iota(jnp.int32, (8, D0), 1) // HEAD
        == lax.broadcasted_iota(jnp.int32, (8, D0), 0)
    ).astype(F32).astype(BF16)
    for b in range(BLOCKS):
        at = slice(BLOCK * b, BLOCK * (b + 1))
        keep = slice(BLOCK * b, BLOCK * b + 10 * C4)
        grad = ga_ref[at].astype(F32)
        product = grad * attended[at].astype(F32)
        upper = product.astype(BF16)
        lower = (product - upper.astype(F32)).astype(BF16)
        sums = dot(pick, upper, 1, 1) + dot(pick, lower, 1, 1)
        stat = jnp.concatenate([sums[h : h + 1] for h in range(H0)], axis=1)
        stack_q = stack_ref[b]
        stack_g = stack_heads(grad).astype(BF16)
        key_block = keys_w[keep]
        probs = probs_ref[b]
        slopes = (probs * (dot(values_w[keep], stack_g, 1, 1) - stat)).astype(BF16)
        dk_ref[keep] += dot(slopes, stack_q, 1, 0)
        dv_ref[keep] += dot(probs.astype(BF16), stack_g, 1, 0)
        if 1 <= b <= 4:
            dq = unstack_heads(dot(slopes, key_block, 0, 0)) * (HEAD**-0.5)
            dq_ref[BLOCK * (b - 1) : BLOCK * b] = dq.astype(BF16)
    own = slice(7 * C4, 7 * C4 + OWN)
    grads = jnp.concatenate(
        [dq_ref[...], dk_ref[own].astype(BF16), dv_ref[own].astype(BF16)], axis=1
    )
    column = lax.broadcasted_iota(jnp.int32, (ROWS, C4, D0), 1).reshape(OWN, D0)
    in_tile = (column >= 4) & (column < 4 + COLS)
    normed, inverse = norm_forward(tokens_own[...].astype(F32))
    rounded = jnp.where(in_tile, normed * gain[...], 0.0).astype(BF16)
    term_qkv = dot(rounded, grads, 0, 0).astype(BF16)
    inner = slice(BLOCK, BLOCK + OWN)
    att = jnp.where(in_tile, attended[inner].astype(F32), 0.0).astype(BF16)
    term_out = dot(att, gh_ref[inner], 0, 0).astype(BF16)
    pick_copy.wait()
    both = dot(jnp.concatenate([term_qkv, term_out], axis=1), pick_block[...], 1, 0)
    low = lax.broadcasted_iota(jnp.int32, (16, 128), 1) < 64
    for r in range(8):
        for m in range(8):
            first = both[32 * r : 32 * r + 16, 128 * m : 128 * (m + 1)]
            last = both[32 * r + 16 : 32 * (r + 1), 128 * m : 128 * (m + 1)]
            terms[16 * r + 2 * m] = jnp.where(low, first, pltpu.roll(last, 64, 1)).astype(BF16)
            terms[16 * r + 2 * m + 1] = jnp.where(low, pltpu.roll(first, 64, 1), last).astype(BF16)
    upstream = dot(grads, w_qkv[...], 1, 1) * gain[...]
    gt_ref[...] = gh_ref[inner].astype(F32) + norm_backward(upstream, normed, inverse)
    for pair in range(ROWS // 2):
        parts = [gt_ref[pl.ds(i * C4 + 4, COLS), :] for i in (2 * pair, 2 * pair + 1)]
        grad_tokens[2 * COLS * pair : 2 * COLS * (pair + 1)] = jnp.concatenate(
            parts, axis=0
        ).astype(BF16)


def run_backward(place, *operands):
    shapes = [((ROWS * COLS, D0), BF16), ((128, 16, 128), BF16)]
    return pl.pallas_call(
        backward_kernel,
        out_shape=[jax.ShapeDtypeStruct(s, d) for s, d in shapes],
        in_specs=[pl.BlockSpec(memory_space=pltpu.SMEM)] + [whole()] * 15 + [far()] * 2,
        out_specs=[whole()] * 2,
        scratch_shapes=[
            pltpu.VMEM((N4, D0), F32),
            pltpu.VMEM((MERGE, EXT, D1), F32),
            pltpu.VMEM((N4, D0), BF16),
            pltpu.VMEM((N4, D0), BF16),
            pltpu.VMEM((OWN, D0), BF16),
            pltpu.VMEM((WROWS * C4, D0), F32),
            pltpu.VMEM((WROWS * C4, D0), F32),
            pltpu.VMEM((OWN, D0), F32),
            pltpu.VMEM((4 * D0, 4 * D0), BF16),
            pltpu.VMEM((MERGE * MERGE * D0, D1), BF16),
            pltpu.VMEM((BLOCKS, H0 * BLOCK, D0), BF16),
            pltpu.VMEM((BLOCKS, 10 * C4, H0 * BLOCK), F32),
            pltpu.SemaphoreType.DMA((4,)),
            pltpu.SemaphoreType.DMA(()),
        ],
        compiler_params=vmem_params(40),
        cost_estimate=pl.CostEstimate(flops=5 * 10**9, bytes_accessed=2 * 10**7, transcendentals=10**6),
        name="backward_kernel",
    )(place, *operands[:-2], *[in_hbm(operand) for operand in operands[-2:]])


def sum_terms(terms, out_qkv, out_out):
    total = jnp.sum(terms[...].astype(F32), axis=0)
    total = jnp.concatenate([total[:, :64], total[:, 64:]], axis=0)
    out_qkv[...] = total[:, :48]
    out_out[...] = total[:, 48:].T


def run_sum_terms(terms):
    return pl.pallas_call(
        sum_terms,
        out_shape=[jax.ShapeDtypeStruct((32, 48), F32), jax.ShapeDtypeStruct((16, 32), F32)],
        in_specs=[whole()],
        out_specs=[whole()] * 2,
        compiler_params=vmem_params(8),
        name="sum_terms",
    )(terms)


def ring(axis, step):
    devices = lax.axis_size(axis)
    return [(i, (i + step) % devices) for i in range(devices)]


def swap_edges(first, last, axis):
    before = lax.ppermute(last, axis, ring(axis, 1))
    after = lax.ppermute(first, axis, ring(axis, -1))
    return before, after


HALO = 8
TOKEN_ROWS = HALO * COLS
FINE_ROWS = 4 * COLS
STRIP_ROWS = TOKEN_ROWS + FINE_ROWS + 4 * CCOLS


def row_strips(tokens, grad_fine, grad_coarse, first, last, flat, held, sems):
    fine_at = pl.ds(TOKEN_ROWS, FINE_ROWS)
    own = ROWS * COLS
    copies = [
        pltpu.make_async_copy(grad_coarse, held, sems.at[0]),
        pltpu.make_async_copy(
            tokens.at[pl.ds(0, TOKEN_ROWS)], first.at[pl.ds(0, TOKEN_ROWS)], sems.at[1]
        ),
        pltpu.make_async_copy(
            tokens.at[pl.ds(own - TOKEN_ROWS, TOKEN_ROWS)],
            last.at[pl.ds(0, TOKEN_ROWS)],
            sems.at[2],
        ),
        pltpu.make_async_copy(grad_fine.at[pl.ds(0, FINE_ROWS)], first.at[fine_at], sems.at[3]),
        pltpu.make_async_copy(
            grad_fine.at[pl.ds(own - FINE_ROWS, FINE_ROWS)], last.at[fine_at], sems.at[4]
        ),
    ]
    for copy in copies:
        copy.start()
    copies[0].wait()
    wide = held[...].astype(F32)
    rows = [wide[:, i, :] for i in range(CROWS)]
    flat[...] = jnp.concatenate(rows, axis=0).astype(BF16)
    for out, coarse in ((first, rows[0]), (last, rows[-1])):
        pieces = [coarse[:, D0 * g : D0 * (g + 1)] for g in range(4)]
        out[TOKEN_ROWS + FINE_ROWS :] = jnp.concatenate(pieces, axis=0).astype(BF16)
    for copy in copies[1:]:
        copy.wait()


def run_row_strips(tokens, grad_fine, grad_coarse):
    shapes = [(STRIP_ROWS, D0), (STRIP_ROWS, D0), (CROWS * CCOLS, D1)]
    operands = (tokens.reshape(-1, D0), grad_fine.reshape(-1, D0), grad_coarse.transpose(1, 0, 2))
    return pl.pallas_call(
        row_strips,
        out_shape=[jax.ShapeDtypeStruct(shape, BF16) for shape in shapes],
        in_specs=[far()] * 3,
        out_specs=[whole()] * 3,
        scratch_shapes=[
            pltpu.VMEM((CCOLS, CROWS, D1), BF16),
            pltpu.SemaphoreType.DMA((5,)),
        ],
        compiler_params=vmem_params(8),
        name="row_strips",
    )(*[in_hbm(operand) for operand in operands])


def column_strips(tokens, above, below, first, last):
    parts = [part[:TOKEN_ROWS].astype(F32) for part in (above, below)]
    parts.insert(1, tokens[...].astype(F32))
    left = []
    right = []
    for part in parts:
        for i in range(part.shape[0] // COLS):
            left.append(part[COLS * i : COLS * i + HALO])
            right.append(part[COLS * (i + 1) - HALO : COLS * (i + 1)])
    first[...] = jnp.concatenate(left, axis=0).astype(BF16)
    last[...] = jnp.concatenate(right, axis=0).astype(BF16)


def run_column_strips(tokens, above, below):
    return pl.pallas_call(
        column_strips,
        out_shape=[jax.ShapeDtypeStruct((R8 * HALO, D0), BF16)] * 2,
        in_specs=[whole()] * 3,
        out_specs=[whole()] * 2,
        compiler_params=vmem_params(8),
        name="column_strips",
    )(in_hbm(tokens.reshape(-1, D0)), above, below)


def grads_of(own_fine, own_coarse, above, below):
    at = TOKEN_ROWS + FINE_ROWS
    fine = []
    coarse = []
    for outer in (above, below):
        outer_fine = outer[TOKEN_ROWS:at].astype(F32)
        outer_coarse = outer[at:].astype(F32)
        fine.append([outer_fine[COLS * i : COLS * (i + 1)] for i in range(4)])
        coarse.append([outer_coarse[CCOLS * g : CCOLS * (g + 1)] for g in range(4)])
    wide = own_fine[...].astype(F32)
    flat = own_coarse[...].astype(F32)
    fine_rows = fine[0] + [wide[COLS * i : COLS * (i + 1)] for i in range(ROWS)] + fine[1]
    own = [
        [flat[CCOLS * i : CCOLS * (i + 1), D0 * g : D0 * (g + 1)] for g in range(4)]
        for i in range(CROWS)
    ]
    return fine_rows, [coarse[0]] + own + [coarse[1]]


def grad_strips(own_fine, own_coarse, above, below, first, last):
    fine, coarse = grads_of(own_fine, own_coarse, above, below)
    left = [row[:4] for row in fine] + [piece[:1] for row in coarse for piece in row]
    right = [row[-4:] for row in fine] + [piece[-1:] for row in coarse for piece in row]
    first[...] = jnp.concatenate(left, axis=0).astype(BF16)
    last[...] = jnp.concatenate(right, axis=0).astype(BF16)


def run_grad_strips(own_fine, own_coarse, above, below):
    return pl.pallas_call(
        grad_strips,
        out_shape=[jax.ShapeDtypeStruct((R4 * 4 + EXT // 2, D0), BF16)] * 2,
        in_specs=[whole()] * 4,
        out_specs=[whole()] * 2,
        compiler_params=vmem_params(8),
        name="grad_strips",
    )(own_fine, own_coarse, above, below)


def on_device(
    tokens,
    grad_fine,
    grad_coarse,
    fine_gain,
    fine_qkv,
    fine_out,
    merge_weight,
    coarse_gain,
    coarse_qkv,
    coarse_out,
):
    row = lax.axis_index("row")
    col = lax.axis_index("col")
    place = jnp.stack([row * ROWS, col * COLS, row]).astype(jnp.int32)
    first, last, grad_coarse = run_row_strips(tokens, grad_fine, grad_coarse)
    above, below = swap_edges(first, last, "row")
    left, right = swap_edges(*run_column_strips(tokens, above, below), "col")
    pieces = (tokens, above, below, left, right)
    grad_heads = jnp.dot(grad_coarse, coarse_out.T, preferred_element_type=F32).astype(BF16)
    packed = run_near(
        place,
        pieces,
        fine_gain,
        fine_qkv,
        fine_out,
        merge_weight,
        coarse_gain,
        coarse_qkv,
        grad_heads,
    )
    packed, grad_fine, grad_coarse, *pieces = lax.optimization_barrier(
        (packed, grad_fine, grad_coarse, *pieces)
    )
    every = lax.all_to_all(
        packed.reshape(8 * H1, CROWS * CCOLS, 256),
        ("row", "col"),
        split_axis=0,
        concat_axis=0,
        tiled=True,
    )
    grads = (grad_fine.reshape(-1, D0), grad_coarse, pieces[1], pieces[2])
    left, right = swap_edges(*run_grad_strips(*grads), "col")
    stash, lse, coarse = run_wide(place, pieces, fine_gain, fine_qkv, fine_out, merge_weight)
    every, left, right, stash, lse, coarse = lax.optimization_barrier(
        (every, left, right, stash, lse, coarse)
    )
    every = every.reshape(SLAB * SLABS, 256)
    strips = jnp.asarray(strip_pick(), BF16)
    own_stats = run_coarse_forward(place, every)
    stats = lax.all_to_all(own_stats, "row", split_axis=0, concat_axis=0, tiled=True)
    edge, dq_own = run_coarse_own(place, every, own_stats, strips)
    tiles, near_coarse, stash = run_coarse_backward(
        place, every, stats, strips, edge, dq_own, coarse_qkv, stash
    )
    tiles = tiles.reshape(H1, EXT, 256)
    terms = lax.all_to_all(tiles, "col", split_axis=0, concat_axis=0, tiled=True)
    grad_tokens, blocks = run_backward(
        place,
        terms,
        *grads,
        left,
        right,
        coarse,
        lse,
        coarse_gain.reshape(1, D1),
        fine_gain.reshape(1, D0),
        fine_qkv,
        fine_out,
        near_coarse,
        stash,
        jnp.asarray(block_pick(), BF16),
        merge_weight,
    )
    blocks = lax.all_to_all(blocks, ("row", "col"), split_axis=0, concat_axis=0, tiled=True)
    grad_qkv, grad_out = run_sum_terms(blocks)
    return grad_tokens.reshape(ROWS, COLS, D0), grad_qkv, grad_out.T


def solution(mesh):
    return jax.shard_map(
        on_device,
        mesh=mesh,
        in_specs=(P("row", "col", None),) * 3 + (P(),) * 7,
        out_specs=(P("row", "col", None), P("row", "col"), P("row", "col")),
        check_vma=False,
    )
```

```python
import jax
import jax.numpy as jnp
import numpy as np
from jax import lax
from jax.experimental import pallas as pl
from jax.experimental.pallas import tpu as pltpu
from jax.sharding import PartitionSpec as P

H0 = 4
H1 = 16
HEAD = 64
MERGE = 4
EPSILON = 1e-05
FAR = 1e30
D0 = 256
D1 = 1024

ROWS, COLS = 16, 24
CROWS, CCOLS = 4, 6
R8, C8 = ROWS + 16, COLS + 16
R4, C4 = ROWS + 8, COLS + 8
N4 = R4 * C4
BLOCK = 4 * C4
BLOCKS = R4 // 4
WROWS = R4 + 6
OWN = ROWS * C4
EXT = (CROWS + 2) * (CCOLS + 2)

F32 = jnp.float32
BF16 = jnp.bfloat16


def vmem_params(mib):
    return pltpu.CompilerParams(vmem_limit_bytes=mib * 1024 * 1024)


def whole():
    return pl.BlockSpec(memory_space=pltpu.VMEM)


def far():
    return pl.BlockSpec(memory_space=pltpu.HBM)


def fetch(source, target, sems, pieces):
    rows = source.shape[0] // pieces
    return [
        pltpu.make_async_copy(
            source.at[pl.ds(n * rows, rows)], target.at[pl.ds(n * rows, rows)], sems.at[n]
        )
        for n in range(pieces)
    ]


def dot(a, b, ca, cb):
    return lax.dot_general(a, b, (((ca,), (cb,)), ((), ())), preferred_element_type=F32)


def norm_forward(values):
    center = values - jnp.mean(values, axis=-1, keepdims=True)
    inverse = lax.rsqrt(jnp.mean(center * center, axis=-1, keepdims=True) + EPSILON)
    return center * inverse, inverse


def norm_backward(scaled, normed, inverse):
    return inverse * (
        scaled
        - jnp.mean(scaled, axis=-1, keepdims=True)
        - normed * jnp.mean(scaled * normed, axis=-1, keepdims=True)
    )


def head_lanes(rows):
    return lax.broadcasted_iota(jnp.int32, (rows, D0), 1) // HEAD


def stack_heads(values):
    lanes = head_lanes(values.shape[0])
    zero = jnp.zeros_like(values)
    return jnp.concatenate([jnp.where(lanes == h, values, zero) for h in range(H0)], axis=0)


def unstack_heads(stacked):
    rows = stacked.shape[0] // H0
    lanes = head_lanes(rows)
    result = stacked[:rows]
    for h in range(1, H0):
        result = jnp.where(lanes == h, stacked[h * rows : (h + 1) * rows], result)
    return result


AT_Q = 0
AT_ATT = N4
AT_K = 2 * N4
AT_V = AT_K + WROWS * C4
AT_X = AT_V + WROWS * C4
STASH = AT_X + OWN


def window_bias(key_cols, col_shift):
    shape = (10, key_cols, BLOCK)
    kr = lax.broadcasted_iota(jnp.int32, shape, 0)
    kc = lax.broadcasted_iota(jnp.int32, shape, 1)
    lane = lax.broadcasted_iota(jnp.int32, shape, 2)
    row_gap = kr - lane // C4
    col_gap = kc - lane % C4 - col_shift
    near = (row_gap >= 0) & (row_gap <= 6) & (col_gap >= 0) & (col_gap <= 6)
    return jnp.where(near, 0.0, -FAR).reshape(10 * key_cols, BLOCK)


def key_bias(key_cols, key_row, key_col):
    shape = (10, key_cols, 1)
    grid_row = key_row + lax.broadcasted_iota(jnp.int32, shape, 0)
    grid_col = key_col + lax.broadcasted_iota(jnp.int32, shape, 1)
    inside = (grid_row >= 0) & (grid_row < 128) & (grid_col >= 0) & (grid_col < 384)
    return jnp.where(inside, 0.0, -FAR).reshape(10 * key_cols, 1)


def all_heads(bias):
    return jnp.concatenate([bias] * H0, axis=1)


def near_kernel(
    place,
    tokens,
    above,
    below,
    left,
    right,
    gain,
    w_qkv,
    w_out,
    w_merge_far,
    gain_coarse,
    w_coarse_far,
    grads,
    packed_far,
    x32,
    keys,
    values,
    hid32,
    merged,
    w_merge,
    w_coarse,
    packed,
    merge_sems,
    coarse_sems,
    packed_sems,
):
    merge_copies = fetch(w_merge_far, w_merge, merge_sems, 2)
    coarse_copies = fetch(w_coarse_far, w_coarse, coarse_sems, 4)
    for copy in merge_copies + coarse_copies:
        copy.start()
    row0 = place[0]
    col0 = place[1]
    middle = [part[: 8 * COLS].astype(F32) for part in (above, below)]
    middle.insert(1, tokens[...].astype(F32))
    sides = [left[...].astype(F32), right[...].astype(F32)]
    for t in range(ROWS + 6):
        e = t + 5
        part, at = (0, e) if e < 8 else (1, e - 8) if e < 8 + ROWS else (2, e - 8 - ROWS)
        x32[C4 * t : C4 * (t + 1)] = jnp.concatenate(
            [
                sides[0][8 * e + 4 : 8 * e + 8],
                middle[part][COLS * at : COLS * (at + 1)],
                sides[1][8 * e : 8 * e + 4],
            ],
            axis=0,
        )
    normed, _ = norm_forward(x32[...])
    normed = (normed * gain[...]).astype(BF16)
    inner = slice(3 * C4, 3 * C4 + OWN)
    queries = dot(normed[inner], w_qkv[:, :D0], 1, 0).astype(BF16).astype(F32) * (HEAD**-0.5)
    keys[...] = dot(normed, w_qkv[:, D0 : 2 * D0], 1, 0).astype(BF16)
    values[...] = dot(normed, w_qkv[:, 2 * D0 :], 1, 0).astype(BF16)
    window = window_bias(C4, -3)
    for b in range(ROWS // 4):
        block = slice(BLOCK * b, BLOCK * b + 10 * C4)
        stacked = stack_heads(queries[BLOCK * b : BLOCK * (b + 1)]).astype(BF16)
        bias = all_heads(window + key_bias(C4, row0 - 3 + 4 * b, col0 - 4))
        scores = dot(keys[block], stacked, 1, 1) + bias
        maxima = jnp.max(scores, axis=0, keepdims=True)
        exponent = jnp.exp(scores - maxima)
        totals = jnp.sum(exponent, axis=0, keepdims=True)
        weights = (exponent * (1.0 / totals)).astype(BF16)
        attended = unstack_heads(dot(weights, values[block], 0, 0)).astype(BF16)
        at = BLOCK * b
        own = x32[3 * C4 + at : 3 * C4 + at + BLOCK]
        total = (own + dot(attended, w_out[...], 1, 0)).astype(BF16).astype(F32)
        hid32[0, at : at + BLOCK] = total[:, :128]
        hid32[1, at : at + BLOCK] = total[:, 128:]
    wide = CCOLS + 2
    merge_rows(hid32, merged, CROWS)
    total = None
    for n in range(4):
        if n % 2 == 0:
            merge_copies[n // 2].wait()
        part = dot(merged[:, D1 * n : D1 * (n + 1)], w_merge[D1 * n : D1 * (n + 1)], 1, 0)
        total = part if total is None else total + part
    normed, _ = norm_forward(total.astype(BF16).astype(F32))
    normed = normed * gain_coarse[...]
    parts = [normed[wide * i + 1 : wide * i + 1 + CCOLS] for i in range(CROWS)]
    normed = jnp.concatenate(parts, axis=0).astype(BF16)
    for copy in coarse_copies:
        copy.wait()
    packed_copies = []
    for n in range(4):
        result = dot(normed, w_coarse[:, 768 * n : 768 * (n + 1)], 1, 0)
        grad = grads[:, 256 * n : 256 * (n + 1)].astype(F32)
        parts = []
        for h in range(4):
            q = result[:, 192 * h : 192 * h + 64]
            k = result[:, 192 * h + 64 : 192 * h + 128]
            v = result[:, 192 * h + 128 : 192 * h + 192]
            g = grad[:, 64 * h : 64 * h + 64]
            parts.append(jnp.concatenate([k, v, q, g], axis=1))
        packed[2 * n] = jnp.concatenate(parts[:2], axis=0).astype(BF16)
        packed[2 * n + 1] = jnp.concatenate(parts[2:], axis=0).astype(BF16)
        at = pl.ds(2 * n, 2)
        for r in range(8):
            packed_copies.append(
                pltpu.make_async_copy(packed.at[at], packed_far.at[r, at], packed_sems.at[n, r])
            )
            packed_copies[-1].start()
    for copy in packed_copies:
        copy.wait()


def merge_rows(hid32, merged, count):
    for pair in range(count // 2):
        for a in range(MERGE):
            for c in range(MERGE):
                for half in range(2):
                    parts = [
                        hid32[half, pl.ds((4 * i + a) * C4 + c, CCOLS + 2, stride=MERGE), :]
                        for i in (2 * pair, 2 * pair + 1)
                    ]
                    at = (a * MERGE + c) * D0 + half * 128
                    merged[16 * pair : 16 * (pair + 1), at : at + 128] = jnp.concatenate(
                        parts, axis=0
                    ).astype(BF16)


def run_near(place, pieces, gain, w_qkv, w_out, w_merge, gain_coarse, w_coarse, grads):
    own = CROWS * CCOLS
    return pl.pallas_call(
        near_kernel,
        out_shape=pltpu.HBM((8, 8, 2 * own, 256), BF16),
        in_specs=[pl.BlockSpec(memory_space=pltpu.SMEM)]
        + [whole()] * 8
        + [far(), whole(), far(), whole()],
        out_specs=far(),
        scratch_shapes=[
            pltpu.VMEM(((ROWS + 6) * C4, D0), F32),
            pltpu.VMEM(((ROWS + 6) * C4, D0), BF16),
            pltpu.VMEM(((ROWS + 6) * C4, D0), BF16),
            pltpu.VMEM((2, OWN, 128), F32),
            pltpu.VMEM((CROWS * (CCOLS + 2), MERGE * MERGE * D0), BF16),
            pltpu.VMEM(w_merge.shape, BF16),
            pltpu.VMEM(w_coarse.shape, BF16),
            pltpu.VMEM((8, 2 * own, 256), BF16),
            pltpu.SemaphoreType.DMA((2,)),
            pltpu.SemaphoreType.DMA((4,)),
            pltpu.SemaphoreType.DMA((4, 8)),
        ],
        compiler_params=vmem_params(48),
        cost_estimate=pl.CostEstimate(flops=3 * 10**9, bytes_accessed=2 * 10**7, transcendentals=10**6),
        name="near_kernel",
    )(
        place,
        *[piece.reshape(-1, D0) for piece in pieces],
        gain.reshape(1, D0),
        w_qkv,
        w_out,
        in_hbm(w_merge),
        gain_coarse.reshape(1, D1),
        in_hbm(w_coarse),
        grads,
    )


def in_hbm(array):
    return pltpu.with_memory_space_constraint(array, pltpu.HBM)


def wide_kernel(
    place,
    tokens,
    above,
    below,
    left,
    right,
    gain,
    w_qkv,
    w_out,
    w_merge_far,
    stash_far,
    lse,
    coarse_out,
    x32,
    q32,
    k32,
    v32,
    hid32,
    stash,
    merged,
    w_merge,
    merge_sems,
    stash_sem,
):
    merge_copies = fetch(w_merge_far, w_merge, merge_sems, 4)
    for copy in merge_copies:
        copy.start()
    queries = stash.at[pl.ds(AT_Q, N4)]
    attended = stash.at[pl.ds(AT_ATT, N4)]
    keys_w = stash.at[pl.ds(AT_K, WROWS * C4)]
    values_w = stash.at[pl.ds(AT_V, WROWS * C4)]
    tokens_own = stash.at[pl.ds(AT_X, OWN)]
    row0 = place[0]
    col0 = place[1]
    middle = [part[: 8 * COLS].astype(F32) for part in (above, below)]
    middle.insert(1, tokens[...].astype(F32))
    sides = [left[...].astype(F32), right[...].astype(F32)]
    for i in range(R8):
        part, at = (0, i) if i < 8 else (1, i - 8) if i < 8 + ROWS else (2, i - 8 - ROWS)
        x32[C8 * i : C8 * i + 8] = sides[0][8 * i : 8 * i + 8]
        x32[C8 * i + 8 : C8 * i + 8 + COLS] = middle[part][COLS * at : COLS * (at + 1)]
        x32[C8 * i + 8 + COLS : C8 * (i + 1)] = sides[1][8 * i : 8 * i + 8]
    normed, _ = norm_forward(x32[...])
    normed = (normed * gain[...]).astype(BF16)
    q32[...] = dot(normed, w_qkv[:, :D0], 1, 0).astype(BF16).astype(F32) * (HEAD**-0.5)
    k32[...] = dot(normed, w_qkv[:, D0 : 2 * D0], 1, 0).astype(BF16).astype(F32)
    v32[...] = dot(normed, w_qkv[:, 2 * D0 :], 1, 0).astype(BF16).astype(F32)
    for i in range(R4):
        queries[C4 * i : C4 * (i + 1)] = q32[pl.ds((i + 4) * C8 + 4, C4), :].astype(BF16)
    for i in range(WROWS):
        keys_w[C4 * i : C4 * (i + 1)] = k32[pl.ds((i + 1) * C8 + 4, C4), :].astype(BF16)
        values_w[C4 * i : C4 * (i + 1)] = v32[pl.ds((i + 1) * C8 + 4, C4), :].astype(BF16)
    for i in range(ROWS):
        tokens_own[C4 * i : C4 * (i + 1)] = x32[pl.ds((i + 8) * C8 + 4, C4), :].astype(BF16)
    lse[...] = jnp.full(lse.shape, FAR, F32)
    window = window_bias(C8, 1)
    for b in range(BLOCKS):
        start = (4 * b + 1) * C8
        key_block = k32[start : start + 10 * C8].astype(BF16)
        value_block = v32[start : start + 10 * C8].astype(BF16)
        stacked = stack_heads(queries[BLOCK * b : BLOCK * (b + 1)].astype(F32)).astype(BF16)
        bias = all_heads(window + key_bias(C8, row0 - 7 + 4 * b, col0 - 8))
        scores = dot(key_block, stacked, 1, 1) + bias
        maxima = jnp.max(scores, axis=0, keepdims=True)
        exponent = jnp.exp(scores - maxima)
        totals = jnp.sum(exponent, axis=0, keepdims=True)
        weights = (exponent * (1.0 / totals)).astype(BF16)
        result = unstack_heads(dot(weights, value_block, 0, 0)).astype(BF16)
        attended[BLOCK * b : BLOCK * (b + 1)] = result
        lane = lax.broadcasted_iota(jnp.int32, (1, H0 * BLOCK), 1) % BLOCK
        q_row = row0 - 4 + 4 * b + lane // C4
        q_col = col0 - 4 + lane % C4
        q_in = (q_row >= 0) & (q_row < 128) & (q_col >= 0) & (q_col < 384)
        lse[b : b + 1] = jnp.where(q_in, maxima + jnp.log(totals), FAR)
        projected = dot(result, w_out[...], 1, 0)
        for a in range(4):
            own = x32[pl.ds((4 * b + a + 4) * C8 + 4, C4), :]
            total = own + projected[C4 * a : C4 * (a + 1)]
            at = BLOCK * b + C4 * a
            total = total.astype(BF16).astype(F32)
            hid32[0, at : at + C4] = total[:, :128]
            hid32[1, at : at + C4] = total[:, 128:]
    merge_rows(hid32, merged, CROWS + 2)
    stash_copy = pltpu.make_async_copy(stash, stash_far, stash_sem)
    stash_copy.start()
    total = None
    for n, copy in enumerate(merge_copies):
        copy.wait()
        part = dot(merged[:, D1 * n : D1 * (n + 1)], w_merge[D1 * n : D1 * (n + 1)], 1, 0)
        total = part if total is None else total + part
    coarse_out[...] = total.astype(BF16)
    stash_copy.wait()


def run_wide(place, pieces, gain, w_qkv, w_out, w_merge):
    flat = R8 * C8
    return pl.pallas_call(
        wide_kernel,
        out_shape=[
            pltpu.HBM((STASH, D0), BF16),
            pltpu.HBM((8, H0 * BLOCK), F32),
            pltpu.HBM((EXT, D1), BF16),
        ],
        in_specs=[pl.BlockSpec(memory_space=pltpu.SMEM)] + [whole()] * 8 + [far()],
        out_specs=[far(), whole(), whole()],
        scratch_shapes=[pltpu.VMEM((flat, D0), F32)] * 4
        + [
            pltpu.VMEM((2, N4, 128), F32),
            pltpu.VMEM((STASH, D0), BF16),
            pltpu.VMEM((EXT, MERGE * MERGE * D0), BF16),
            pltpu.VMEM(w_merge.shape, BF16),
            pltpu.SemaphoreType.DMA((4,)),
            pltpu.SemaphoreType.DMA(()),
        ],
        compiler_params=vmem_params(40),
        cost_estimate=pl.CostEstimate(flops=3 * 10**9, bytes_accessed=10**7, transcendentals=10**6),
        name="wide_kernel",
    )(
        place,
        *[piece.reshape(-1, D0) for piece in pieces],
        gain.reshape(1, D0),
        w_qkv,
        w_out,
        in_hbm(w_merge),
    )


def lane_half(values, low):
    lanes = lax.broadcasted_iota(jnp.int32, values.shape, 1)
    keep = lanes < HEAD if low else lanes >= HEAD
    return jnp.where(keep, values, jnp.zeros_like(values))


SLAB = 384
SLABS = 8
STRIP = 96
EDGE = SLAB + 2 * STRIP


def strip_pick():
    tile, j = np.divmod(np.arange(STRIP), CCOLS)
    pick = np.zeros((2, STRIP, SLAB), np.float32)
    last = (CROWS - 1) * CCOLS
    pick[0, np.arange(STRIP), tile * CROWS * CCOLS + last + j] = 1
    pick[1, np.arange(STRIP), tile * CROWS * CCOLS + j] = 1
    return pick


def tile_pick():
    c, i, j = np.meshgrid(np.arange(H1), np.arange(6), np.arange(8), indexing="ij")
    tile = (c + (j == 7) - (j == 0)) % H1
    jj = np.where(j == 0, 5, np.where(j == 7, 0, j - 1))
    middle = tile * 24 + (i - 1) * 6 + jj
    source = np.where(i == 0, SLAB + tile * 6 + jj, np.where(i == 5, SLAB + STRIP + tile * 6 + jj, middle))
    pick = np.zeros((H1 * EXT, EDGE), np.float32)
    pick[np.arange(H1 * EXT), source.reshape(-1)] = 1
    return pick


def coarse_forward(place, every, stats, scores_ref):
    keyval = every[:, :128]
    own = every[pl.ds(pl.multiple_of(place[2] * SLAB, SLAB), SLAB), 128:]
    queries = lane_half(own.astype(F32) * (HEAD**-0.5), True).astype(BF16)
    columns = []
    for b in range(3):
        rows = slice(128 * b, 128 * (b + 1))
        scores_ref[b] = dot(queries[rows], keyval, 1, 1)
        maxima = jnp.max(scores_ref[b], axis=1, keepdims=True)
        exponent = jnp.exp(scores_ref[b] - maxima)
        totals = jnp.sum(exponent, axis=1, keepdims=True)
        weights = (exponent * (1.0 / totals)).astype(BF16)
        attended = dot(weights, keyval, 1, 0).astype(BF16).astype(F32)
        product = lane_half(own[rows].astype(F32) * attended, False)
        columns.append((maxima + jnp.log(totals), jnp.sum(product, axis=1, keepdims=True)))
    lane = lax.broadcasted_iota(jnp.int32, (128, 128), 1)
    turned = [
        jnp.where(lane == 0, log, jnp.where(lane == 1, stat, 0.0)).T for log, stat in columns
    ]
    result = jnp.concatenate(
        [t[0:1] for t in turned] + [t[1:2] for t in turned] + [jnp.zeros((2, 128), F32)], axis=0
    )
    for r in range(SLABS):
        stats[r] = result


def run_coarse_forward(place, every):
    return pl.pallas_call(
        coarse_forward,
        out_shape=jax.ShapeDtypeStruct((SLABS, 8, 128), F32),
        in_specs=[pl.BlockSpec(memory_space=pltpu.SMEM), whole()],
        out_specs=whole(),
        scratch_shapes=[pltpu.VMEM((3, 128, SLAB * SLABS), F32)],
        compiler_params=vmem_params(16),
        cost_estimate=pl.CostEstimate(flops=10**9, bytes_accessed=2 * 10**6, transcendentals=10**6),
        name="coarse_forward",
    )(place, every)


def stat_rows(stats):
    lse = jnp.concatenate([stats[k : k + 1] for k in range(3)], axis=1)
    stat = jnp.concatenate([stats[k : k + 1] for k in range(3, 6)], axis=1)
    return lse, stat


def slab_rows(index):
    return pl.ds(pl.multiple_of(index * SLAB, SLAB), SLAB)


def turn(lse, stat):
    filler = jnp.zeros((128 - 2, lse.shape[1]), F32)
    turned = jnp.concatenate([lse, stat, filler], axis=0).T
    return turned[:, 0:1], turned[:, 1:2]


def query_side(every, rows, queries, grads, lse, stat):
    keyval = every[rows, :128]
    probs = jnp.exp(dot(queries, keyval, 1, 1) - lse)
    slopes = (probs * (dot(grads, keyval, 1, 1) - stat)).astype(BF16)
    return dot(slopes, keyval, 1, 0)


def halves(pair):
    wide = pair.astype(F32)
    return lane_half(wide * (HEAD**-0.5), True).astype(BF16), lane_half(wide, False).astype(BF16)


def coarse_own(place, every, stats, strips, edge, dq_out, dq_ref):
    row = place[2]
    edge[:SLAB] = every[slab_rows(row)]
    others = (lax.rem(row + SLABS - 1, SLABS), lax.rem(row + 1, SLABS))
    for k, other in enumerate(others):
        at = SLAB + STRIP * k
        edge[at : at + STRIP] = dot(strips[k], every[slab_rows(other)], 1, 0).astype(BF16)
    lse, stat = turn(*stat_rows(stats[0]))
    queries, grads = halves(edge[:SLAB, 128:])
    for n in range(SLABS // 2):
        rows = slice(2 * n * SLAB, 2 * (n + 1) * SLAB)
        term = query_side(every, rows, queries, grads, lse, stat)
        dq_ref[...] = term if n == 0 else dq_ref[...] + term
    dq_out[...] = (dq_ref[...] * (HEAD**-0.5)).astype(BF16)


def run_coarse_own(place, every, stats, strips):
    return pl.pallas_call(
        coarse_own,
        out_shape=[
            pltpu.HBM((EDGE, 256), BF16),
            pltpu.HBM((SLAB, 128), BF16),
        ],
        in_specs=[pl.BlockSpec(memory_space=pltpu.SMEM)] + [whole()] * 3,
        out_specs=[whole()] * 2,
        scratch_shapes=[pltpu.VMEM((SLAB, 128), F32)],
        compiler_params=vmem_params(24),
        cost_estimate=pl.CostEstimate(flops=10**9, bytes_accessed=2 * 10**6, transcendentals=10**6),
        name="coarse_own",
    )(place, every, stats, strips)


def coarse_backward(
    place,
    every,
    stats,
    strips,
    edge,
    dq_own,
    tiles_far,
    coarse_far,
    stash_far,
    merge_far,
    pick_far,
    out,
    w_coarse,
    stash,
    w_merge,
    pick,
    dq_ref,
    dk_ref,
    dv_ref,
    tiles,
    sems,
):
    pairs = (
        (tiles_far, tiles, 1),
        (coarse_far, w_coarse, 2),
        (stash_far, stash, 1),
        (merge_far, w_merge, 2),
        (pick_far, pick, 1),
    )
    copies = []
    for n, (source, target, pieces) in enumerate(pairs):
        copies += fetch(source, target, sems.at[n], pieces)
    for copy in copies:
        copy.start()
    row = place[2]
    others = (lax.rem(row + SLABS - 1, SLABS), lax.rem(row + 1, SLABS))
    taken = []
    for k, other in enumerate(others):
        both = jnp.concatenate(stat_rows(stats[other]) + (jnp.zeros((6, SLAB), F32),), axis=0)
        taken.append(
            lax.dot_general(
                both,
                strips[k].astype(F32),
                (((1,), (1,)), ((), ())),
                precision=lax.Precision.HIGHEST,
                preferred_element_type=F32,
            )
        )
    strip_lse, strip_stat = turn(
        jnp.concatenate([t[0:1] for t in taken], axis=1),
        jnp.concatenate([t[1:2] for t in taken], axis=1),
    )
    edge_k, edge_v = halves(edge[:, :128])
    edge_q, edge_g = halves(edge[SLAB:, 128:])
    for n in range(SLABS // 2):
        rows = slice(2 * n * SLAB, 2 * (n + 1) * SLAB)
        dq = query_side(every, rows, edge_q, edge_g, strip_lse, strip_stat)
        query = every[rows, 128:]
        both = [stat_rows(stats[2 * n + k]) for k in range(2)]
        lse = jnp.concatenate([pair[0] for pair in both], axis=1)
        stat = jnp.concatenate([pair[1] for pair in both], axis=1)
        probs = jnp.exp(dot(edge_k, query, 1, 1) - lse)
        slopes = (probs * (dot(edge_v, query, 1, 1) - stat)).astype(BF16)
        dk = dot(slopes, query, 1, 0)
        dv = dot(probs.astype(BF16), query, 1, 0)
        if n == 0:
            dq_ref[...] = dq
            dk_ref[...] = dk
            dv_ref[...] = dv
        else:
            dq_ref[...] += dq
            dk_ref[...] += dk
            dv_ref[...] += dv
    lanes = lax.broadcasted_iota(jnp.int32, (EDGE, 128), 1)
    keyval = jnp.where(lanes < HEAD, dk_ref[...] * (HEAD**-0.5), dv_ref[...]).astype(BF16)
    query = jnp.concatenate(
        [dq_own[...], (dq_ref[...] * (HEAD**-0.5)).astype(BF16)], axis=0
    )
    copies[0].wait()
    out[...] = dot(tiles[...], jnp.concatenate([keyval, query], axis=1), 1, 0).astype(BF16)
    for copy in copies[1:]:
        copy.wait()


def run_coarse_backward(place, every, stats, strips, edge, dq_own, *later):
    tiles = jnp.asarray(tile_pick(), BF16)
    return pl.pallas_call(
        coarse_backward,
        out_shape=[pltpu.HBM((H1 * EXT, 256), BF16)]
        + [pltpu.VMEM(array.shape, array.dtype) for array in later],
        in_specs=[pl.BlockSpec(memory_space=pltpu.SMEM)] + [whole()] * 5 + [far()] * 5,
        out_specs=[whole()] * 5,
        scratch_shapes=[
            pltpu.VMEM((2 * STRIP, 128), F32),
            pltpu.VMEM((EDGE, 128), F32),
            pltpu.VMEM((EDGE, 128), F32),
            pltpu.VMEM(tiles.shape, BF16),
            pltpu.SemaphoreType.DMA((5, 4)),
        ],
        compiler_params=vmem_params(16),
        cost_estimate=pl.CostEstimate(flops=3 * 10**9, bytes_accessed=2 * 10**6, transcendentals=4 * 10**6),
        name="coarse_backward",
    )(
        place,
        every,
        stats,
        strips,
        in_hbm(edge),
        in_hbm(dq_own),
        *[in_hbm(array) for array in (tiles,) + later],
    )


def block_pick():
    c, b = np.meshgrid(np.arange(H1), np.arange(64), indexing="ij")
    source = np.where(b < 48, 48 * c + b, 3 * D0 + 16 * c + b - 48).reshape(-1)
    pick = np.zeros((4 * D0, 4 * D0), np.float32)
    pick[source, np.arange(4 * D0)] = 1
    return pick


def merged_order(back):
    rows = lax.broadcasted_iota(jnp.int32, (BLOCK, BLOCK), 0)
    cols = lax.broadcasted_iota(jnp.int32, (BLOCK, BLOCK), 1)
    merged, grid = (cols, rows) if back else (rows, cols)
    a = merged // C4
    c = merged // 8 % MERGE
    j = merged % 8
    return (grid == a * C4 + j * MERGE + c).astype(F32).astype(BF16)


def backward_kernel(
    place,
    terms_coarse,
    own_fine,
    own_coarse,
    above,
    below,
    grads_left,
    grads_right,
    coarse,
    lse,
    gain_coarse,
    gain,
    w_qkv,
    w_out,
    w_coarse,
    stash,
    pick_block,
    w_merge,
    grad_tokens,
    terms,
    grad_fine,
    sp32,
    gh_ref,
    ga_ref,
    dq_ref,
    dk_ref,
    dv_ref,
    gt_ref,
    stack_ref,
    probs_ref,
):
    queries = stash.at[pl.ds(AT_Q, N4)]
    attended = stash.at[pl.ds(AT_ATT, N4)]
    keys_w = stash.at[pl.ds(AT_K, WROWS * C4)]
    values_w = stash.at[pl.ds(AT_V, WROWS * C4)]
    tokens_own = stash.at[pl.ds(AT_X, OWN)]
    row0 = place[0]
    col0 = place[1]
    wide = CCOLS + 2
    fine_rows, coarse_rows = grads_of(own_fine, own_coarse, above, below)
    side = [part[...].astype(F32) for part in (grads_left, grads_right)]
    for i, row in enumerate(fine_rows):
        outer = [part[4 * i : 4 * (i + 1)] for part in side]
        grad_fine[C4 * i : C4 * (i + 1)] = jnp.concatenate([outer[0], row, outer[1]], axis=0)
    grad_coarse = []
    for i, row in enumerate(coarse_rows):
        parts = []
        for g, piece in enumerate(row):
            at = 4 * R4 + 4 * i + g
            outer = [part[at : at + 1] for part in side]
            parts.append(jnp.concatenate([outer[0], piece, outer[1]], axis=0))
        grad_coarse.append(jnp.concatenate(parts, axis=1))
    grad_coarse = jnp.concatenate(grad_coarse, axis=0)
    parts = []
    for h in range(H1):
        block = terms_coarse[h].astype(F32)
        parts += [block[:, 128:192], block[:, :128]]
    heads = jnp.concatenate(parts, axis=1).astype(BF16)
    upstream = dot(heads, w_coarse[...], 1, 1) * gain_coarse[...]
    normed, inverse = norm_forward(coarse[...].astype(F32))
    back = norm_backward(upstream, normed, inverse)
    change = (grad_coarse + back).astype(BF16)
    for a in range(MERGE):
        sp32[a] = dot(change, w_merge[D1 * a : D1 * (a + 1)], 1, 1)
    window = window_bias(C4, -3)
    for b in range(BLOCKS):
        stacked = stack_heads(queries[BLOCK * b : BLOCK * (b + 1)].astype(F32)).astype(BF16)
        stack_ref[b] = stacked
        bias = all_heads(window + key_bias(C4, row0 - 7 + 4 * b, col0 - 4))
        scores = dot(keys_w[BLOCK * b : BLOCK * b + 10 * C4], stacked, 1, 1) + bias
        probs_ref[b] = jnp.exp(scores - lse[b : b + 1])
    to_merged = merged_order(False)
    to_grid = merged_order(True)
    for i in range(CROWS + 2):
        block = slice(BLOCK * i, BLOCK * (i + 1))
        rows = slice(wide * i, wide * (i + 1))
        spread = [
            sp32[a, rows, D0 * c : D0 * (c + 1)] for a in range(MERGE) for c in range(MERGE)
        ]
        total = dot(to_merged, grad_fine[block].astype(BF16), 1, 0) + jnp.concatenate(spread, axis=0)
        gh_ref[block] = dot(to_grid, total.astype(BF16), 1, 0).astype(BF16)
    ga_ref[...] = dot(gh_ref[...], w_out[...], 1, 1).astype(BF16)
    dk_ref[...] = jnp.zeros_like(dk_ref)
    dv_ref[...] = jnp.zeros_like(dv_ref)
    pick = (
        lax.broadcasted_iota(jnp.int32, (8, D0), 1) // HEAD
        == lax.broadcasted_iota(jnp.int32, (8, D0), 0)
    ).astype(F32).astype(BF16)
    for b in range(BLOCKS):
        at = slice(BLOCK * b, BLOCK * (b + 1))
        keep = slice(BLOCK * b, BLOCK * b + 10 * C4)
        grad = ga_ref[at].astype(F32)
        product = grad * attended[at].astype(F32)
        upper = product.astype(BF16)
        lower = (product - upper.astype(F32)).astype(BF16)
        sums = dot(pick, upper, 1, 1) + dot(pick, lower, 1, 1)
        stat = jnp.concatenate([sums[h : h + 1] for h in range(H0)], axis=1)
        stack_q = stack_ref[b]
        stack_g = stack_heads(grad).astype(BF16)
        key_block = keys_w[keep]
        probs = probs_ref[b]
        slopes = (probs * (dot(values_w[keep], stack_g, 1, 1) - stat)).astype(BF16)
        dk_ref[keep] += dot(slopes, stack_q, 1, 0)
        dv_ref[keep] += dot(probs.astype(BF16), stack_g, 1, 0)
        if 1 <= b <= 4:
            dq = unstack_heads(dot(slopes, key_block, 0, 0)) * (HEAD**-0.5)
            dq_ref[BLOCK * (b - 1) : BLOCK * b] = dq.astype(BF16)
    own = slice(7 * C4, 7 * C4 + OWN)
    grads = jnp.concatenate(
        [dq_ref[...], dk_ref[own].astype(BF16), dv_ref[own].astype(BF16)], axis=1
    )
    column = lax.broadcasted_iota(jnp.int32, (ROWS, C4, D0), 1).reshape(OWN, D0)
    in_tile = (column >= 4) & (column < 4 + COLS)
    normed, inverse = norm_forward(tokens_own[...].astype(F32))
    rounded = jnp.where(in_tile, normed * gain[...], 0.0).astype(BF16)
    term_qkv = dot(rounded, grads, 0, 0).astype(BF16)
    inner = slice(BLOCK, BLOCK + OWN)
    att = jnp.where(in_tile, attended[inner].astype(F32), 0.0).astype(BF16)
    term_out = dot(att, gh_ref[inner], 0, 0).astype(BF16)
    both = dot(jnp.concatenate([term_qkv, term_out], axis=1), pick_block[...], 1, 0)
    low = lax.broadcasted_iota(jnp.int32, (16, 128), 1) < 64
    for r in range(8):
        for m in range(8):
            first = both[32 * r : 32 * r + 16, 128 * m : 128 * (m + 1)]
            last = both[32 * r + 16 : 32 * (r + 1), 128 * m : 128 * (m + 1)]
            terms[16 * r + 2 * m] = jnp.where(low, first, pltpu.roll(last, 64, 1)).astype(BF16)
            terms[16 * r + 2 * m + 1] = jnp.where(low, pltpu.roll(first, 64, 1), last).astype(BF16)
    upstream = dot(grads, w_qkv[...], 1, 1) * gain[...]
    gt_ref[...] = gh_ref[inner].astype(F32) + norm_backward(upstream, normed, inverse)
    for pair in range(ROWS // 2):
        parts = [gt_ref[pl.ds(i * C4 + 4, COLS), :] for i in (2 * pair, 2 * pair + 1)]
        grad_tokens[2 * COLS * pair : 2 * COLS * (pair + 1)] = jnp.concatenate(
            parts, axis=0
        ).astype(BF16)


def run_backward(place, *operands):
    shapes = [((ROWS * COLS, D0), BF16), ((128, 16, 128), BF16)]
    return pl.pallas_call(
        backward_kernel,
        out_shape=[jax.ShapeDtypeStruct(s, d) for s, d in shapes],
        in_specs=[pl.BlockSpec(memory_space=pltpu.SMEM)] + [whole()] * 17,
        out_specs=[whole()] * 2,
        scratch_shapes=[
            pltpu.VMEM((N4, D0), F32),
            pltpu.VMEM((MERGE, EXT, D1), F32),
            pltpu.VMEM((N4, D0), BF16),
            pltpu.VMEM((N4, D0), BF16),
            pltpu.VMEM((OWN, D0), BF16),
            pltpu.VMEM((WROWS * C4, D0), F32),
            pltpu.VMEM((WROWS * C4, D0), F32),
            pltpu.VMEM((OWN, D0), F32),
            pltpu.VMEM((BLOCKS, H0 * BLOCK, D0), BF16),
            pltpu.VMEM((BLOCKS, 10 * C4, H0 * BLOCK), F32),
        ],
        compiler_params=vmem_params(20),
        cost_estimate=pl.CostEstimate(flops=5 * 10**9, bytes_accessed=2 * 10**7, transcendentals=10**6),
        name="backward_kernel",
    )(place, *operands)


def sum_terms(terms, out_qkv, out_out):
    total = jnp.sum(terms[...].astype(F32), axis=0)
    total = jnp.concatenate([total[:, :64], total[:, 64:]], axis=0)
    out_qkv[...] = total[:, :48]
    out_out[...] = total[:, 48:].T


def run_sum_terms(terms):
    return pl.pallas_call(
        sum_terms,
        out_shape=[jax.ShapeDtypeStruct((32, 48), F32), jax.ShapeDtypeStruct((16, 32), F32)],
        in_specs=[whole()],
        out_specs=[whole()] * 2,
        compiler_params=vmem_params(8),
        name="sum_terms",
    )(terms)


def ring(axis, step):
    devices = lax.axis_size(axis)
    return [(i, (i + step) % devices) for i in range(devices)]


def swap_edges(first, last, axis):
    before = lax.ppermute(last, axis, ring(axis, 1))
    after = lax.ppermute(first, axis, ring(axis, -1))
    return before, after


HALO = 8
TOKEN_ROWS = HALO * COLS
FINE_ROWS = 4 * COLS
STRIP_ROWS = TOKEN_ROWS + FINE_ROWS + 4 * CCOLS


def row_strips(tokens, grad_fine, grad_coarse, first, last, flat, held, sems):
    fine_at = pl.ds(TOKEN_ROWS, FINE_ROWS)
    own = ROWS * COLS
    copies = [
        pltpu.make_async_copy(grad_coarse, held, sems.at[0]),
        pltpu.make_async_copy(
            tokens.at[pl.ds(0, TOKEN_ROWS)], first.at[pl.ds(0, TOKEN_ROWS)], sems.at[1]
        ),
        pltpu.make_async_copy(
            tokens.at[pl.ds(own - TOKEN_ROWS, TOKEN_ROWS)],
            last.at[pl.ds(0, TOKEN_ROWS)],
            sems.at[2],
        ),
        pltpu.make_async_copy(grad_fine.at[pl.ds(0, FINE_ROWS)], first.at[fine_at], sems.at[3]),
        pltpu.make_async_copy(
            grad_fine.at[pl.ds(own - FINE_ROWS, FINE_ROWS)], last.at[fine_at], sems.at[4]
        ),
    ]
    for copy in copies:
        copy.start()
    copies[0].wait()
    wide = held[...].astype(F32)
    rows = [wide[:, i, :] for i in range(CROWS)]
    flat[...] = jnp.concatenate(rows, axis=0).astype(BF16)
    for out, coarse in ((first, rows[0]), (last, rows[-1])):
        pieces = [coarse[:, D0 * g : D0 * (g + 1)] for g in range(4)]
        out[TOKEN_ROWS + FINE_ROWS :] = jnp.concatenate(pieces, axis=0).astype(BF16)
    for copy in copies[1:]:
        copy.wait()


def run_row_strips(tokens, grad_fine, grad_coarse):
    shapes = [(STRIP_ROWS, D0), (STRIP_ROWS, D0), (CROWS * CCOLS, D1)]
    operands = (tokens.reshape(-1, D0), grad_fine.reshape(-1, D0), grad_coarse.transpose(1, 0, 2))
    return pl.pallas_call(
        row_strips,
        out_shape=[jax.ShapeDtypeStruct(shape, BF16) for shape in shapes],
        in_specs=[far()] * 3,
        out_specs=[whole()] * 3,
        scratch_shapes=[
            pltpu.VMEM((CCOLS, CROWS, D1), BF16),
            pltpu.SemaphoreType.DMA((5,)),
        ],
        compiler_params=vmem_params(8),
        name="row_strips",
    )(*[in_hbm(operand) for operand in operands])


def column_strips(tokens, above, below, first, last):
    parts = [part[:TOKEN_ROWS].astype(F32) for part in (above, below)]
    parts.insert(1, tokens[...].astype(F32))
    left = []
    right = []
    for part in parts:
        for i in range(part.shape[0] // COLS):
            left.append(part[COLS * i : COLS * i + HALO])
            right.append(part[COLS * (i + 1) - HALO : COLS * (i + 1)])
    first[...] = jnp.concatenate(left, axis=0).astype(BF16)
    last[...] = jnp.concatenate(right, axis=0).astype(BF16)


def run_column_strips(tokens, above, below):
    return pl.pallas_call(
        column_strips,
        out_shape=[jax.ShapeDtypeStruct((R8 * HALO, D0), BF16)] * 2,
        in_specs=[whole()] * 3,
        out_specs=[whole()] * 2,
        compiler_params=vmem_params(8),
        name="column_strips",
    )(in_hbm(tokens.reshape(-1, D0)), above, below)


def grads_of(own_fine, own_coarse, above, below):
    at = TOKEN_ROWS + FINE_ROWS
    fine = []
    coarse = []
    for outer in (above, below):
        outer_fine = outer[TOKEN_ROWS:at].astype(F32)
        outer_coarse = outer[at:].astype(F32)
        fine.append([outer_fine[COLS * i : COLS * (i + 1)] for i in range(4)])
        coarse.append([outer_coarse[CCOLS * g : CCOLS * (g + 1)] for g in range(4)])
    wide = own_fine[...].astype(F32)
    flat = own_coarse[...].astype(F32)
    fine_rows = fine[0] + [wide[COLS * i : COLS * (i + 1)] for i in range(ROWS)] + fine[1]
    own = [
        [flat[CCOLS * i : CCOLS * (i + 1), D0 * g : D0 * (g + 1)] for g in range(4)]
        for i in range(CROWS)
    ]
    return fine_rows, [coarse[0]] + own + [coarse[1]]


def grad_strips(own_fine, own_coarse, above, below, first, last):
    fine, coarse = grads_of(own_fine, own_coarse, above, below)
    left = [row[:4] for row in fine] + [piece[:1] for row in coarse for piece in row]
    right = [row[-4:] for row in fine] + [piece[-1:] for row in coarse for piece in row]
    first[...] = jnp.concatenate(left, axis=0).astype(BF16)
    last[...] = jnp.concatenate(right, axis=0).astype(BF16)


def run_grad_strips(own_fine, own_coarse, above, below):
    return pl.pallas_call(
        grad_strips,
        out_shape=[jax.ShapeDtypeStruct((R4 * 4 + EXT // 2, D0), BF16)] * 2,
        in_specs=[whole()] * 4,
        out_specs=[whole()] * 2,
        compiler_params=vmem_params(8),
        name="grad_strips",
    )(own_fine, own_coarse, above, below)


def on_device(
    tokens,
    grad_fine,
    grad_coarse,
    fine_gain,
    fine_qkv,
    fine_out,
    merge_weight,
    coarse_gain,
    coarse_qkv,
    coarse_out,
):
    row = lax.axis_index("row")
    col = lax.axis_index("col")
    place = jnp.stack([row * ROWS, col * COLS, row]).astype(jnp.int32)
    first, last, grad_coarse = run_row_strips(tokens, grad_fine, grad_coarse)
    above, below = swap_edges(first, last, "row")
    left, right = swap_edges(*run_column_strips(tokens, above, below), "col")
    pieces = (tokens, above, below, left, right)
    grad_heads = jnp.dot(grad_coarse, coarse_out.T, preferred_element_type=F32).astype(BF16)
    packed = run_near(
        place,
        pieces,
        fine_gain,
        fine_qkv,
        fine_out,
        merge_weight,
        coarse_gain,
        coarse_qkv,
        grad_heads,
    )
    packed, grad_fine, grad_coarse, *pieces = lax.optimization_barrier(
        (packed, grad_fine, grad_coarse, *pieces)
    )
    every = lax.all_to_all(
        packed.reshape(8 * H1, CROWS * CCOLS, 256),
        ("row", "col"),
        split_axis=0,
        concat_axis=0,
        tiled=True,
    )
    grads = (grad_fine.reshape(-1, D0), grad_coarse, pieces[1], pieces[2])
    left, right = swap_edges(*run_grad_strips(*grads), "col")
    stash, lse, coarse = run_wide(place, pieces, fine_gain, fine_qkv, fine_out, merge_weight)
    every, left, right, stash, lse, coarse = lax.optimization_barrier(
        (every, left, right, stash, lse, coarse)
    )
    every = every.reshape(SLAB * SLABS, 256)
    strips = jnp.asarray(strip_pick(), BF16)
    own_stats = run_coarse_forward(place, every)
    stats = lax.all_to_all(own_stats, "row", split_axis=0, concat_axis=0, tiled=True)
    edge, dq_own = run_coarse_own(place, every, own_stats, strips)
    pick = jnp.asarray(block_pick(), BF16)
    tiles, near_coarse, stash, near_merge, pick = run_coarse_backward(
        place, every, stats, strips, edge, dq_own, coarse_qkv, stash, merge_weight, pick
    )
    tiles = tiles.reshape(H1, EXT, 256)
    terms = lax.all_to_all(tiles, "col", split_axis=0, concat_axis=0, tiled=True)
    grad_tokens, blocks = run_backward(
        place,
        terms,
        *grads,
        left,
        right,
        coarse,
        lse,
        coarse_gain.reshape(1, D1),
        fine_gain.reshape(1, D0),
        fine_qkv,
        fine_out,
        near_coarse,
        stash,
        pick,
        near_merge,
    )
    blocks = lax.all_to_all(blocks, ("row", "col"), split_axis=0, concat_axis=0, tiled=True)
    grad_qkv, grad_out = run_sum_terms(blocks)
    return grad_tokens.reshape(ROWS, COLS, D0), grad_qkv, grad_out.T


def solution(mesh):
    return jax.shard_map(
        on_device,
        mesh=mesh,
        in_specs=(P("row", "col", None),) * 3 + (P(),) * 7,
        out_specs=(P("row", "col", None), P("row", "col"), P("row", "col")),
        check_vma=False,
    )
```

```python
import jax
import jax.numpy as jnp
import numpy as np
from jax import lax
from jax.experimental import pallas as pl
from jax.experimental.pallas import tpu as pltpu
from jax.sharding import PartitionSpec as P

H0 = 4
H1 = 16
HEAD = 64
MERGE = 4
EPSILON = 1e-05
FAR = 1e30
D0 = 256
D1 = 1024

ROWS, COLS = 16, 24
CROWS, CCOLS = 4, 6
R8, C8 = ROWS + 16, COLS + 16
R4, C4 = ROWS + 8, COLS + 8
N4 = R4 * C4
BLOCK = 4 * C4
BLOCKS = R4 // 4
WROWS = R4 + 6
OWN = ROWS * C4
EXT = (CROWS + 2) * (CCOLS + 2)

F32 = jnp.float32
BF16 = jnp.bfloat16


def vmem_params(mib):
    return pltpu.CompilerParams(vmem_limit_bytes=mib * 1024 * 1024)


def whole():
    return pl.BlockSpec(memory_space=pltpu.VMEM)


def far():
    return pl.BlockSpec(memory_space=pltpu.HBM)


def fetch(source, target, sems, pieces):
    rows = source.shape[0] // pieces
    return [
        pltpu.make_async_copy(
            source.at[pl.ds(n * rows, rows)], target.at[pl.ds(n * rows, rows)], sems.at[n]
        )
        for n in range(pieces)
    ]


def dot(a, b, ca, cb):
    return lax.dot_general(a, b, (((ca,), (cb,)), ((), ())), preferred_element_type=F32)


def norm_forward(values):
    center = values - jnp.mean(values, axis=-1, keepdims=True)
    inverse = lax.rsqrt(jnp.mean(center * center, axis=-1, keepdims=True) + EPSILON)
    return center * inverse, inverse


def norm_backward(scaled, normed, inverse):
    return inverse * (
        scaled
        - jnp.mean(scaled, axis=-1, keepdims=True)
        - normed * jnp.mean(scaled * normed, axis=-1, keepdims=True)
    )


def head_lanes(rows):
    return lax.broadcasted_iota(jnp.int32, (rows, D0), 1) // HEAD


def stack_heads(values):
    lanes = head_lanes(values.shape[0])
    zero = jnp.zeros_like(values)
    return jnp.concatenate([jnp.where(lanes == h, values, zero) for h in range(H0)], axis=0)


def unstack_heads(stacked):
    rows = stacked.shape[0] // H0
    lanes = head_lanes(rows)
    result = stacked[:rows]
    for h in range(1, H0):
        result = jnp.where(lanes == h, stacked[h * rows : (h + 1) * rows], result)
    return result


AT_Q = 0
AT_ATT = N4
AT_K = 2 * N4
AT_V = AT_K + WROWS * C4
AT_X = AT_V + WROWS * C4
STASH = AT_X + OWN


def window_bias(key_cols, col_shift):
    shape = (10, key_cols, BLOCK)
    kr = lax.broadcasted_iota(jnp.int32, shape, 0)
    kc = lax.broadcasted_iota(jnp.int32, shape, 1)
    lane = lax.broadcasted_iota(jnp.int32, shape, 2)
    row_gap = kr - lane // C4
    col_gap = kc - lane % C4 - col_shift
    near = (row_gap >= 0) & (row_gap <= 6) & (col_gap >= 0) & (col_gap <= 6)
    return jnp.where(near, 0.0, -FAR).reshape(10 * key_cols, BLOCK)


def key_bias(key_cols, key_row, key_col):
    shape = (10, key_cols, 1)
    grid_row = key_row + lax.broadcasted_iota(jnp.int32, shape, 0)
    grid_col = key_col + lax.broadcasted_iota(jnp.int32, shape, 1)
    inside = (grid_row >= 0) & (grid_row < 128) & (grid_col >= 0) & (grid_col < 384)
    return jnp.where(inside, 0.0, -FAR).reshape(10 * key_cols, 1)


def all_heads(bias):
    return jnp.concatenate([bias] * H0, axis=1)


def near_kernel(
    place,
    tokens,
    above,
    below,
    left,
    right,
    gain,
    w_qkv,
    w_out,
    w_merge_far,
    gain_coarse,
    w_coarse_far,
    grads,
    packed_far,
    x32,
    keys,
    values,
    hid32,
    merged,
    w_merge,
    w_coarse,
    packed,
    merge_sems,
    coarse_sems,
    packed_sems,
):
    merge_copies = fetch(w_merge_far, w_merge, merge_sems, 2)
    coarse_copies = fetch(w_coarse_far, w_coarse, coarse_sems, 4)
    for copy in merge_copies + coarse_copies:
        copy.start()
    row0 = place[0]
    col0 = place[1]
    middle = [part[: 8 * COLS].astype(F32) for part in (above, below)]
    middle.insert(1, tokens[...].astype(F32))
    sides = [left[...].astype(F32), right[...].astype(F32)]
    for t in range(ROWS + 6):
        e = t + 5
        part, at = (0, e) if e < 8 else (1, e - 8) if e < 8 + ROWS else (2, e - 8 - ROWS)
        x32[C4 * t : C4 * (t + 1)] = jnp.concatenate(
            [
                sides[0][8 * e + 4 : 8 * e + 8],
                middle[part][COLS * at : COLS * (at + 1)],
                sides[1][8 * e : 8 * e + 4],
            ],
            axis=0,
        )
    normed, _ = norm_forward(x32[...])
    normed = (normed * gain[...]).astype(BF16)
    inner = slice(3 * C4, 3 * C4 + OWN)
    queries = dot(normed[inner], w_qkv[:, :D0], 1, 0).astype(BF16).astype(F32) * (HEAD**-0.5)
    keys[...] = dot(normed, w_qkv[:, D0 : 2 * D0], 1, 0).astype(BF16)
    values[...] = dot(normed, w_qkv[:, 2 * D0 :], 1, 0).astype(BF16)
    window = window_bias(C4, -3)
    for b in range(ROWS // 4):
        block = slice(BLOCK * b, BLOCK * b + 10 * C4)
        stacked = stack_heads(queries[BLOCK * b : BLOCK * (b + 1)]).astype(BF16)
        bias = all_heads(window + key_bias(C4, row0 - 3 + 4 * b, col0 - 4))
        scores = dot(keys[block], stacked, 1, 1) + bias
        maxima = jnp.max(scores, axis=0, keepdims=True)
        exponent = jnp.exp(scores - maxima)
        totals = jnp.sum(exponent, axis=0, keepdims=True)
        weights = (exponent * (1.0 / totals)).astype(BF16)
        attended = unstack_heads(dot(weights, values[block], 0, 0)).astype(BF16)
        at = BLOCK * b
        own = x32[3 * C4 + at : 3 * C4 + at + BLOCK]
        total = (own + dot(attended, w_out[...], 1, 0)).astype(BF16).astype(F32)
        hid32[0, at : at + BLOCK] = total[:, :128]
        hid32[1, at : at + BLOCK] = total[:, 128:]
    wide = CCOLS + 2
    merge_rows(hid32, merged, CROWS)
    total = None
    for n in range(4):
        if n % 2 == 0:
            merge_copies[n // 2].wait()
        part = dot(merged[:, D1 * n : D1 * (n + 1)], w_merge[D1 * n : D1 * (n + 1)], 1, 0)
        total = part if total is None else total + part
    normed, _ = norm_forward(total.astype(BF16).astype(F32))
    normed = normed * gain_coarse[...]
    parts = [normed[wide * i + 1 : wide * i + 1 + CCOLS] for i in range(CROWS)]
    normed = jnp.concatenate(parts, axis=0).astype(BF16)
    for copy in coarse_copies:
        copy.wait()
    packed_copies = []
    for n in range(4):
        result = dot(normed, w_coarse[:, 768 * n : 768 * (n + 1)], 1, 0)
        grad = grads[:, 256 * n : 256 * (n + 1)].astype(F32)
        parts = []
        for h in range(4):
            q = result[:, 192 * h : 192 * h + 64]
            k = result[:, 192 * h + 64 : 192 * h + 128]
            v = result[:, 192 * h + 128 : 192 * h + 192]
            g = grad[:, 64 * h : 64 * h + 64]
            parts.append(jnp.concatenate([k, v, q, g], axis=1))
        packed[2 * n] = jnp.concatenate(parts[:2], axis=0).astype(BF16)
        packed[2 * n + 1] = jnp.concatenate(parts[2:], axis=0).astype(BF16)
        at = pl.ds(2 * n, 2)
        for r in range(8):
            packed_copies.append(
                pltpu.make_async_copy(packed.at[at], packed_far.at[r, at], packed_sems.at[n, r])
            )
            packed_copies[-1].start()
    for copy in packed_copies:
        copy.wait()


def merge_rows(hid32, merged, count):
    for pair in range(count // 2):
        for a in range(MERGE):
            for c in range(MERGE):
                for half in range(2):
                    parts = [
                        hid32[half, pl.ds((4 * i + a) * C4 + c, CCOLS + 2, stride=MERGE), :]
                        for i in (2 * pair, 2 * pair + 1)
                    ]
                    at = (a * MERGE + c) * D0 + half * 128
                    merged[16 * pair : 16 * (pair + 1), at : at + 128] = jnp.concatenate(
                        parts, axis=0
                    ).astype(BF16)


def run_near(place, pieces, gain, w_qkv, w_out, w_merge, gain_coarse, w_coarse, grads):
    own = CROWS * CCOLS
    return pl.pallas_call(
        near_kernel,
        out_shape=pltpu.HBM((8, 8, 2 * own, 256), BF16),
        in_specs=[pl.BlockSpec(memory_space=pltpu.SMEM)]
        + [whole()] * 8
        + [far(), whole(), far(), whole()],
        out_specs=far(),
        scratch_shapes=[
            pltpu.VMEM(((ROWS + 6) * C4, D0), F32),
            pltpu.VMEM(((ROWS + 6) * C4, D0), BF16),
            pltpu.VMEM(((ROWS + 6) * C4, D0), BF16),
            pltpu.VMEM((2, OWN, 128), F32),
            pltpu.VMEM((CROWS * (CCOLS + 2), MERGE * MERGE * D0), BF16),
            pltpu.VMEM(w_merge.shape, BF16),
            pltpu.VMEM(w_coarse.shape, BF16),
            pltpu.VMEM((8, 2 * own, 256), BF16),
            pltpu.SemaphoreType.DMA((2,)),
            pltpu.SemaphoreType.DMA((4,)),
            pltpu.SemaphoreType.DMA((4, 8)),
        ],
        compiler_params=vmem_params(48),
        cost_estimate=pl.CostEstimate(flops=3 * 10**9, bytes_accessed=2 * 10**7, transcendentals=10**6),
        name="near_kernel",
    )(
        place,
        *[piece.reshape(-1, D0) for piece in pieces],
        gain.reshape(1, D0),
        w_qkv,
        w_out,
        in_hbm(w_merge),
        gain_coarse.reshape(1, D1),
        in_hbm(w_coarse),
        grads,
    )


def in_hbm(array):
    return pltpu.with_memory_space_constraint(array, pltpu.HBM)


def wide_kernel(
    place,
    tokens,
    above,
    below,
    left,
    right,
    gain,
    w_qkv,
    w_out,
    w_merge_far,
    stash_far,
    lse,
    coarse_out,
    x32,
    q32,
    k32,
    v32,
    hid32,
    stash,
    merged,
    w_merge,
    merge_sems,
    stash_sem,
):
    merge_copies = fetch(w_merge_far, w_merge, merge_sems, 4)
    for copy in merge_copies:
        copy.start()
    queries = stash.at[pl.ds(AT_Q, N4)]
    attended = stash.at[pl.ds(AT_ATT, N4)]
    keys_w = stash.at[pl.ds(AT_K, WROWS * C4)]
    values_w = stash.at[pl.ds(AT_V, WROWS * C4)]
    tokens_own = stash.at[pl.ds(AT_X, OWN)]
    row0 = place[0]
    col0 = place[1]
    middle = [part[: 8 * COLS].astype(F32) for part in (above, below)]
    middle.insert(1, tokens[...].astype(F32))
    sides = [left[...].astype(F32), right[...].astype(F32)]
    for i in range(R8):
        part, at = (0, i) if i < 8 else (1, i - 8) if i < 8 + ROWS else (2, i - 8 - ROWS)
        x32[C8 * i : C8 * i + 8] = sides[0][8 * i : 8 * i + 8]
        x32[C8 * i + 8 : C8 * i + 8 + COLS] = middle[part][COLS * at : COLS * (at + 1)]
        x32[C8 * i + 8 + COLS : C8 * (i + 1)] = sides[1][8 * i : 8 * i + 8]
    normed, _ = norm_forward(x32[...])
    normed = (normed * gain[...]).astype(BF16)
    q32[...] = dot(normed, w_qkv[:, :D0], 1, 0).astype(BF16).astype(F32) * (HEAD**-0.5)
    k32[...] = dot(normed, w_qkv[:, D0 : 2 * D0], 1, 0).astype(BF16).astype(F32)
    v32[...] = dot(normed, w_qkv[:, 2 * D0 :], 1, 0).astype(BF16).astype(F32)
    for i in range(R4):
        queries[C4 * i : C4 * (i + 1)] = q32[pl.ds((i + 4) * C8 + 4, C4), :].astype(BF16)
    for i in range(WROWS):
        keys_w[C4 * i : C4 * (i + 1)] = k32[pl.ds((i + 1) * C8 + 4, C4), :].astype(BF16)
        values_w[C4 * i : C4 * (i + 1)] = v32[pl.ds((i + 1) * C8 + 4, C4), :].astype(BF16)
    for i in range(ROWS):
        tokens_own[C4 * i : C4 * (i + 1)] = x32[pl.ds((i + 8) * C8 + 4, C4), :].astype(BF16)
    lse[...] = jnp.full(lse.shape, FAR, F32)
    window = window_bias(C8, 1)
    for b in range(BLOCKS):
        start = (4 * b + 1) * C8
        key_block = k32[start : start + 10 * C8].astype(BF16)
        value_block = v32[start : start + 10 * C8].astype(BF16)
        stacked = stack_heads(queries[BLOCK * b : BLOCK * (b + 1)].astype(F32)).astype(BF16)
        bias = all_heads(window + key_bias(C8, row0 - 7 + 4 * b, col0 - 8))
        scores = dot(key_block, stacked, 1, 1) + bias
        maxima = jnp.max(scores, axis=0, keepdims=True)
        exponent = jnp.exp(scores - maxima)
        totals = jnp.sum(exponent, axis=0, keepdims=True)
        weights = (exponent * (1.0 / totals)).astype(BF16)
        result = unstack_heads(dot(weights, value_block, 0, 0)).astype(BF16)
        attended[BLOCK * b : BLOCK * (b + 1)] = result
        lane = lax.broadcasted_iota(jnp.int32, (1, H0 * BLOCK), 1) % BLOCK
        q_row = row0 - 4 + 4 * b + lane // C4
        q_col = col0 - 4 + lane % C4
        q_in = (q_row >= 0) & (q_row < 128) & (q_col >= 0) & (q_col < 384)
        lse[b : b + 1] = jnp.where(q_in, maxima + jnp.log(totals), FAR)
        projected = dot(result, w_out[...], 1, 0)
        for a in range(4):
            own = x32[pl.ds((4 * b + a + 4) * C8 + 4, C4), :]
            total = own + projected[C4 * a : C4 * (a + 1)]
            at = BLOCK * b + C4 * a
            total = total.astype(BF16).astype(F32)
            hid32[0, at : at + C4] = total[:, :128]
            hid32[1, at : at + C4] = total[:, 128:]
    merge_rows(hid32, merged, CROWS + 2)
    stash_copy = pltpu.make_async_copy(stash, stash_far, stash_sem)
    stash_copy.start()
    total = None
    for n, copy in enumerate(merge_copies):
        copy.wait()
        part = dot(merged[:, D1 * n : D1 * (n + 1)], w_merge[D1 * n : D1 * (n + 1)], 1, 0)
        total = part if total is None else total + part
    coarse_out[...] = total.astype(BF16)
    stash_copy.wait()


def run_wide(place, pieces, gain, w_qkv, w_out, w_merge):
    flat = R8 * C8
    return pl.pallas_call(
        wide_kernel,
        out_shape=[
            pltpu.HBM((STASH, D0), BF16),
            pltpu.HBM((8, H0 * BLOCK), F32),
            pltpu.HBM((EXT, D1), BF16),
        ],
        in_specs=[pl.BlockSpec(memory_space=pltpu.SMEM)] + [whole()] * 8 + [far()],
        out_specs=[far(), whole(), whole()],
        scratch_shapes=[pltpu.VMEM((flat, D0), F32)] * 4
        + [
            pltpu.VMEM((2, N4, 128), F32),
            pltpu.VMEM((STASH, D0), BF16),
            pltpu.VMEM((EXT, MERGE * MERGE * D0), BF16),
            pltpu.VMEM(w_merge.shape, BF16),
            pltpu.SemaphoreType.DMA((4,)),
            pltpu.SemaphoreType.DMA(()),
        ],
        compiler_params=vmem_params(40),
        cost_estimate=pl.CostEstimate(flops=3 * 10**9, bytes_accessed=10**7, transcendentals=10**6),
        name="wide_kernel",
    )(
        place,
        *[piece.reshape(-1, D0) for piece in pieces],
        gain.reshape(1, D0),
        w_qkv,
        w_out,
        in_hbm(w_merge),
    )


def lane_half(values, low):
    lanes = lax.broadcasted_iota(jnp.int32, values.shape, 1)
    keep = lanes < HEAD if low else lanes >= HEAD
    return jnp.where(keep, values, jnp.zeros_like(values))


SLAB = 384
SLABS = 8
STRIP = 96
EDGE = SLAB + 2 * STRIP


def strip_pick():
    tile, j = np.divmod(np.arange(STRIP), CCOLS)
    pick = np.zeros((2, STRIP, SLAB), np.float32)
    last = (CROWS - 1) * CCOLS
    pick[0, np.arange(STRIP), tile * CROWS * CCOLS + last + j] = 1
    pick[1, np.arange(STRIP), tile * CROWS * CCOLS + j] = 1
    return pick


def tile_pick():
    c, i, j = np.meshgrid(np.arange(H1), np.arange(6), np.arange(8), indexing="ij")
    tile = (c + (j == 7) - (j == 0)) % H1
    jj = np.where(j == 0, 5, np.where(j == 7, 0, j - 1))
    middle = tile * 24 + (i - 1) * 6 + jj
    source = np.where(i == 0, SLAB + tile * 6 + jj, np.where(i == 5, SLAB + STRIP + tile * 6 + jj, middle))
    pick = np.zeros((H1 * EXT, EDGE), np.float32)
    pick[np.arange(H1 * EXT), source.reshape(-1)] = 1
    return pick


def coarse_forward(place, every, stats, scores_ref):
    keyval = every[:, :128]
    own = every[pl.ds(pl.multiple_of(place[2] * SLAB, SLAB), SLAB), 128:]
    queries = lane_half(own.astype(F32) * (HEAD**-0.5), True).astype(BF16)
    columns = []
    for b in range(3):
        rows = slice(128 * b, 128 * (b + 1))
        scores_ref[b] = dot(queries[rows], keyval, 1, 1)
        maxima = jnp.max(scores_ref[b], axis=1, keepdims=True)
        exponent = jnp.exp(scores_ref[b] - maxima)
        totals = jnp.sum(exponent, axis=1, keepdims=True)
        weights = (exponent * (1.0 / totals)).astype(BF16)
        attended = dot(weights, keyval, 1, 0).astype(BF16).astype(F32)
        product = lane_half(own[rows].astype(F32) * attended, False)
        columns.append((maxima + jnp.log(totals), jnp.sum(product, axis=1, keepdims=True)))
    lane = lax.broadcasted_iota(jnp.int32, (128, 128), 1)
    turned = [
        jnp.where(lane == 0, log, jnp.where(lane == 1, stat, 0.0)).T for log, stat in columns
    ]
    result = jnp.concatenate(
        [t[0:1] for t in turned] + [t[1:2] for t in turned] + [jnp.zeros((2, 128), F32)], axis=0
    )
    for r in range(SLABS):
        stats[r] = result


def run_coarse_forward(place, every):
    return pl.pallas_call(
        coarse_forward,
        out_shape=jax.ShapeDtypeStruct((SLABS, 8, 128), F32),
        in_specs=[pl.BlockSpec(memory_space=pltpu.SMEM), whole()],
        out_specs=whole(),
        scratch_shapes=[pltpu.VMEM((3, 128, SLAB * SLABS), F32)],
        compiler_params=vmem_params(16),
        cost_estimate=pl.CostEstimate(flops=10**9, bytes_accessed=2 * 10**6, transcendentals=10**6),
        name="coarse_forward",
    )(place, every)


def stat_rows(stats):
    lse = jnp.concatenate([stats[k : k + 1] for k in range(3)], axis=1)
    stat = jnp.concatenate([stats[k : k + 1] for k in range(3, 6)], axis=1)
    return lse, stat


def slab_rows(index):
    return pl.ds(pl.multiple_of(index * SLAB, SLAB), SLAB)


def turn(lse, stat):
    filler = jnp.zeros((128 - 2, lse.shape[1]), F32)
    turned = jnp.concatenate([lse, stat, filler], axis=0).T
    return turned[:, 0:1], turned[:, 1:2]


def query_side(every, rows, queries, grads, lse, stat):
    keyval = every[rows, :128]
    probs = jnp.exp(dot(queries, keyval, 1, 1) - lse)
    slopes = (probs * (dot(grads, keyval, 1, 1) - stat)).astype(BF16)
    return dot(slopes, keyval, 1, 0)


def halves(pair):
    wide = pair.astype(F32)
    return lane_half(wide * (HEAD**-0.5), True).astype(BF16), lane_half(wide, False).astype(BF16)


def coarse_own(place, every, stats, strips, edge, dq_out, dq_ref):
    row = place[2]
    edge[:SLAB] = every[slab_rows(row)]
    others = (lax.rem(row + SLABS - 1, SLABS), lax.rem(row + 1, SLABS))
    for k, other in enumerate(others):
        at = SLAB + STRIP * k
        edge[at : at + STRIP] = dot(strips[k], every[slab_rows(other)], 1, 0).astype(BF16)
    lse, stat = turn(*stat_rows(stats[0]))
    queries, grads = halves(edge[:SLAB, 128:])
    for n in range(SLABS // 2):
        rows = slice(2 * n * SLAB, 2 * (n + 1) * SLAB)
        term = query_side(every, rows, queries, grads, lse, stat)
        dq_ref[...] = term if n == 0 else dq_ref[...] + term
    dq_out[...] = (dq_ref[...] * (HEAD**-0.5)).astype(BF16)


def run_coarse_own(place, every, stats, strips):
    return pl.pallas_call(
        coarse_own,
        out_shape=[
            pltpu.HBM((EDGE, 256), BF16),
            pltpu.HBM((SLAB, 128), BF16),
        ],
        in_specs=[pl.BlockSpec(memory_space=pltpu.SMEM)] + [whole()] * 3,
        out_specs=[whole()] * 2,
        scratch_shapes=[pltpu.VMEM((SLAB, 128), F32)],
        compiler_params=vmem_params(24),
        cost_estimate=pl.CostEstimate(flops=10**9, bytes_accessed=2 * 10**6, transcendentals=10**6),
        name="coarse_own",
    )(place, every, stats, strips)


def coarse_backward(
    place,
    every,
    stats,
    strips,
    edge,
    dq_own,
    tiles_far,
    coarse_far,
    stash_far,
    merge_far,
    pick_far,
    out,
    w_coarse,
    stash,
    w_merge,
    pick,
    dq_ref,
    dk_ref,
    dv_ref,
    tiles,
    sems,
):
    pairs = (
        (tiles_far, tiles, 1),
        (coarse_far, w_coarse, 2),
        (stash_far, stash, 1),
        (merge_far, w_merge, 2),
        (pick_far, pick, 1),
    )
    copies = []
    for n, (source, target, pieces) in enumerate(pairs):
        copies += fetch(source, target, sems.at[n], pieces)
    for copy in copies:
        copy.start()
    row = place[2]
    others = (lax.rem(row + SLABS - 1, SLABS), lax.rem(row + 1, SLABS))
    taken = []
    for k, other in enumerate(others):
        both = jnp.concatenate(stat_rows(stats[other]) + (jnp.zeros((6, SLAB), F32),), axis=0)
        taken.append(
            lax.dot_general(
                both,
                strips[k].astype(F32),
                (((1,), (1,)), ((), ())),
                precision=lax.Precision.HIGHEST,
                preferred_element_type=F32,
            )
        )
    strip_lse, strip_stat = turn(
        jnp.concatenate([t[0:1] for t in taken], axis=1),
        jnp.concatenate([t[1:2] for t in taken], axis=1),
    )
    edge_k, edge_v = halves(edge[:, :128])
    edge_q, edge_g = halves(edge[SLAB:, 128:])
    for n in range(SLABS // 2):
        rows = slice(2 * n * SLAB, 2 * (n + 1) * SLAB)
        dq = query_side(every, rows, edge_q, edge_g, strip_lse, strip_stat)
        query = every[rows, 128:]
        both = [stat_rows(stats[2 * n + k]) for k in range(2)]
        lse = jnp.concatenate([pair[0] for pair in both], axis=1)
        stat = jnp.concatenate([pair[1] for pair in both], axis=1)
        probs = jnp.exp(dot(edge_k, query, 1, 1) - lse)
        slopes = (probs * (dot(edge_v, query, 1, 1) - stat)).astype(BF16)
        dk = dot(slopes, query, 1, 0)
        dv = dot(probs.astype(BF16), query, 1, 0)
        if n == 0:
            dq_ref[...] = dq
            dk_ref[...] = dk
            dv_ref[...] = dv
        else:
            dq_ref[...] += dq
            dk_ref[...] += dk
            dv_ref[...] += dv
    lanes = lax.broadcasted_iota(jnp.int32, (EDGE, 128), 1)
    keyval = jnp.where(lanes < HEAD, dk_ref[...] * (HEAD**-0.5), dv_ref[...]).astype(BF16)
    query = jnp.concatenate(
        [dq_own[...], (dq_ref[...] * (HEAD**-0.5)).astype(BF16)], axis=0
    )
    copies[0].wait()
    out[...] = dot(tiles[...], jnp.concatenate([keyval, query], axis=1), 1, 0).astype(BF16)
    for copy in copies[1:]:
        copy.wait()


def run_coarse_backward(place, every, stats, strips, edge, dq_own, *later):
    tiles = jnp.asarray(tile_pick(), BF16)
    return pl.pallas_call(
        coarse_backward,
        out_shape=[pltpu.HBM((H1 * EXT, 256), BF16)]
        + [pltpu.VMEM(array.shape, array.dtype) for array in later],
        in_specs=[pl.BlockSpec(memory_space=pltpu.SMEM)] + [whole()] * 5 + [far()] * 5,
        out_specs=[whole()] * 5,
        scratch_shapes=[
            pltpu.VMEM((2 * STRIP, 128), F32),
            pltpu.VMEM((EDGE, 128), F32),
            pltpu.VMEM((EDGE, 128), F32),
            pltpu.VMEM(tiles.shape, BF16),
            pltpu.SemaphoreType.DMA((5, 4)),
        ],
        compiler_params=vmem_params(16),
        cost_estimate=pl.CostEstimate(flops=3 * 10**9, bytes_accessed=2 * 10**6, transcendentals=4 * 10**6),
        name="coarse_backward",
    )(
        place,
        every,
        stats,
        strips,
        in_hbm(edge),
        in_hbm(dq_own),
        *[in_hbm(array) for array in (tiles,) + later],
    )


def block_pick():
    c, b = np.meshgrid(np.arange(H1), np.arange(64), indexing="ij")
    source = np.where(b < 48, 48 * c + b, 3 * D0 + 16 * c + b - 48).reshape(-1)
    pick = np.zeros((4 * D0, 4 * D0), np.float32)
    pick[source, np.arange(4 * D0)] = 1
    return pick


def merged_order(back):
    rows = lax.broadcasted_iota(jnp.int32, (BLOCK, BLOCK), 0)
    cols = lax.broadcasted_iota(jnp.int32, (BLOCK, BLOCK), 1)
    merged, grid = (cols, rows) if back else (rows, cols)
    a = merged // C4
    c = merged // 8 % MERGE
    j = merged % 8
    return (grid == a * C4 + j * MERGE + c).astype(F32).astype(BF16)


def backward_kernel(
    place,
    terms_coarse,
    own_fine,
    own_coarse,
    above,
    below,
    grads_left,
    grads_right,
    coarse,
    lse,
    gain_coarse,
    gain,
    w_qkv,
    w_out,
    w_coarse,
    stash,
    pick_block,
    w_merge,
    grad_tokens,
    terms,
    grad_fine,
    sp32,
    gh_ref,
    ga_ref,
    dq_ref,
    dk_ref,
    dv_ref,
    gt_ref,
    stack_ref,
    probs_ref,
):
    queries = stash.at[pl.ds(AT_Q, N4)]
    attended = stash.at[pl.ds(AT_ATT, N4)]
    keys_w = stash.at[pl.ds(AT_K, WROWS * C4)]
    values_w = stash.at[pl.ds(AT_V, WROWS * C4)]
    tokens_own = stash.at[pl.ds(AT_X, OWN)]
    row0 = place[0]
    col0 = place[1]
    wide = CCOLS + 2
    fine_rows, coarse_rows = grads_of(own_fine, own_coarse, above, below)
    side = [part[...].astype(F32) for part in (grads_left, grads_right)]
    for i, row in enumerate(fine_rows):
        outer = [part[4 * i : 4 * (i + 1)] for part in side]
        grad_fine[C4 * i : C4 * (i + 1)] = jnp.concatenate([outer[0], row, outer[1]], axis=0)
    grad_coarse = []
    for i, row in enumerate(coarse_rows):
        parts = []
        for g, piece in enumerate(row):
            at = 4 * R4 + 4 * i + g
            outer = [part[at : at + 1] for part in side]
            parts.append(jnp.concatenate([outer[0], piece, outer[1]], axis=0))
        grad_coarse.append(jnp.concatenate(parts, axis=1))
    grad_coarse = jnp.concatenate(grad_coarse, axis=0)
    parts = []
    for h in range(H1):
        block = terms_coarse[h].astype(F32)
        parts += [block[:, 128:192], block[:, :128]]
    heads = jnp.concatenate(parts, axis=1).astype(BF16)
    upstream = dot(heads, w_coarse[...], 1, 1) * gain_coarse[...]
    normed, inverse = norm_forward(coarse[...].astype(F32))
    back = norm_backward(upstream, normed, inverse)
    change = (grad_coarse + back).astype(BF16)
    for a in range(MERGE):
        sp32[a] = dot(change, w_merge[D1 * a : D1 * (a + 1)], 1, 1)
    window = window_bias(C4, -3)
    for b in range(BLOCKS):
        stacked = stack_heads(queries[BLOCK * b : BLOCK * (b + 1)].astype(F32)).astype(BF16)
        stack_ref[b] = stacked
        bias = all_heads(window + key_bias(C4, row0 - 7 + 4 * b, col0 - 4))
        scores = dot(keys_w[BLOCK * b : BLOCK * b + 10 * C4], stacked, 1, 1) + bias
        probs_ref[b] = jnp.exp(scores - lse[b : b + 1])
    to_merged = merged_order(False)
    to_grid = merged_order(True)
    for i in range(CROWS + 2):
        block = slice(BLOCK * i, BLOCK * (i + 1))
        rows = slice(wide * i, wide * (i + 1))
        spread = [
            sp32[a, rows, D0 * c : D0 * (c + 1)] for a in range(MERGE) for c in range(MERGE)
        ]
        total = dot(to_merged, grad_fine[block].astype(BF16), 1, 0) + jnp.concatenate(spread, axis=0)
        gh_ref[block] = dot(to_grid, total.astype(BF16), 1, 0).astype(BF16)
    ga_ref[...] = dot(gh_ref[...], w_out[...], 1, 1).astype(BF16)
    dk_ref[...] = jnp.zeros_like(dk_ref)
    dv_ref[...] = jnp.zeros_like(dv_ref)
    pick = (
        lax.broadcasted_iota(jnp.int32, (8, D0), 1) // HEAD
        == lax.broadcasted_iota(jnp.int32, (8, D0), 0)
    ).astype(F32).astype(BF16)
    for b in range(BLOCKS):
        at = slice(BLOCK * b, BLOCK * (b + 1))
        keep = slice(BLOCK * b, BLOCK * b + 10 * C4)
        grad = ga_ref[at].astype(F32)
        product = grad * attended[at].astype(F32)
        upper = product.astype(BF16)
        lower = (product - upper.astype(F32)).astype(BF16)
        sums = dot(pick, upper, 1, 1) + dot(pick, lower, 1, 1)
        stat = jnp.concatenate([sums[h : h + 1] for h in range(H0)], axis=1)
        stack_q = stack_ref[b]
        stack_g = stack_heads(grad).astype(BF16)
        key_block = keys_w[keep]
        probs = probs_ref[b]
        slopes = (probs * (dot(values_w[keep], stack_g, 1, 1) - stat)).astype(BF16)
        dk_ref[keep] += dot(slopes, stack_q, 1, 0)
        dv_ref[keep] += dot(probs.astype(BF16), stack_g, 1, 0)
        if 1 <= b <= 4:
            dq = unstack_heads(dot(slopes, key_block, 0, 0)) * (HEAD**-0.5)
            dq_ref[BLOCK * (b - 1) : BLOCK * b] = dq.astype(BF16)
    own = slice(7 * C4, 7 * C4 + OWN)
    grads = jnp.concatenate(
        [dq_ref[...], dk_ref[own].astype(BF16), dv_ref[own].astype(BF16)], axis=1
    )
    column = lax.broadcasted_iota(jnp.int32, (ROWS, C4, D0), 1).reshape(OWN, D0)
    in_tile = (column >= 4) & (column < 4 + COLS)
    normed, inverse = norm_forward(tokens_own[...].astype(F32))
    rounded = jnp.where(in_tile, normed * gain[...], 0.0).astype(BF16)
    term_qkv = dot(rounded, grads, 0, 0).astype(BF16)
    inner = slice(BLOCK, BLOCK + OWN)
    att = jnp.where(in_tile, attended[inner].astype(F32), 0.0).astype(BF16)
    term_out = dot(att, gh_ref[inner], 0, 0).astype(BF16)
    both = dot(jnp.concatenate([term_qkv, term_out], axis=1), pick_block[...], 1, 0)
    low = lax.broadcasted_iota(jnp.int32, (16, 128), 1) < 64
    for r in range(8):
        for m in range(8):
            first = both[32 * r : 32 * r + 16, 128 * m : 128 * (m + 1)]
            last = both[32 * r + 16 : 32 * (r + 1), 128 * m : 128 * (m + 1)]
            terms[16 * r + 2 * m] = jnp.where(low, first, pltpu.roll(last, 64, 1)).astype(BF16)
            terms[16 * r + 2 * m + 1] = jnp.where(low, pltpu.roll(first, 64, 1), last).astype(BF16)
    upstream = dot(grads, w_qkv[...], 1, 1) * gain[...]
    gt_ref[...] = gh_ref[inner].astype(F32) + norm_backward(upstream, normed, inverse)
    for pair in range(ROWS // 2):
        parts = [gt_ref[pl.ds(i * C4 + 4, COLS), :] for i in (2 * pair, 2 * pair + 1)]
        grad_tokens[2 * COLS * pair : 2 * COLS * (pair + 1)] = jnp.concatenate(
            parts, axis=0
        ).astype(BF16)


def run_backward(place, *operands):
    shapes = [((ROWS * COLS, D0), BF16), ((128, 16, 128), BF16)]
    return pl.pallas_call(
        backward_kernel,
        out_shape=[jax.ShapeDtypeStruct(s, d) for s, d in shapes],
        in_specs=[pl.BlockSpec(memory_space=pltpu.SMEM)] + [whole()] * 17,
        out_specs=[whole()] * 2,
        scratch_shapes=[
            pltpu.VMEM((N4, D0), F32),
            pltpu.VMEM((MERGE, EXT, D1), F32),
            pltpu.VMEM((N4, D0), BF16),
            pltpu.VMEM((N4, D0), BF16),
            pltpu.VMEM((OWN, D0), BF16),
            pltpu.VMEM((WROWS * C4, D0), F32),
            pltpu.VMEM((WROWS * C4, D0), F32),
            pltpu.VMEM((OWN, D0), F32),
            pltpu.VMEM((BLOCKS, H0 * BLOCK, D0), BF16),
            pltpu.VMEM((BLOCKS, 10 * C4, H0 * BLOCK), F32),
        ],
        compiler_params=vmem_params(20),
        cost_estimate=pl.CostEstimate(flops=5 * 10**9, bytes_accessed=2 * 10**7, transcendentals=10**6),
        name="backward_kernel",
    )(place, *operands)


def sum_terms(terms, out_qkv, out_out):
    total = jnp.sum(terms[...].astype(F32), axis=0)
    total = jnp.concatenate([total[:, :64], total[:, 64:]], axis=0)
    out_qkv[...] = total[:, :48]
    out_out[...] = total[:, 48:].T


def run_sum_terms(terms):
    return pl.pallas_call(
        sum_terms,
        out_shape=[jax.ShapeDtypeStruct((32, 48), F32), jax.ShapeDtypeStruct((16, 32), F32)],
        in_specs=[whole()],
        out_specs=[whole()] * 2,
        compiler_params=vmem_params(8),
        name="sum_terms",
    )(terms)


def ring(axis, step):
    devices = lax.axis_size(axis)
    return [(i, (i + step) % devices) for i in range(devices)]


def swap_edges(first, last, axis):
    before = lax.ppermute(last, axis, ring(axis, 1))
    after = lax.ppermute(first, axis, ring(axis, -1))
    return before, after


HALO = 8
TOKEN_ROWS = HALO * COLS
FINE_ROWS = 4 * COLS
STRIP_ROWS = TOKEN_ROWS + FINE_ROWS + 4 * CCOLS


def row_strips(tokens, grad_fine, grad_coarse, first, last, flat, held, sems):
    fine_at = pl.ds(TOKEN_ROWS, FINE_ROWS)
    own = ROWS * COLS
    copies = [
        pltpu.make_async_copy(grad_coarse, held, sems.at[0]),
        pltpu.make_async_copy(
            tokens.at[pl.ds(0, TOKEN_ROWS)], first.at[pl.ds(0, TOKEN_ROWS)], sems.at[1]
        ),
        pltpu.make_async_copy(
            tokens.at[pl.ds(own - TOKEN_ROWS, TOKEN_ROWS)],
            last.at[pl.ds(0, TOKEN_ROWS)],
            sems.at[2],
        ),
        pltpu.make_async_copy(grad_fine.at[pl.ds(0, FINE_ROWS)], first.at[fine_at], sems.at[3]),
        pltpu.make_async_copy(
            grad_fine.at[pl.ds(own - FINE_ROWS, FINE_ROWS)], last.at[fine_at], sems.at[4]
        ),
    ]
    for copy in copies:
        copy.start()
    copies[0].wait()
    wide = held[...].astype(F32)
    rows = [wide[:, i, :] for i in range(CROWS)]
    flat[...] = jnp.concatenate(rows, axis=0).astype(BF16)
    for out, coarse in ((first, rows[0]), (last, rows[-1])):
        pieces = [coarse[:, D0 * g : D0 * (g + 1)] for g in range(4)]
        out[TOKEN_ROWS + FINE_ROWS :] = jnp.concatenate(pieces, axis=0).astype(BF16)
    for copy in copies[1:]:
        copy.wait()


def run_row_strips(tokens, grad_fine, grad_coarse):
    shapes = [(STRIP_ROWS, D0), (STRIP_ROWS, D0), (CROWS * CCOLS, D1)]
    operands = (tokens.reshape(-1, D0), grad_fine.reshape(-1, D0), grad_coarse.transpose(1, 0, 2))
    return pl.pallas_call(
        row_strips,
        out_shape=[jax.ShapeDtypeStruct(shape, BF16) for shape in shapes],
        in_specs=[far()] * 3,
        out_specs=[whole()] * 3,
        scratch_shapes=[
            pltpu.VMEM((CCOLS, CROWS, D1), BF16),
            pltpu.SemaphoreType.DMA((5,)),
        ],
        compiler_params=vmem_params(8),
        name="row_strips",
    )(*[in_hbm(operand) for operand in operands])


def own_columns(tokens, first, last):
    wide = tokens[...].astype(F32)
    rows = [wide[COLS * i : COLS * (i + 1)] for i in range(ROWS)]
    first[...] = jnp.concatenate([row[:HALO] for row in rows], axis=0).astype(BF16)
    last[...] = jnp.concatenate([row[-HALO:] for row in rows], axis=0).astype(BF16)


def run_own_columns(tokens):
    return pl.pallas_call(
        own_columns,
        out_shape=[jax.ShapeDtypeStruct((ROWS * HALO, D0), BF16)] * 2,
        in_specs=[whole()],
        out_specs=[whole()] * 2,
        compiler_params=vmem_params(8),
        name="own_columns",
    )(in_hbm(tokens.reshape(-1, D0)))


def column_strips(own_first, own_last, above, below, first, last):
    upper, lower = [part[:TOKEN_ROWS].astype(F32) for part in (above, below)]
    upper, lower = [
        [part[COLS * i : COLS * (i + 1)] for i in range(HALO)] for part in (upper, lower)
    ]
    for out, own, at in (
        (first, own_first, slice(0, HALO)),
        (last, own_last, slice(COLS - HALO, COLS)),
    ):
        rows = HALO * HALO
        out[:rows] = jnp.concatenate([row[at] for row in upper], axis=0).astype(BF16)
        out[rows:-rows] = own[...]
        out[-rows:] = jnp.concatenate([row[at] for row in lower], axis=0).astype(BF16)


def run_column_strips(own_first, own_last, above, below):
    return pl.pallas_call(
        column_strips,
        out_shape=[jax.ShapeDtypeStruct((R8 * HALO, D0), BF16)] * 2,
        in_specs=[whole()] * 4,
        out_specs=[whole()] * 2,
        compiler_params=vmem_params(8),
        name="column_strips",
    )(own_first, own_last, above, below)


def grads_of(own_fine, own_coarse, above, below):
    at = TOKEN_ROWS + FINE_ROWS
    fine = []
    coarse = []
    for outer in (above, below):
        outer_fine = outer[TOKEN_ROWS:at].astype(F32)
        outer_coarse = outer[at:].astype(F32)
        fine.append([outer_fine[COLS * i : COLS * (i + 1)] for i in range(4)])
        coarse.append([outer_coarse[CCOLS * g : CCOLS * (g + 1)] for g in range(4)])
    wide = own_fine[...].astype(F32)
    flat = own_coarse[...].astype(F32)
    fine_rows = fine[0] + [wide[COLS * i : COLS * (i + 1)] for i in range(ROWS)] + fine[1]
    own = [
        [flat[CCOLS * i : CCOLS * (i + 1), D0 * g : D0 * (g + 1)] for g in range(4)]
        for i in range(CROWS)
    ]
    return fine_rows, [coarse[0]] + own + [coarse[1]]


def grad_strips(own_fine, own_coarse, above, below, first, last):
    fine, coarse = grads_of(own_fine, own_coarse, above, below)
    left = [row[:4] for row in fine] + [piece[:1] for row in coarse for piece in row]
    right = [row[-4:] for row in fine] + [piece[-1:] for row in coarse for piece in row]
    first[...] = jnp.concatenate(left, axis=0).astype(BF16)
    last[...] = jnp.concatenate(right, axis=0).astype(BF16)


def run_grad_strips(own_fine, own_coarse, above, below):
    return pl.pallas_call(
        grad_strips,
        out_shape=[jax.ShapeDtypeStruct((R4 * 4 + EXT // 2, D0), BF16)] * 2,
        in_specs=[whole()] * 4,
        out_specs=[whole()] * 2,
        compiler_params=vmem_params(8),
        name="grad_strips",
    )(own_fine, own_coarse, above, below)


def on_device(
    tokens,
    grad_fine,
    grad_coarse,
    fine_gain,
    fine_qkv,
    fine_out,
    merge_weight,
    coarse_gain,
    coarse_qkv,
    coarse_out,
):
    row = lax.axis_index("row")
    col = lax.axis_index("col")
    place = jnp.stack([row * ROWS, col * COLS, row]).astype(jnp.int32)
    first, last, grad_coarse = run_row_strips(tokens, grad_fine, grad_coarse)
    above, below = swap_edges(first, last, "row")
    columns = run_own_columns(tokens)
    left, right = swap_edges(*run_column_strips(*columns, above, below), "col")
    pieces = (tokens, above, below, left, right)
    grad_heads = jnp.dot(grad_coarse, coarse_out.T, preferred_element_type=F32).astype(BF16)
    packed = run_near(
        place,
        pieces,
        fine_gain,
        fine_qkv,
        fine_out,
        merge_weight,
        coarse_gain,
        coarse_qkv,
        grad_heads,
    )
    packed, grad_fine, grad_coarse, *pieces = lax.optimization_barrier(
        (packed, grad_fine, grad_coarse, *pieces)
    )
    every = lax.all_to_all(
        packed.reshape(8 * H1, CROWS * CCOLS, 256),
        ("row", "col"),
        split_axis=0,
        concat_axis=0,
        tiled=True,
    )
    grads = (grad_fine.reshape(-1, D0), grad_coarse, pieces[1], pieces[2])
    left, right = swap_edges(*run_grad_strips(*grads), "col")
    stash, lse, coarse = run_wide(place, pieces, fine_gain, fine_qkv, fine_out, merge_weight)
    every, left, right, stash, lse, coarse = lax.optimization_barrier(
        (every, left, right, stash, lse, coarse)
    )
    every = every.reshape(SLAB * SLABS, 256)
    edges = jnp.asarray(strip_pick(), BF16)
    own_stats = run_coarse_forward(place, every)
    stats = lax.all_to_all(own_stats, "row", split_axis=0, concat_axis=0, tiled=True)
    edge, dq_own = run_coarse_own(place, every, own_stats, edges)
    pick = jnp.asarray(block_pick(), BF16)
    tiles, near_coarse, stash, near_merge, pick = run_coarse_backward(
        place, every, stats, edges, edge, dq_own, coarse_qkv, stash, merge_weight, pick
    )
    tiles = tiles.reshape(H1, EXT, 256)
    terms = lax.all_to_all(tiles, "col", split_axis=0, concat_axis=0, tiled=True)
    grad_tokens, blocks = run_backward(
        place,
        terms,
        *grads,
        left,
        right,
        coarse,
        lse,
        coarse_gain.reshape(1, D1),
        fine_gain.reshape(1, D0),
        fine_qkv,
        fine_out,
        near_coarse,
        stash,
        pick,
        near_merge,
    )
    blocks = lax.all_to_all(blocks, ("row", "col"), split_axis=0, concat_axis=0, tiled=True)
    grad_qkv, grad_out = run_sum_terms(blocks)
    return grad_tokens.reshape(ROWS, COLS, D0), grad_qkv, grad_out.T


def solution(mesh):
    return jax.shard_map(
        on_device,
        mesh=mesh,
        in_specs=(P("row", "col", None),) * 3 + (P(),) * 7,
        out_specs=(P("row", "col", None), P("row", "col"), P("row", "col")),
        check_vma=False,
    )
```

```python
import jax
import jax.numpy as jnp
import numpy as np
from jax import lax
from jax.experimental import pallas as pl
from jax.experimental.pallas import tpu as pltpu
from jax.sharding import PartitionSpec as P

H0 = 4
H1 = 16
HEAD = 64
MERGE = 4
EPSILON = 1e-05
FAR = 1e30
D0 = 256
D1 = 1024

ROWS, COLS = 16, 24
CROWS, CCOLS = 4, 6
R8, C8 = ROWS + 16, COLS + 16
R4, C4 = ROWS + 8, COLS + 8
N4 = R4 * C4
BLOCK = 4 * C4
BLOCKS = R4 // 4
WROWS = R4 + 6
OWN = ROWS * C4
EXT = (CROWS + 2) * (CCOLS + 2)

F32 = jnp.float32
BF16 = jnp.bfloat16


def vmem_params(mib):
    return pltpu.CompilerParams(vmem_limit_bytes=mib * 1024 * 1024)


def whole():
    return pl.BlockSpec(memory_space=pltpu.VMEM)


def far():
    return pl.BlockSpec(memory_space=pltpu.HBM)


def fetch(source, target, sems, pieces):
    rows = source.shape[0] // pieces
    return [
        pltpu.make_async_copy(
            source.at[pl.ds(n * rows, rows)], target.at[pl.ds(n * rows, rows)], sems.at[n]
        )
        for n in range(pieces)
    ]


def dot(a, b, ca, cb):
    return lax.dot_general(a, b, (((ca,), (cb,)), ((), ())), preferred_element_type=F32)


def norm_forward(values):
    center = values - jnp.mean(values, axis=-1, keepdims=True)
    inverse = lax.rsqrt(jnp.mean(center * center, axis=-1, keepdims=True) + EPSILON)
    return center * inverse, inverse


def norm_backward(scaled, normed, inverse):
    return inverse * (
        scaled
        - jnp.mean(scaled, axis=-1, keepdims=True)
        - normed * jnp.mean(scaled * normed, axis=-1, keepdims=True)
    )


def head_lanes(rows):
    return lax.broadcasted_iota(jnp.int32, (rows, D0), 1) // HEAD


def stack_heads(values):
    lanes = head_lanes(values.shape[0])
    zero = jnp.zeros_like(values)
    return jnp.concatenate([jnp.where(lanes == h, values, zero) for h in range(H0)], axis=0)


def unstack_heads(stacked):
    rows = stacked.shape[0] // H0
    lanes = head_lanes(rows)
    result = stacked[:rows]
    for h in range(1, H0):
        result = jnp.where(lanes == h, stacked[h * rows : (h + 1) * rows], result)
    return result


AT_Q = 0
AT_ATT = N4
AT_K = 2 * N4
AT_V = AT_K + WROWS * C4
AT_X = AT_V + WROWS * C4
STASH = AT_X + OWN


def window_bias(key_cols, col_shift):
    shape = (10, key_cols, BLOCK)
    kr = lax.broadcasted_iota(jnp.int32, shape, 0)
    kc = lax.broadcasted_iota(jnp.int32, shape, 1)
    lane = lax.broadcasted_iota(jnp.int32, shape, 2)
    row_gap = kr - lane // C4
    col_gap = kc - lane % C4 - col_shift
    near = (row_gap >= 0) & (row_gap <= 6) & (col_gap >= 0) & (col_gap <= 6)
    return jnp.where(near, 0.0, -FAR).reshape(10 * key_cols, BLOCK)


def key_bias(key_cols, key_row, key_col):
    shape = (10, key_cols, 1)
    grid_row = key_row + lax.broadcasted_iota(jnp.int32, shape, 0)
    grid_col = key_col + lax.broadcasted_iota(jnp.int32, shape, 1)
    inside = (grid_row >= 0) & (grid_row < 128) & (grid_col >= 0) & (grid_col < 384)
    return jnp.where(inside, 0.0, -FAR).reshape(10 * key_cols, 1)


def all_heads(bias):
    return jnp.concatenate([bias] * H0, axis=1)


def near_kernel(
    place,
    tokens,
    above,
    below,
    left,
    right,
    gain,
    w_qkv,
    w_out,
    w_merge_far,
    gain_coarse,
    w_coarse_far,
    grads,
    packed_far,
    x32,
    keys,
    values,
    hid32,
    merged,
    w_merge,
    w_coarse,
    packed,
    merge_sems,
    coarse_sems,
    packed_sems,
):
    merge_copies = fetch(w_merge_far, w_merge, merge_sems, 2)
    coarse_copies = fetch(w_coarse_far, w_coarse, coarse_sems, 4)
    for copy in merge_copies + coarse_copies:
        copy.start()
    row0 = place[0]
    col0 = place[1]
    middle = [part[: 8 * COLS].astype(F32) for part in (above, below)]
    middle.insert(1, tokens[...].astype(F32))
    sides = [left[...].astype(F32), right[...].astype(F32)]
    for t in range(ROWS + 6):
        e = t + 5
        part, at = (0, e) if e < 8 else (1, e - 8) if e < 8 + ROWS else (2, e - 8 - ROWS)
        x32[C4 * t : C4 * (t + 1)] = jnp.concatenate(
            [
                sides[0][8 * e + 4 : 8 * e + 8],
                middle[part][COLS * at : COLS * (at + 1)],
                sides[1][8 * e : 8 * e + 4],
            ],
            axis=0,
        )
    normed, _ = norm_forward(x32[...])
    normed = (normed * gain[...]).astype(BF16)
    inner = slice(3 * C4, 3 * C4 + OWN)
    queries = dot(normed[inner], w_qkv[:, :D0], 1, 0).astype(BF16).astype(F32) * (HEAD**-0.5)
    keys[...] = dot(normed, w_qkv[:, D0 : 2 * D0], 1, 0).astype(BF16)
    values[...] = dot(normed, w_qkv[:, 2 * D0 :], 1, 0).astype(BF16)
    window = window_bias(C4, -3)
    for b in range(ROWS // 4):
        block = slice(BLOCK * b, BLOCK * b + 10 * C4)
        stacked = stack_heads(queries[BLOCK * b : BLOCK * (b + 1)]).astype(BF16)
        bias = all_heads(window + key_bias(C4, row0 - 3 + 4 * b, col0 - 4))
        scores = dot(keys[block], stacked, 1, 1) + bias
        maxima = jnp.max(scores, axis=0, keepdims=True)
        exponent = jnp.exp(scores - maxima)
        totals = jnp.sum(exponent, axis=0, keepdims=True)
        weights = (exponent * (1.0 / totals)).astype(BF16)
        attended = unstack_heads(dot(weights, values[block], 0, 0)).astype(BF16)
        at = BLOCK * b
        own = x32[3 * C4 + at : 3 * C4 + at + BLOCK]
        total = (own + dot(attended, w_out[...], 1, 0)).astype(BF16).astype(F32)
        hid32[0, at : at + BLOCK] = total[:, :128]
        hid32[1, at : at + BLOCK] = total[:, 128:]
    wide = CCOLS + 2
    merge_rows(hid32, merged, CROWS)
    total = None
    for n in range(4):
        if n % 2 == 0:
            merge_copies[n // 2].wait()
        part = dot(merged[:, D1 * n : D1 * (n + 1)], w_merge[D1 * n : D1 * (n + 1)], 1, 0)
        total = part if total is None else total + part
    normed, _ = norm_forward(total.astype(BF16).astype(F32))
    normed = normed * gain_coarse[...]
    parts = [normed[wide * i + 1 : wide * i + 1 + CCOLS] for i in range(CROWS)]
    normed = jnp.concatenate(parts, axis=0).astype(BF16)
    for copy in coarse_copies:
        copy.wait()
    packed_copies = []
    for n in range(4):
        result = dot(normed, w_coarse[:, 768 * n : 768 * (n + 1)], 1, 0)
        grad = grads[:, 256 * n : 256 * (n + 1)].astype(F32)
        parts = []
        for h in range(4):
            q = result[:, 192 * h : 192 * h + 64]
            k = result[:, 192 * h + 64 : 192 * h + 128]
            v = result[:, 192 * h + 128 : 192 * h + 192]
            g = grad[:, 64 * h : 64 * h + 64]
            parts.append(jnp.concatenate([k, v, q, g], axis=1))
        packed[2 * n] = jnp.concatenate(parts[:2], axis=0).astype(BF16)
        packed[2 * n + 1] = jnp.concatenate(parts[2:], axis=0).astype(BF16)
        at = pl.ds(2 * n, 2)
        for r in range(8):
            packed_copies.append(
                pltpu.make_async_copy(packed.at[at], packed_far.at[r, at], packed_sems.at[n, r])
            )
            packed_copies[-1].start()
    for copy in packed_copies:
        copy.wait()


def merge_rows(hid32, merged, count):
    for pair in range(count // 2):
        for a in range(MERGE):
            for c in range(MERGE):
                for half in range(2):
                    parts = [
                        hid32[half, pl.ds((4 * i + a) * C4 + c, CCOLS + 2, stride=MERGE), :]
                        for i in (2 * pair, 2 * pair + 1)
                    ]
                    at = (a * MERGE + c) * D0 + half * 128
                    merged[16 * pair : 16 * (pair + 1), at : at + 128] = jnp.concatenate(
                        parts, axis=0
                    ).astype(BF16)


def run_near(place, pieces, gain, w_qkv, w_out, w_merge, gain_coarse, w_coarse, grads):
    own = CROWS * CCOLS
    return pl.pallas_call(
        near_kernel,
        out_shape=pltpu.HBM((8, 8, 2 * own, 256), BF16),
        in_specs=[pl.BlockSpec(memory_space=pltpu.SMEM)]
        + [whole()] * 8
        + [far(), whole(), far(), whole()],
        out_specs=far(),
        scratch_shapes=[
            pltpu.VMEM(((ROWS + 6) * C4, D0), F32),
            pltpu.VMEM(((ROWS + 6) * C4, D0), BF16),
            pltpu.VMEM(((ROWS + 6) * C4, D0), BF16),
            pltpu.VMEM((2, OWN, 128), F32),
            pltpu.VMEM((CROWS * (CCOLS + 2), MERGE * MERGE * D0), BF16),
            pltpu.VMEM(w_merge.shape, BF16),
            pltpu.VMEM(w_coarse.shape, BF16),
            pltpu.VMEM((8, 2 * own, 256), BF16),
            pltpu.SemaphoreType.DMA((2,)),
            pltpu.SemaphoreType.DMA((4,)),
            pltpu.SemaphoreType.DMA((4, 8)),
        ],
        compiler_params=vmem_params(48),
        cost_estimate=pl.CostEstimate(flops=3 * 10**9, bytes_accessed=2 * 10**7, transcendentals=10**6),
        name="near_kernel",
    )(
        place,
        *[piece.reshape(-1, D0) for piece in pieces],
        gain.reshape(1, D0),
        w_qkv,
        w_out,
        in_hbm(w_merge),
        gain_coarse.reshape(1, D1),
        in_hbm(w_coarse),
        grads,
    )


def in_hbm(array):
    return pltpu.with_memory_space_constraint(array, pltpu.HBM)


def wide_kernel(
    place,
    tokens,
    above,
    below,
    left,
    right,
    gain,
    w_qkv,
    w_out,
    w_merge_far,
    stash_far,
    lse,
    coarse_out,
    x32,
    q32,
    k32,
    v32,
    hid32,
    stash,
    merged,
    w_merge,
    merge_sems,
    stash_sem,
):
    merge_copies = fetch(w_merge_far, w_merge, merge_sems, 4)
    for copy in merge_copies:
        copy.start()
    queries = stash.at[pl.ds(AT_Q, N4)]
    attended = stash.at[pl.ds(AT_ATT, N4)]
    keys_w = stash.at[pl.ds(AT_K, WROWS * C4)]
    values_w = stash.at[pl.ds(AT_V, WROWS * C4)]
    tokens_own = stash.at[pl.ds(AT_X, OWN)]
    row0 = place[0]
    col0 = place[1]
    middle = [part[: 8 * COLS].astype(F32) for part in (above, below)]
    middle.insert(1, tokens[...].astype(F32))
    sides = [left[...].astype(F32), right[...].astype(F32)]
    for i in range(R8):
        part, at = (0, i) if i < 8 else (1, i - 8) if i < 8 + ROWS else (2, i - 8 - ROWS)
        x32[C8 * i : C8 * i + 8] = sides[0][8 * i : 8 * i + 8]
        x32[C8 * i + 8 : C8 * i + 8 + COLS] = middle[part][COLS * at : COLS * (at + 1)]
        x32[C8 * i + 8 + COLS : C8 * (i + 1)] = sides[1][8 * i : 8 * i + 8]
    normed, _ = norm_forward(x32[...])
    normed = (normed * gain[...]).astype(BF16)
    q32[...] = dot(normed, w_qkv[:, :D0], 1, 0).astype(BF16).astype(F32) * (HEAD**-0.5)
    k32[...] = dot(normed, w_qkv[:, D0 : 2 * D0], 1, 0).astype(BF16).astype(F32)
    v32[...] = dot(normed, w_qkv[:, 2 * D0 :], 1, 0).astype(BF16).astype(F32)
    for i in range(R4):
        queries[C4 * i : C4 * (i + 1)] = q32[pl.ds((i + 4) * C8 + 4, C4), :].astype(BF16)
    for i in range(WROWS):
        keys_w[C4 * i : C4 * (i + 1)] = k32[pl.ds((i + 1) * C8 + 4, C4), :].astype(BF16)
        values_w[C4 * i : C4 * (i + 1)] = v32[pl.ds((i + 1) * C8 + 4, C4), :].astype(BF16)
    for i in range(ROWS):
        tokens_own[C4 * i : C4 * (i + 1)] = x32[pl.ds((i + 8) * C8 + 4, C4), :].astype(BF16)
    lse[...] = jnp.full(lse.shape, FAR, F32)
    window = window_bias(C8, 1)
    for b in range(BLOCKS):
        start = (4 * b + 1) * C8
        key_block = k32[start : start + 10 * C8].astype(BF16)
        value_block = v32[start : start + 10 * C8].astype(BF16)
        stacked = stack_heads(queries[BLOCK * b : BLOCK * (b + 1)].astype(F32)).astype(BF16)
        bias = all_heads(window + key_bias(C8, row0 - 7 + 4 * b, col0 - 8))
        scores = dot(key_block, stacked, 1, 1) + bias
        maxima = jnp.max(scores, axis=0, keepdims=True)
        exponent = jnp.exp(scores - maxima)
        totals = jnp.sum(exponent, axis=0, keepdims=True)
        weights = (exponent * (1.0 / totals)).astype(BF16)
        result = unstack_heads(dot(weights, value_block, 0, 0)).astype(BF16)
        attended[BLOCK * b : BLOCK * (b + 1)] = result
        lane = lax.broadcasted_iota(jnp.int32, (1, H0 * BLOCK), 1) % BLOCK
        q_row = row0 - 4 + 4 * b + lane // C4
        q_col = col0 - 4 + lane % C4
        q_in = (q_row >= 0) & (q_row < 128) & (q_col >= 0) & (q_col < 384)
        lse[b : b + 1] = jnp.where(q_in, maxima + jnp.log(totals), FAR)
        projected = dot(result, w_out[...], 1, 0)
        for a in range(4):
            own = x32[pl.ds((4 * b + a + 4) * C8 + 4, C4), :]
            total = own + projected[C4 * a : C4 * (a + 1)]
            at = BLOCK * b + C4 * a
            total = total.astype(BF16).astype(F32)
            hid32[0, at : at + C4] = total[:, :128]
            hid32[1, at : at + C4] = total[:, 128:]
    merge_rows(hid32, merged, CROWS + 2)
    stash_copy = pltpu.make_async_copy(stash, stash_far, stash_sem)
    stash_copy.start()
    total = None
    for n, copy in enumerate(merge_copies):
        copy.wait()
        part = dot(merged[:, D1 * n : D1 * (n + 1)], w_merge[D1 * n : D1 * (n + 1)], 1, 0)
        total = part if total is None else total + part
    coarse_out[...] = total.astype(BF16)
    stash_copy.wait()


def run_wide(place, pieces, gain, w_qkv, w_out, w_merge):
    flat = R8 * C8
    return pl.pallas_call(
        wide_kernel,
        out_shape=[
            pltpu.HBM((STASH, D0), BF16),
            pltpu.HBM((8, H0 * BLOCK), F32),
            pltpu.HBM((EXT, D1), BF16),
        ],
        in_specs=[pl.BlockSpec(memory_space=pltpu.SMEM)] + [whole()] * 8 + [far()],
        out_specs=[far(), whole(), whole()],
        scratch_shapes=[pltpu.VMEM((flat, D0), F32)] * 4
        + [
            pltpu.VMEM((2, N4, 128), F32),
            pltpu.VMEM((STASH, D0), BF16),
            pltpu.VMEM((EXT, MERGE * MERGE * D0), BF16),
            pltpu.VMEM(w_merge.shape, BF16),
            pltpu.SemaphoreType.DMA((4,)),
            pltpu.SemaphoreType.DMA(()),
        ],
        compiler_params=vmem_params(40),
        cost_estimate=pl.CostEstimate(flops=3 * 10**9, bytes_accessed=10**7, transcendentals=10**6),
        name="wide_kernel",
    )(
        place,
        *[piece.reshape(-1, D0) for piece in pieces],
        gain.reshape(1, D0),
        w_qkv,
        w_out,
        in_hbm(w_merge),
    )


def lane_half(values, low):
    lanes = lax.broadcasted_iota(jnp.int32, values.shape, 1)
    keep = lanes < HEAD if low else lanes >= HEAD
    return jnp.where(keep, values, jnp.zeros_like(values))


SLAB = 384
SLABS = 8
STRIP = 96
EDGE = SLAB + 2 * STRIP


def strip_pick():
    tile, j = np.divmod(np.arange(STRIP), CCOLS)
    pick = np.zeros((2, STRIP, SLAB), np.float32)
    last = (CROWS - 1) * CCOLS
    pick[0, np.arange(STRIP), tile * CROWS * CCOLS + last + j] = 1
    pick[1, np.arange(STRIP), tile * CROWS * CCOLS + j] = 1
    return pick


def tile_pick():
    c, i, j = np.meshgrid(np.arange(H1), np.arange(6), np.arange(8), indexing="ij")
    tile = (c + (j == 7) - (j == 0)) % H1
    jj = np.where(j == 0, 5, np.where(j == 7, 0, j - 1))
    middle = tile * 24 + (i - 1) * 6 + jj
    source = np.where(i == 0, SLAB + tile * 6 + jj, np.where(i == 5, SLAB + STRIP + tile * 6 + jj, middle))
    pick = np.zeros((H1 * EXT, EDGE), np.float32)
    pick[np.arange(H1 * EXT), source.reshape(-1)] = 1
    return pick


def coarse_forward(place, every, stats, scores_ref):
    keyval = every[:, :128]
    own = every[pl.ds(pl.multiple_of(place[2] * SLAB, SLAB), SLAB), 128:]
    queries = lane_half(own.astype(F32) * (HEAD**-0.5), True).astype(BF16)
    columns = []
    for b in range(3):
        rows = slice(128 * b, 128 * (b + 1))
        scores_ref[b] = dot(queries[rows], keyval, 1, 1)
        maxima = jnp.max(scores_ref[b], axis=1, keepdims=True)
        exponent = jnp.exp(scores_ref[b] - maxima)
        totals = jnp.sum(exponent, axis=1, keepdims=True)
        weights = (exponent * (1.0 / totals)).astype(BF16)
        attended = dot(weights, keyval, 1, 0).astype(BF16).astype(F32)
        product = lane_half(own[rows].astype(F32) * attended, False)
        columns.append((maxima + jnp.log(totals), jnp.sum(product, axis=1, keepdims=True)))
    lane = lax.broadcasted_iota(jnp.int32, (128, 128), 1)
    turned = [
        jnp.where(lane == 0, log, jnp.where(lane == 1, stat, 0.0)).T for log, stat in columns
    ]
    result = jnp.concatenate(
        [t[0:1] for t in turned] + [t[1:2] for t in turned] + [jnp.zeros((2, 128), F32)], axis=0
    )
    for r in range(SLABS):
        stats[r] = result


def run_coarse_forward(place, every):
    return pl.pallas_call(
        coarse_forward,
        out_shape=jax.ShapeDtypeStruct((SLABS, 8, 128), F32),
        in_specs=[pl.BlockSpec(memory_space=pltpu.SMEM), whole()],
        out_specs=whole(),
        scratch_shapes=[pltpu.VMEM((3, 128, SLAB * SLABS), F32)],
        compiler_params=vmem_params(16),
        cost_estimate=pl.CostEstimate(flops=10**9, bytes_accessed=2 * 10**6, transcendentals=10**6),
        name="coarse_forward",
    )(place, every)


def stat_rows(stats):
    lse = jnp.concatenate([stats[k : k + 1] for k in range(3)], axis=1)
    stat = jnp.concatenate([stats[k : k + 1] for k in range(3, 6)], axis=1)
    return lse, stat


def slab_rows(index):
    return pl.ds(pl.multiple_of(index * SLAB, SLAB), SLAB)


def turn(lse, stat):
    filler = jnp.zeros((128 - 2, lse.shape[1]), F32)
    turned = jnp.concatenate([lse, stat, filler], axis=0).T
    return turned[:, 0:1], turned[:, 1:2]


def query_side(every, rows, queries, grads, lse, stat):
    keyval = every[rows, :128]
    probs = jnp.exp(dot(queries, keyval, 1, 1) - lse)
    slopes = (probs * (dot(grads, keyval, 1, 1) - stat)).astype(BF16)
    return dot(slopes, keyval, 1, 0)


def halves(pair):
    wide = pair.astype(F32)
    return lane_half(wide * (HEAD**-0.5), True).astype(BF16), lane_half(wide, False).astype(BF16)


def coarse_own(place, every, stats, strips, edge, dq_out, dq_ref):
    row = place[2]
    edge[:SLAB] = every[slab_rows(row)]
    others = (lax.rem(row + SLABS - 1, SLABS), lax.rem(row + 1, SLABS))
    for k, other in enumerate(others):
        at = SLAB + STRIP * k
        edge[at : at + STRIP] = dot(strips[k], every[slab_rows(other)], 1, 0).astype(BF16)
    lse, stat = turn(*stat_rows(stats[0]))
    queries, grads = halves(edge[:SLAB, 128:])
    for n in range(SLABS // 2):
        rows = slice(2 * n * SLAB, 2 * (n + 1) * SLAB)
        term = query_side(every, rows, queries, grads, lse, stat)
        dq_ref[...] = term if n == 0 else dq_ref[...] + term
    dq_out[...] = (dq_ref[...] * (HEAD**-0.5)).astype(BF16)


def run_coarse_own(place, every, stats, strips):
    return pl.pallas_call(
        coarse_own,
        out_shape=[
            pltpu.HBM((EDGE, 256), BF16),
            pltpu.HBM((SLAB, 128), BF16),
        ],
        in_specs=[pl.BlockSpec(memory_space=pltpu.SMEM)] + [whole()] * 3,
        out_specs=[whole()] * 2,
        scratch_shapes=[pltpu.VMEM((SLAB, 128), F32)],
        compiler_params=vmem_params(24),
        cost_estimate=pl.CostEstimate(flops=10**9, bytes_accessed=2 * 10**6, transcendentals=10**6),
        name="coarse_own",
    )(place, every, stats, strips)


def coarse_backward(
    place,
    every,
    stats,
    strips,
    edge,
    dq_own,
    tiles_far,
    coarse_far,
    stash_far,
    merge_far,
    pick_far,
    out,
    w_coarse,
    stash,
    w_merge,
    pick,
    dq_ref,
    dk_ref,
    dv_ref,
    tiles,
    sems,
):
    pairs = (
        (tiles_far, tiles, 1),
        (coarse_far, w_coarse, 2),
        (stash_far, stash, 1),
        (merge_far, w_merge, 2),
        (pick_far, pick, 1),
    )
    copies = []
    for n, (source, target, pieces) in enumerate(pairs):
        copies += fetch(source, target, sems.at[n], pieces)
    for copy in copies:
        copy.start()
    row = place[2]
    others = (lax.rem(row + SLABS - 1, SLABS), lax.rem(row + 1, SLABS))
    taken = []
    for k, other in enumerate(others):
        both = jnp.concatenate(stat_rows(stats[other]) + (jnp.zeros((6, SLAB), F32),), axis=0)
        taken.append(
            lax.dot_general(
                both,
                strips[k].astype(F32),
                (((1,), (1,)), ((), ())),
                precision=lax.Precision.HIGHEST,
                preferred_element_type=F32,
            )
        )
    strip_lse, strip_stat = turn(
        jnp.concatenate([t[0:1] for t in taken], axis=1),
        jnp.concatenate([t[1:2] for t in taken], axis=1),
    )
    edge_k, edge_v = halves(edge[:, :128])
    edge_q, edge_g = halves(edge[SLAB:, 128:])
    for n in range(SLABS // 2):
        rows = slice(2 * n * SLAB, 2 * (n + 1) * SLAB)
        dq = query_side(every, rows, edge_q, edge_g, strip_lse, strip_stat)
        query = every[rows, 128:]
        both = [stat_rows(stats[2 * n + k]) for k in range(2)]
        lse = jnp.concatenate([pair[0] for pair in both], axis=1)
        stat = jnp.concatenate([pair[1] for pair in both], axis=1)
        probs = jnp.exp(dot(edge_k, query, 1, 1) - lse)
        slopes = (probs * (dot(edge_v, query, 1, 1) - stat)).astype(BF16)
        dk = dot(slopes, query, 1, 0)
        dv = dot(probs.astype(BF16), query, 1, 0)
        if n == 0:
            dq_ref[...] = dq
            dk_ref[...] = dk
            dv_ref[...] = dv
        else:
            dq_ref[...] += dq
            dk_ref[...] += dk
            dv_ref[...] += dv
    lanes = lax.broadcasted_iota(jnp.int32, (EDGE, 128), 1)
    keyval = jnp.where(lanes < HEAD, dk_ref[...] * (HEAD**-0.5), dv_ref[...]).astype(BF16)
    query = jnp.concatenate(
        [dq_own[...], (dq_ref[...] * (HEAD**-0.5)).astype(BF16)], axis=0
    )
    copies[0].wait()
    out[...] = dot(tiles[...], jnp.concatenate([keyval, query], axis=1), 1, 0).astype(BF16)
    for copy in copies[1:]:
        copy.wait()


def run_coarse_backward(place, every, stats, strips, edge, dq_own, *later):
    tiles = jnp.asarray(tile_pick(), BF16)
    return pl.pallas_call(
        coarse_backward,
        out_shape=[pltpu.HBM((H1 * EXT, 256), BF16)]
        + [pltpu.VMEM(array.shape, array.dtype) for array in later],
        in_specs=[pl.BlockSpec(memory_space=pltpu.SMEM)] + [whole()] * 5 + [far()] * 5,
        out_specs=[whole()] * 5,
        scratch_shapes=[
            pltpu.VMEM((2 * STRIP, 128), F32),
            pltpu.VMEM((EDGE, 128), F32),
            pltpu.VMEM((EDGE, 128), F32),
            pltpu.VMEM(tiles.shape, BF16),
            pltpu.SemaphoreType.DMA((5, 4)),
        ],
        compiler_params=vmem_params(16),
        cost_estimate=pl.CostEstimate(flops=3 * 10**9, bytes_accessed=2 * 10**6, transcendentals=4 * 10**6),
        name="coarse_backward",
    )(
        place,
        every,
        stats,
        strips,
        in_hbm(edge),
        in_hbm(dq_own),
        *[in_hbm(array) for array in (tiles,) + later],
    )


def block_pick():
    c, b = np.meshgrid(np.arange(H1), np.arange(64), indexing="ij")
    source = np.where(b < 48, 48 * c + b, 3 * D0 + 16 * c + b - 48).reshape(-1)
    pick = np.zeros((4 * D0, 4 * D0), np.float32)
    pick[source, np.arange(4 * D0)] = 1
    return pick


def merged_order(back):
    rows = lax.broadcasted_iota(jnp.int32, (BLOCK, BLOCK), 0)
    cols = lax.broadcasted_iota(jnp.int32, (BLOCK, BLOCK), 1)
    merged, grid = (cols, rows) if back else (rows, cols)
    a = merged // C4
    c = merged // 8 % MERGE
    j = merged % 8
    return (grid == a * C4 + j * MERGE + c).astype(F32).astype(BF16)


def backward_kernel(
    place,
    terms_coarse,
    own_fine,
    own_coarse,
    above,
    below,
    grads_left,
    grads_right,
    coarse,
    lse,
    gain_coarse,
    gain,
    w_qkv,
    w_out,
    w_coarse,
    stash,
    pick_block,
    w_merge,
    grad_tokens,
    terms,
    grad_fine,
    sp32,
    gh_ref,
    ga_ref,
    dq_ref,
    dk_ref,
    dv_ref,
    gt_ref,
    stack_ref,
    probs_ref,
):
    queries = stash.at[pl.ds(AT_Q, N4)]
    attended = stash.at[pl.ds(AT_ATT, N4)]
    keys_w = stash.at[pl.ds(AT_K, WROWS * C4)]
    values_w = stash.at[pl.ds(AT_V, WROWS * C4)]
    tokens_own = stash.at[pl.ds(AT_X, OWN)]
    row0 = place[0]
    col0 = place[1]
    wide = CCOLS + 2
    fine_rows, coarse_rows = grads_of(own_fine, own_coarse, above, below)
    side = [part[...].astype(F32) for part in (grads_left, grads_right)]
    for i, row in enumerate(fine_rows):
        outer = [part[4 * i : 4 * (i + 1)] for part in side]
        grad_fine[C4 * i : C4 * (i + 1)] = jnp.concatenate([outer[0], row, outer[1]], axis=0)
    grad_coarse = []
    for i, row in enumerate(coarse_rows):
        parts = []
        for g, piece in enumerate(row):
            at = 4 * R4 + 4 * i + g
            outer = [part[at : at + 1] for part in side]
            parts.append(jnp.concatenate([outer[0], piece, outer[1]], axis=0))
        grad_coarse.append(jnp.concatenate(parts, axis=1))
    grad_coarse = jnp.concatenate(grad_coarse, axis=0)
    parts = []
    for h in range(H1):
        block = terms_coarse[h].astype(F32)
        parts += [block[:, 128:192], block[:, :128]]
    heads = jnp.concatenate(parts, axis=1).astype(BF16)
    upstream = dot(heads, w_coarse[...], 1, 1) * gain_coarse[...]
    normed, inverse = norm_forward(coarse[...].astype(F32))
    back = norm_backward(upstream, normed, inverse)
    change = (grad_coarse + back).astype(BF16)
    for a in range(MERGE):
        sp32[a] = dot(change, w_merge[D1 * a : D1 * (a + 1)], 1, 1)
    window = window_bias(C4, -3)
    for b in range(BLOCKS):
        stacked = stack_heads(queries[BLOCK * b : BLOCK * (b + 1)].astype(F32)).astype(BF16)
        stack_ref[b] = stacked
        bias = all_heads(window + key_bias(C4, row0 - 7 + 4 * b, col0 - 4))
        scores = dot(keys_w[BLOCK * b : BLOCK * b + 10 * C4], stacked, 1, 1) + bias
        probs_ref[b] = jnp.exp(scores - lse[b : b + 1])
    to_merged = merged_order(False)
    to_grid = merged_order(True)
    for i in range(CROWS + 2):
        block = slice(BLOCK * i, BLOCK * (i + 1))
        rows = slice(wide * i, wide * (i + 1))
        spread = [
            sp32[a, rows, D0 * c : D0 * (c + 1)] for a in range(MERGE) for c in range(MERGE)
        ]
        total = dot(to_merged, grad_fine[block].astype(BF16), 1, 0) + jnp.concatenate(spread, axis=0)
        gh_ref[block] = dot(to_grid, total.astype(BF16), 1, 0).astype(BF16)
    ga_ref[...] = dot(gh_ref[...], w_out[...], 1, 1).astype(BF16)
    dk_ref[...] = jnp.zeros_like(dk_ref)
    dv_ref[...] = jnp.zeros_like(dv_ref)
    pick = (
        lax.broadcasted_iota(jnp.int32, (8, D0), 1) // HEAD
        == lax.broadcasted_iota(jnp.int32, (8, D0), 0)
    ).astype(F32).astype(BF16)
    for b in range(BLOCKS):
        at = slice(BLOCK * b, BLOCK * (b + 1))
        keep = slice(BLOCK * b, BLOCK * b + 10 * C4)
        grad = ga_ref[at].astype(F32)
        product = grad * attended[at].astype(F32)
        upper = product.astype(BF16)
        lower = (product - upper.astype(F32)).astype(BF16)
        sums = dot(pick, upper, 1, 1) + dot(pick, lower, 1, 1)
        stat = jnp.concatenate([sums[h : h + 1] for h in range(H0)], axis=1)
        stack_q = stack_ref[b]
        stack_g = stack_heads(grad).astype(BF16)
        key_block = keys_w[keep]
        probs = probs_ref[b]
        slopes = (probs * (dot(values_w[keep], stack_g, 1, 1) - stat)).astype(BF16)
        dk_ref[keep] += dot(slopes, stack_q, 1, 0)
        dv_ref[keep] += dot(probs.astype(BF16), stack_g, 1, 0)
        if 1 <= b <= 4:
            dq = unstack_heads(dot(slopes, key_block, 0, 0)) * (HEAD**-0.5)
            dq_ref[BLOCK * (b - 1) : BLOCK * b] = dq.astype(BF16)
    own = slice(7 * C4, 7 * C4 + OWN)
    grads = jnp.concatenate(
        [dq_ref[...], dk_ref[own].astype(BF16), dv_ref[own].astype(BF16)], axis=1
    )
    column = lax.broadcasted_iota(jnp.int32, (ROWS, C4, D0), 1).reshape(OWN, D0)
    in_tile = (column >= 4) & (column < 4 + COLS)
    normed, inverse = norm_forward(tokens_own[...].astype(F32))
    rounded = jnp.where(in_tile, normed * gain[...], 0.0).astype(BF16)
    term_qkv = dot(rounded, grads, 0, 0).astype(BF16)
    inner = slice(BLOCK, BLOCK + OWN)
    att = jnp.where(in_tile, attended[inner].astype(F32), 0.0).astype(BF16)
    term_out = dot(att, gh_ref[inner], 0, 0).astype(BF16)
    both = dot(jnp.concatenate([term_qkv, term_out], axis=1), pick_block[...], 1, 0)
    low = lax.broadcasted_iota(jnp.int32, (16, 128), 1) < 64
    for r in range(8):
        for m in range(8):
            first = both[32 * r : 32 * r + 16, 128 * m : 128 * (m + 1)]
            last = both[32 * r + 16 : 32 * (r + 1), 128 * m : 128 * (m + 1)]
            terms[16 * r + 2 * m] = jnp.where(low, first, pltpu.roll(last, 64, 1)).astype(BF16)
            terms[16 * r + 2 * m + 1] = jnp.where(low, pltpu.roll(first, 64, 1), last).astype(BF16)
    upstream = dot(grads, w_qkv[...], 1, 1) * gain[...]
    gt_ref[...] = gh_ref[inner].astype(F32) + norm_backward(upstream, normed, inverse)
    for pair in range(ROWS // 2):
        parts = [gt_ref[pl.ds(i * C4 + 4, COLS), :] for i in (2 * pair, 2 * pair + 1)]
        grad_tokens[2 * COLS * pair : 2 * COLS * (pair + 1)] = jnp.concatenate(
            parts, axis=0
        ).astype(BF16)


def run_backward(place, *operands):
    shapes = [((ROWS * COLS, D0), BF16), ((128, 16, 128), BF16)]
    return pl.pallas_call(
        backward_kernel,
        out_shape=[jax.ShapeDtypeStruct(s, d) for s, d in shapes],
        in_specs=[pl.BlockSpec(memory_space=pltpu.SMEM)] + [whole()] * 17,
        out_specs=[whole()] * 2,
        scratch_shapes=[
            pltpu.VMEM((N4, D0), F32),
            pltpu.VMEM((MERGE, EXT, D1), F32),
            pltpu.VMEM((N4, D0), BF16),
            pltpu.VMEM((N4, D0), BF16),
            pltpu.VMEM((OWN, D0), BF16),
            pltpu.VMEM((WROWS * C4, D0), F32),
            pltpu.VMEM((WROWS * C4, D0), F32),
            pltpu.VMEM((OWN, D0), F32),
            pltpu.VMEM((BLOCKS, H0 * BLOCK, D0), BF16),
            pltpu.VMEM((BLOCKS, 10 * C4, H0 * BLOCK), F32),
        ],
        compiler_params=vmem_params(20),
        cost_estimate=pl.CostEstimate(flops=5 * 10**9, bytes_accessed=2 * 10**7, transcendentals=10**6),
        name="backward_kernel",
    )(place, *operands)


def sum_terms(terms, out_qkv, out_out):
    total = jnp.sum(terms[...].astype(F32), axis=0)
    total = jnp.concatenate([total[:, :64], total[:, 64:]], axis=0)
    out_qkv[...] = total[:, :48]
    out_out[...] = total[:, 48:].T


def run_sum_terms(terms):
    return pl.pallas_call(
        sum_terms,
        out_shape=[jax.ShapeDtypeStruct((32, 48), F32), jax.ShapeDtypeStruct((16, 32), F32)],
        in_specs=[whole()],
        out_specs=[whole()] * 2,
        compiler_params=vmem_params(8),
        name="sum_terms",
    )(terms)


def ring(axis, step):
    devices = lax.axis_size(axis)
    return [(i, (i + step) % devices) for i in range(devices)]


def swap_edges(first, last, axis):
    before = lax.ppermute(last, axis, ring(axis, 1))
    after = lax.ppermute(first, axis, ring(axis, -1))
    return before, after


HALO = 8
TOKEN_ROWS = HALO * COLS
FINE_ROWS = 4 * COLS
FILL = 8
STRIP_ROWS = TOKEN_ROWS + FINE_ROWS + 4 * CCOLS + FILL


def row_strips(tokens, grad_fine, grad_coarse, first, last, flat, held, sems):
    fine_at = pl.ds(TOKEN_ROWS, FINE_ROWS)
    own = ROWS * COLS
    copies = [
        pltpu.make_async_copy(grad_coarse, held, sems.at[0]),
        pltpu.make_async_copy(
            tokens.at[pl.ds(0, TOKEN_ROWS)], first.at[pl.ds(0, TOKEN_ROWS)], sems.at[1]
        ),
        pltpu.make_async_copy(
            tokens.at[pl.ds(own - TOKEN_ROWS, TOKEN_ROWS)],
            last.at[pl.ds(0, TOKEN_ROWS)],
            sems.at[2],
        ),
        pltpu.make_async_copy(grad_fine.at[pl.ds(0, FINE_ROWS)], first.at[fine_at], sems.at[3]),
        pltpu.make_async_copy(
            grad_fine.at[pl.ds(own - FINE_ROWS, FINE_ROWS)], last.at[fine_at], sems.at[4]
        ),
    ]
    for copy in copies:
        copy.start()
    copies[0].wait()
    wide = held[...].astype(F32)
    rows = [wide[:, i, :] for i in range(CROWS)]
    flat[...] = jnp.concatenate(rows, axis=0).astype(BF16)
    for out, coarse in ((first, rows[0]), (last, rows[-1])):
        pieces = [coarse[:, D0 * g : D0 * (g + 1)] for g in range(4)]
        pieces.append(jnp.zeros((FILL, D0), F32))
        out[TOKEN_ROWS + FINE_ROWS :] = jnp.concatenate(pieces, axis=0).astype(BF16)
    for copy in copies[1:]:
        copy.wait()


def run_row_strips(tokens, grad_fine, grad_coarse):
    shapes = [(STRIP_ROWS, D0), (STRIP_ROWS, D0), (CROWS * CCOLS, D1)]
    operands = (tokens.reshape(-1, D0), grad_fine.reshape(-1, D0), grad_coarse.transpose(1, 0, 2))
    return pl.pallas_call(
        row_strips,
        out_shape=[jax.ShapeDtypeStruct(shape, BF16) for shape in shapes],
        in_specs=[far()] * 3,
        out_specs=[whole()] * 3,
        scratch_shapes=[
            pltpu.VMEM((CCOLS, CROWS, D1), BF16),
            pltpu.SemaphoreType.DMA((5,)),
        ],
        compiler_params=vmem_params(8),
        name="row_strips",
    )(*[in_hbm(operand) for operand in operands])


def own_columns(tokens, first, last):
    wide = tokens[...].astype(F32)
    rows = [wide[COLS * i : COLS * (i + 1)] for i in range(ROWS)]
    first[...] = jnp.concatenate([row[:HALO] for row in rows], axis=0).astype(BF16)
    last[...] = jnp.concatenate([row[-HALO:] for row in rows], axis=0).astype(BF16)


def run_own_columns(tokens):
    return pl.pallas_call(
        own_columns,
        out_shape=[jax.ShapeDtypeStruct((ROWS * HALO, D0), BF16)] * 2,
        in_specs=[whole()],
        out_specs=[whole()] * 2,
        compiler_params=vmem_params(8),
        name="own_columns",
    )(in_hbm(tokens.reshape(-1, D0)))


def column_strips(own_first, own_last, above, below, first, last):
    upper, lower = [part[:TOKEN_ROWS].astype(F32) for part in (above, below)]
    upper, lower = [
        [part[COLS * i : COLS * (i + 1)] for i in range(HALO)] for part in (upper, lower)
    ]
    for out, own, at in (
        (first, own_first, slice(0, HALO)),
        (last, own_last, slice(COLS - HALO, COLS)),
    ):
        rows = HALO * HALO
        out[:rows] = jnp.concatenate([row[at] for row in upper], axis=0).astype(BF16)
        out[rows:-rows] = own[...]
        out[-rows:] = jnp.concatenate([row[at] for row in lower], axis=0).astype(BF16)


def run_column_strips(own_first, own_last, above, below):
    return pl.pallas_call(
        column_strips,
        out_shape=[jax.ShapeDtypeStruct((R8 * HALO, D0), BF16)] * 2,
        in_specs=[whole()] * 4,
        out_specs=[whole()] * 2,
        compiler_params=vmem_params(8),
        name="column_strips",
    )(own_first, own_last, above, below)


def grads_of(own_fine, own_coarse, above, below):
    at = TOKEN_ROWS + FINE_ROWS
    fine = []
    coarse = []
    for outer in (above, below):
        outer_fine = outer[TOKEN_ROWS:at].astype(F32)
        outer_coarse = outer[at:].astype(F32)
        fine.append([outer_fine[COLS * i : COLS * (i + 1)] for i in range(4)])
        coarse.append([outer_coarse[CCOLS * g : CCOLS * (g + 1)] for g in range(4)])
    wide = own_fine[...].astype(F32)
    flat = own_coarse[...].astype(F32)
    fine_rows = fine[0] + [wide[COLS * i : COLS * (i + 1)] for i in range(ROWS)] + fine[1]
    own = [
        [flat[CCOLS * i : CCOLS * (i + 1), D0 * g : D0 * (g + 1)] for g in range(4)]
        for i in range(CROWS)
    ]
    return fine_rows, [coarse[0]] + own + [coarse[1]]


def grad_strips(own_fine, own_coarse, above, below, first, last):
    fine, coarse = grads_of(own_fine, own_coarse, above, below)
    left = [row[:4] for row in fine] + [piece[:1] for row in coarse for piece in row]
    right = [row[-4:] for row in fine] + [piece[-1:] for row in coarse for piece in row]
    left.append(jnp.zeros((FILL, D0), F32))
    right.append(jnp.zeros((FILL, D0), F32))
    first[...] = jnp.concatenate(left, axis=0).astype(BF16)
    last[...] = jnp.concatenate(right, axis=0).astype(BF16)


def run_grad_strips(own_fine, own_coarse, above, below):
    return pl.pallas_call(
        grad_strips,
        out_shape=[jax.ShapeDtypeStruct((R4 * 4 + EXT // 2 + FILL, D0), BF16)] * 2,
        in_specs=[whole()] * 4,
        out_specs=[whole()] * 2,
        compiler_params=vmem_params(8),
        name="grad_strips",
    )(own_fine, own_coarse, above, below)


def on_device(
    tokens,
    grad_fine,
    grad_coarse,
    fine_gain,
    fine_qkv,
    fine_out,
    merge_weight,
    coarse_gain,
    coarse_qkv,
    coarse_out,
):
    row = lax.axis_index("row")
    col = lax.axis_index("col")
    place = jnp.stack([row * ROWS, col * COLS, row]).astype(jnp.int32)
    first, last, grad_coarse = run_row_strips(tokens, grad_fine, grad_coarse)
    above, below = swap_edges(first, last, "row")
    columns = run_own_columns(tokens)
    left, right = swap_edges(*run_column_strips(*columns, above, below), "col")
    pieces = (tokens, above, below, left, right)
    grad_heads = jnp.dot(grad_coarse, coarse_out.T, preferred_element_type=F32).astype(BF16)
    packed = run_near(
        place,
        pieces,
        fine_gain,
        fine_qkv,
        fine_out,
        merge_weight,
        coarse_gain,
        coarse_qkv,
        grad_heads,
    )
    packed, grad_fine, grad_coarse, *pieces = lax.optimization_barrier(
        (packed, grad_fine, grad_coarse, *pieces)
    )
    every = lax.all_to_all(
        packed.reshape(8 * H1, CROWS * CCOLS, 256),
        ("row", "col"),
        split_axis=0,
        concat_axis=0,
        tiled=True,
    )
    grads = (grad_fine.reshape(-1, D0), grad_coarse, pieces[1], pieces[2])
    left, right = swap_edges(*run_grad_strips(*grads), "col")
    stash, lse, coarse = run_wide(place, pieces, fine_gain, fine_qkv, fine_out, merge_weight)
    every, left, right, stash, lse, coarse = lax.optimization_barrier(
        (every, left, right, stash, lse, coarse)
    )
    every = every.reshape(SLAB * SLABS, 256)
    edges = jnp.asarray(strip_pick(), BF16)
    own_stats = run_coarse_forward(place, every)
    stats = lax.all_to_all(own_stats, "row", split_axis=0, concat_axis=0, tiled=True)
    edge, dq_own = run_coarse_own(place, every, own_stats, edges)
    pick = jnp.asarray(block_pick(), BF16)
    tiles, near_coarse, stash, near_merge, pick = run_coarse_backward(
        place, every, stats, edges, edge, dq_own, coarse_qkv, stash, merge_weight, pick
    )
    tiles = tiles.reshape(H1, EXT, 256)
    terms = lax.all_to_all(tiles, "col", split_axis=0, concat_axis=0, tiled=True)
    grad_tokens, blocks = run_backward(
        place,
        terms,
        *grads,
        left,
        right,
        coarse,
        lse,
        coarse_gain.reshape(1, D1),
        fine_gain.reshape(1, D0),
        fine_qkv,
        fine_out,
        near_coarse,
        stash,
        pick,
        near_merge,
    )
    blocks = lax.all_to_all(blocks, ("row", "col"), split_axis=0, concat_axis=0, tiled=True)
    grad_qkv, grad_out = run_sum_terms(blocks)
    return grad_tokens.reshape(ROWS, COLS, D0), grad_qkv, grad_out.T


def solution(mesh):
    return jax.shard_map(
        on_device,
        mesh=mesh,
        in_specs=(P("row", "col", None),) * 3 + (P(),) * 7,
        out_specs=(P("row", "col", None), P("row", "col"), P("row", "col")),
        check_vma=False,
    )
```

```python
import jax
import jax.numpy as jnp
import numpy as np
from jax import lax
from jax.experimental import pallas as pl
from jax.experimental.pallas import tpu as pltpu
from jax.sharding import PartitionSpec as P

H0 = 4
H1 = 16
HEAD = 64
MERGE = 4
EPSILON = 1e-05
FAR = 1e30
D0 = 256
D1 = 1024

ROWS, COLS = 16, 24
CROWS, CCOLS = 4, 6
R8, C8 = ROWS + 16, COLS + 16
R4, C4 = ROWS + 8, COLS + 8
N4 = R4 * C4
BLOCK = 4 * C4
BLOCKS = R4 // 4
WROWS = R4 + 6
OWN = ROWS * C4
EXT = (CROWS + 2) * (CCOLS + 2)

F32 = jnp.float32
BF16 = jnp.bfloat16


def vmem_params(mib):
    return pltpu.CompilerParams(vmem_limit_bytes=mib * 1024 * 1024)


def whole():
    return pl.BlockSpec(memory_space=pltpu.VMEM)


def far():
    return pl.BlockSpec(memory_space=pltpu.HBM)


def fetch(source, target, sems, pieces):
    rows = source.shape[0] // pieces
    return [
        pltpu.make_async_copy(
            source.at[pl.ds(n * rows, rows)], target.at[pl.ds(n * rows, rows)], sems.at[n]
        )
        for n in range(pieces)
    ]


def dot(a, b, ca, cb):
    return lax.dot_general(a, b, (((ca,), (cb,)), ((), ())), preferred_element_type=F32)


def norm_forward(values):
    center = values - jnp.mean(values, axis=-1, keepdims=True)
    inverse = lax.rsqrt(jnp.mean(center * center, axis=-1, keepdims=True) + EPSILON)
    return center * inverse, inverse


def norm_backward(scaled, normed, inverse):
    return inverse * (
        scaled
        - jnp.mean(scaled, axis=-1, keepdims=True)
        - normed * jnp.mean(scaled * normed, axis=-1, keepdims=True)
    )


def head_lanes(rows):
    return lax.broadcasted_iota(jnp.int32, (rows, D0), 1) // HEAD


def stack_heads(values):
    lanes = head_lanes(values.shape[0])
    zero = jnp.zeros_like(values)
    return jnp.concatenate([jnp.where(lanes == h, values, zero) for h in range(H0)], axis=0)


def unstack_heads(stacked):
    rows = stacked.shape[0] // H0
    lanes = head_lanes(rows)
    result = stacked[:rows]
    for h in range(1, H0):
        result = jnp.where(lanes == h, stacked[h * rows : (h + 1) * rows], result)
    return result


AT_Q = 0
AT_ATT = N4
AT_K = 2 * N4
AT_V = AT_K + WROWS * C4
AT_X = AT_V + WROWS * C4
STASH = AT_X + OWN


def window_bias(key_cols, col_shift):
    shape = (10, key_cols, BLOCK)
    kr = lax.broadcasted_iota(jnp.int32, shape, 0)
    kc = lax.broadcasted_iota(jnp.int32, shape, 1)
    lane = lax.broadcasted_iota(jnp.int32, shape, 2)
    row_gap = kr - lane // C4
    col_gap = kc - lane % C4 - col_shift
    near = (row_gap >= 0) & (row_gap <= 6) & (col_gap >= 0) & (col_gap <= 6)
    return jnp.where(near, 0.0, -FAR).reshape(10 * key_cols, BLOCK)


def key_bias(key_cols, key_row, key_col):
    shape = (10, key_cols, 1)
    grid_row = key_row + lax.broadcasted_iota(jnp.int32, shape, 0)
    grid_col = key_col + lax.broadcasted_iota(jnp.int32, shape, 1)
    inside = (grid_row >= 0) & (grid_row < 128) & (grid_col >= 0) & (grid_col < 384)
    return jnp.where(inside, 0.0, -FAR).reshape(10 * key_cols, 1)


def all_heads(bias):
    return jnp.concatenate([bias] * H0, axis=1)


def near_kernel(
    place,
    tokens,
    above,
    below,
    left,
    right,
    gain,
    w_qkv,
    w_out,
    w_merge_far,
    gain_coarse,
    w_coarse_far,
    grads,
    packed_far,
    x32,
    keys,
    values,
    hid32,
    merged,
    w_merge,
    w_coarse,
    packed,
    merge_sems,
    coarse_sems,
    packed_sems,
):
    merge_copies = fetch(w_merge_far, w_merge, merge_sems, 2)
    coarse_copies = fetch(w_coarse_far, w_coarse, coarse_sems, 4)
    for copy in merge_copies + coarse_copies:
        copy.start()
    row0 = place[0]
    col0 = place[1]
    middle = [part[: 8 * COLS].astype(F32) for part in (above, below)]
    middle.insert(1, tokens[...].astype(F32))
    sides = [left[...].astype(F32), right[...].astype(F32)]
    for t in range(ROWS + 6):
        e = t + 5
        part, at = (0, e) if e < 8 else (1, e - 8) if e < 8 + ROWS else (2, e - 8 - ROWS)
        x32[C4 * t : C4 * (t + 1)] = jnp.concatenate(
            [
                sides[0][8 * e + 4 : 8 * e + 8],
                middle[part][COLS * at : COLS * (at + 1)],
                sides[1][8 * e : 8 * e + 4],
            ],
            axis=0,
        )
    normed, _ = norm_forward(x32[...])
    normed = (normed * gain[...]).astype(BF16)
    inner = slice(3 * C4, 3 * C4 + OWN)
    queries = dot(normed[inner], w_qkv[:, :D0], 1, 0).astype(BF16).astype(F32) * (HEAD**-0.5)
    keys[...] = dot(normed, w_qkv[:, D0 : 2 * D0], 1, 0).astype(BF16)
    values[...] = dot(normed, w_qkv[:, 2 * D0 :], 1, 0).astype(BF16)
    window = window_bias(C4, -3)
    for b in range(ROWS // 4):
        block = slice(BLOCK * b, BLOCK * b + 10 * C4)
        stacked = stack_heads(queries[BLOCK * b : BLOCK * (b + 1)]).astype(BF16)
        bias = all_heads(window + key_bias(C4, row0 - 3 + 4 * b, col0 - 4))
        scores = dot(keys[block], stacked, 1, 1) + bias
        maxima = jnp.max(scores, axis=0, keepdims=True)
        exponent = jnp.exp(scores - maxima)
        totals = jnp.sum(exponent, axis=0, keepdims=True)
        weights = (exponent * (1.0 / totals)).astype(BF16)
        attended = unstack_heads(dot(weights, values[block], 0, 0)).astype(BF16)
        at = BLOCK * b
        own = x32[3 * C4 + at : 3 * C4 + at + BLOCK]
        total = (own + dot(attended, w_out[...], 1, 0)).astype(BF16).astype(F32)
        hid32[0, at : at + BLOCK] = total[:, :128]
        hid32[1, at : at + BLOCK] = total[:, 128:]
    wide = CCOLS + 2
    merge_rows(hid32, merged, CROWS)
    total = None
    for n in range(4):
        if n % 2 == 0:
            merge_copies[n // 2].wait()
        part = dot(merged[:, D1 * n : D1 * (n + 1)], w_merge[D1 * n : D1 * (n + 1)], 1, 0)
        total = part if total is None else total + part
    normed, _ = norm_forward(total.astype(BF16).astype(F32))
    normed = normed * gain_coarse[...]
    parts = [normed[wide * i + 1 : wide * i + 1 + CCOLS] for i in range(CROWS)]
    normed = jnp.concatenate(parts, axis=0).astype(BF16)
    for copy in coarse_copies:
        copy.wait()
    packed_copies = []
    for n in range(4):
        result = dot(normed, w_coarse[:, 768 * n : 768 * (n + 1)], 1, 0)
        grad = grads[:, 256 * n : 256 * (n + 1)].astype(F32)
        parts = []
        for h in range(4):
            q = result[:, 192 * h : 192 * h + 64]
            k = result[:, 192 * h + 64 : 192 * h + 128]
            v = result[:, 192 * h + 128 : 192 * h + 192]
            g = grad[:, 64 * h : 64 * h + 64]
            parts.append(jnp.concatenate([k, v, q, g], axis=1))
        packed[2 * n] = jnp.concatenate(parts[:2], axis=0).astype(BF16)
        packed[2 * n + 1] = jnp.concatenate(parts[2:], axis=0).astype(BF16)
        at = pl.ds(2 * n, 2)
        for r in range(8):
            packed_copies.append(
                pltpu.make_async_copy(packed.at[at], packed_far.at[r, at], packed_sems.at[n, r])
            )
            packed_copies[-1].start()
    for copy in packed_copies:
        copy.wait()


def merge_rows(hid32, merged, count):
    for pair in range(count // 2):
        for a in range(MERGE):
            for c in range(MERGE):
                for half in range(2):
                    parts = [
                        hid32[half, pl.ds((4 * i + a) * C4 + c, CCOLS + 2, stride=MERGE), :]
                        for i in (2 * pair, 2 * pair + 1)
                    ]
                    at = (a * MERGE + c) * D0 + half * 128
                    merged[16 * pair : 16 * (pair + 1), at : at + 128] = jnp.concatenate(
                        parts, axis=0
                    ).astype(BF16)


def run_near(place, pieces, gain, w_qkv, w_out, w_merge, gain_coarse, w_coarse, grads):
    own = CROWS * CCOLS
    return pl.pallas_call(
        near_kernel,
        out_shape=pltpu.HBM((8, 8, 2 * own, 256), BF16),
        in_specs=[pl.BlockSpec(memory_space=pltpu.SMEM)]
        + [whole()] * 8
        + [far(), whole(), far(), whole()],
        out_specs=far(),
        scratch_shapes=[
            pltpu.VMEM(((ROWS + 6) * C4, D0), F32),
            pltpu.VMEM(((ROWS + 6) * C4, D0), BF16),
            pltpu.VMEM(((ROWS + 6) * C4, D0), BF16),
            pltpu.VMEM((2, OWN, 128), F32),
            pltpu.VMEM((CROWS * (CCOLS + 2), MERGE * MERGE * D0), BF16),
            pltpu.VMEM(w_merge.shape, BF16),
            pltpu.VMEM(w_coarse.shape, BF16),
            pltpu.VMEM((8, 2 * own, 256), BF16),
            pltpu.SemaphoreType.DMA((2,)),
            pltpu.SemaphoreType.DMA((4,)),
            pltpu.SemaphoreType.DMA((4, 8)),
        ],
        compiler_params=vmem_params(48),
        cost_estimate=pl.CostEstimate(flops=3 * 10**9, bytes_accessed=2 * 10**7, transcendentals=10**6),
        name="near_kernel",
    )(
        place,
        *[piece.reshape(-1, D0) for piece in pieces],
        gain.reshape(1, D0),
        w_qkv,
        w_out,
        in_hbm(w_merge),
        gain_coarse.reshape(1, D1),
        in_hbm(w_coarse),
        grads,
    )


def in_hbm(array):
    return pltpu.with_memory_space_constraint(array, pltpu.HBM)


def wide_kernel(
    place,
    tokens,
    above,
    below,
    left,
    right,
    gain,
    w_qkv,
    w_out,
    w_merge_far,
    stash_far,
    lse,
    coarse_out,
    x32,
    q32,
    k32,
    v32,
    hid32,
    stash,
    merged,
    w_merge,
    merge_sems,
    stash_sem,
):
    merge_copies = fetch(w_merge_far, w_merge, merge_sems, 4)
    for copy in merge_copies:
        copy.start()
    queries = stash.at[pl.ds(AT_Q, N4)]
    attended = stash.at[pl.ds(AT_ATT, N4)]
    keys_w = stash.at[pl.ds(AT_K, WROWS * C4)]
    values_w = stash.at[pl.ds(AT_V, WROWS * C4)]
    tokens_own = stash.at[pl.ds(AT_X, OWN)]
    row0 = place[0]
    col0 = place[1]
    middle = [part[: 8 * COLS].astype(F32) for part in (above, below)]
    middle.insert(1, tokens[...].astype(F32))
    sides = [left[...].astype(F32), right[...].astype(F32)]
    for i in range(R8):
        part, at = (0, i) if i < 8 else (1, i - 8) if i < 8 + ROWS else (2, i - 8 - ROWS)
        x32[C8 * i : C8 * i + 8] = sides[0][8 * i : 8 * i + 8]
        x32[C8 * i + 8 : C8 * i + 8 + COLS] = middle[part][COLS * at : COLS * (at + 1)]
        x32[C8 * i + 8 + COLS : C8 * (i + 1)] = sides[1][8 * i : 8 * i + 8]
    normed, _ = norm_forward(x32[...])
    normed = (normed * gain[...]).astype(BF16)
    q32[...] = dot(normed, w_qkv[:, :D0], 1, 0).astype(BF16).astype(F32) * (HEAD**-0.5)
    k32[...] = dot(normed, w_qkv[:, D0 : 2 * D0], 1, 0).astype(BF16).astype(F32)
    v32[...] = dot(normed, w_qkv[:, 2 * D0 :], 1, 0).astype(BF16).astype(F32)
    for i in range(R4):
        queries[C4 * i : C4 * (i + 1)] = q32[pl.ds((i + 4) * C8 + 4, C4), :].astype(BF16)
    for i in range(WROWS):
        keys_w[C4 * i : C4 * (i + 1)] = k32[pl.ds((i + 1) * C8 + 4, C4), :].astype(BF16)
        values_w[C4 * i : C4 * (i + 1)] = v32[pl.ds((i + 1) * C8 + 4, C4), :].astype(BF16)
    for i in range(ROWS):
        tokens_own[C4 * i : C4 * (i + 1)] = x32[pl.ds((i + 8) * C8 + 4, C4), :].astype(BF16)
    lse[...] = jnp.full(lse.shape, FAR, F32)
    window = window_bias(C8, 1)
    for b in range(BLOCKS):
        start = (4 * b + 1) * C8
        key_block = k32[start : start + 10 * C8].astype(BF16)
        value_block = v32[start : start + 10 * C8].astype(BF16)
        stacked = stack_heads(queries[BLOCK * b : BLOCK * (b + 1)].astype(F32)).astype(BF16)
        bias = all_heads(window + key_bias(C8, row0 - 7 + 4 * b, col0 - 8))
        scores = dot(key_block, stacked, 1, 1) + bias
        maxima = jnp.max(scores, axis=0, keepdims=True)
        exponent = jnp.exp(scores - maxima)
        totals = jnp.sum(exponent, axis=0, keepdims=True)
        weights = (exponent * (1.0 / totals)).astype(BF16)
        result = unstack_heads(dot(weights, value_block, 0, 0)).astype(BF16)
        attended[BLOCK * b : BLOCK * (b + 1)] = result
        lane = lax.broadcasted_iota(jnp.int32, (1, H0 * BLOCK), 1) % BLOCK
        q_row = row0 - 4 + 4 * b + lane // C4
        q_col = col0 - 4 + lane % C4
        q_in = (q_row >= 0) & (q_row < 128) & (q_col >= 0) & (q_col < 384)
        lse[b : b + 1] = jnp.where(q_in, maxima + jnp.log(totals), FAR)
        projected = dot(result, w_out[...], 1, 0)
        for a in range(4):
            own = x32[pl.ds((4 * b + a + 4) * C8 + 4, C4), :]
            total = own + projected[C4 * a : C4 * (a + 1)]
            at = BLOCK * b + C4 * a
            total = total.astype(BF16).astype(F32)
            hid32[0, at : at + C4] = total[:, :128]
            hid32[1, at : at + C4] = total[:, 128:]
    merge_rows(hid32, merged, CROWS + 2)
    stash_copy = pltpu.make_async_copy(stash, stash_far, stash_sem)
    stash_copy.start()
    total = None
    for n, copy in enumerate(merge_copies):
        copy.wait()
        part = dot(merged[:, D1 * n : D1 * (n + 1)], w_merge[D1 * n : D1 * (n + 1)], 1, 0)
        total = part if total is None else total + part
    coarse_out[...] = total.astype(BF16)
    stash_copy.wait()


def run_wide(place, pieces, gain, w_qkv, w_out, w_merge):
    flat = R8 * C8
    return pl.pallas_call(
        wide_kernel,
        out_shape=[
            pltpu.HBM((STASH, D0), BF16),
            pltpu.HBM((8, H0 * BLOCK), F32),
            pltpu.HBM((EXT, D1), BF16),
        ],
        in_specs=[pl.BlockSpec(memory_space=pltpu.SMEM)] + [whole()] * 8 + [far()],
        out_specs=[far(), whole(), whole()],
        scratch_shapes=[pltpu.VMEM((flat, D0), F32)] * 4
        + [
            pltpu.VMEM((2, N4, 128), F32),
            pltpu.VMEM((STASH, D0), BF16),
            pltpu.VMEM((EXT, MERGE * MERGE * D0), BF16),
            pltpu.VMEM(w_merge.shape, BF16),
            pltpu.SemaphoreType.DMA((4,)),
            pltpu.SemaphoreType.DMA(()),
        ],
        compiler_params=vmem_params(40),
        cost_estimate=pl.CostEstimate(flops=3 * 10**9, bytes_accessed=10**7, transcendentals=10**6),
        name="wide_kernel",
    )(
        place,
        *[piece.reshape(-1, D0) for piece in pieces],
        gain.reshape(1, D0),
        w_qkv,
        w_out,
        in_hbm(w_merge),
    )


def lane_half(values, low):
    lanes = lax.broadcasted_iota(jnp.int32, values.shape, 1)
    keep = lanes < HEAD if low else lanes >= HEAD
    return jnp.where(keep, values, jnp.zeros_like(values))


SLAB = 384
SLABS = 8
STRIP = 96
EDGE = SLAB + 2 * STRIP


def strip_pick():
    tile, j = np.divmod(np.arange(STRIP), CCOLS)
    pick = np.zeros((2, STRIP, SLAB), np.float32)
    last = (CROWS - 1) * CCOLS
    pick[0, np.arange(STRIP), tile * CROWS * CCOLS + last + j] = 1
    pick[1, np.arange(STRIP), tile * CROWS * CCOLS + j] = 1
    return pick


def tile_pick():
    c, i, j = np.meshgrid(np.arange(H1), np.arange(6), np.arange(8), indexing="ij")
    tile = (c + (j == 7) - (j == 0)) % H1
    jj = np.where(j == 0, 5, np.where(j == 7, 0, j - 1))
    middle = tile * 24 + (i - 1) * 6 + jj
    source = np.where(i == 0, SLAB + tile * 6 + jj, np.where(i == 5, SLAB + STRIP + tile * 6 + jj, middle))
    pick = np.zeros((H1 * EXT, EDGE), np.float32)
    pick[np.arange(H1 * EXT), source.reshape(-1)] = 1
    return pick


def coarse_forward(place, every, stats, scores_ref):
    keyval = every[:, :128]
    own = every[pl.ds(pl.multiple_of(place[2] * SLAB, SLAB), SLAB), 128:]
    queries = lane_half(own.astype(F32) * (HEAD**-0.5), True).astype(BF16)
    columns = []
    for b in range(3):
        rows = slice(128 * b, 128 * (b + 1))
        scores_ref[b] = dot(queries[rows], keyval, 1, 1)
        maxima = jnp.max(scores_ref[b], axis=1, keepdims=True)
        exponent = jnp.exp(scores_ref[b] - maxima)
        totals = jnp.sum(exponent, axis=1, keepdims=True)
        attended = dot(exponent.astype(BF16), keyval, 1, 0) * (1.0 / totals)
        attended = attended.astype(BF16).astype(F32)
        product = lane_half(own[rows].astype(F32) * attended, False)
        columns.append((maxima + jnp.log(totals), jnp.sum(product, axis=1, keepdims=True)))
    lane = lax.broadcasted_iota(jnp.int32, (128, 128), 1)
    turned = [
        jnp.where(lane == 0, log, jnp.where(lane == 1, stat, 0.0)).T for log, stat in columns
    ]
    result = jnp.concatenate(
        [t[0:1] for t in turned] + [t[1:2] for t in turned] + [jnp.zeros((2, 128), F32)], axis=0
    )
    for r in range(SLABS):
        stats[r] = result


def run_coarse_forward(place, every):
    return pl.pallas_call(
        coarse_forward,
        out_shape=jax.ShapeDtypeStruct((SLABS, 8, 128), F32),
        in_specs=[pl.BlockSpec(memory_space=pltpu.SMEM), whole()],
        out_specs=whole(),
        scratch_shapes=[pltpu.VMEM((3, 128, SLAB * SLABS), F32)],
        compiler_params=vmem_params(16),
        cost_estimate=pl.CostEstimate(flops=10**9, bytes_accessed=2 * 10**6, transcendentals=10**6),
        name="coarse_forward",
    )(place, every)


def stat_rows(stats):
    lse = jnp.concatenate([stats[k : k + 1] for k in range(3)], axis=1)
    stat = jnp.concatenate([stats[k : k + 1] for k in range(3, 6)], axis=1)
    return lse, stat


def slab_rows(index):
    return pl.ds(pl.multiple_of(index * SLAB, SLAB), SLAB)


def turn(lse, stat):
    filler = jnp.zeros((128 - 2, lse.shape[1]), F32)
    turned = jnp.concatenate([lse, stat, filler], axis=0).T
    return turned[:, 0:1], turned[:, 1:2]


def query_side(every, rows, queries, grads, lse, stat):
    keyval = every[rows, :128]
    probs = jnp.exp(dot(queries, keyval, 1, 1) - lse)
    slopes = (probs * (dot(grads, keyval, 1, 1) - stat)).astype(BF16)
    return dot(slopes, keyval, 1, 0)


def halves(pair):
    wide = pair.astype(F32)
    return lane_half(wide * (HEAD**-0.5), True).astype(BF16), lane_half(wide, False).astype(BF16)


def coarse_own(place, every, stats, strips, edge, dq_out, dq_ref):
    row = place[2]
    edge[:SLAB] = every[slab_rows(row)]
    others = (lax.rem(row + SLABS - 1, SLABS), lax.rem(row + 1, SLABS))
    for k, other in enumerate(others):
        at = SLAB + STRIP * k
        edge[at : at + STRIP] = dot(strips[k], every[slab_rows(other)], 1, 0).astype(BF16)
    lse, stat = turn(*stat_rows(stats[0]))
    queries, grads = halves(edge[:SLAB, 128:])
    for n in range(SLABS // 2):
        rows = slice(2 * n * SLAB, 2 * (n + 1) * SLAB)
        term = query_side(every, rows, queries, grads, lse, stat)
        dq_ref[...] = term if n == 0 else dq_ref[...] + term
    dq_out[...] = (dq_ref[...] * (HEAD**-0.5)).astype(BF16)


def run_coarse_own(place, every, stats, strips):
    return pl.pallas_call(
        coarse_own,
        out_shape=[
            pltpu.HBM((EDGE, 256), BF16),
            pltpu.HBM((SLAB, 128), BF16),
        ],
        in_specs=[pl.BlockSpec(memory_space=pltpu.SMEM)] + [whole()] * 3,
        out_specs=[whole()] * 2,
        scratch_shapes=[pltpu.VMEM((SLAB, 128), F32)],
        compiler_params=vmem_params(24),
        cost_estimate=pl.CostEstimate(flops=10**9, bytes_accessed=2 * 10**6, transcendentals=10**6),
        name="coarse_own",
    )(place, every, stats, strips)


def coarse_backward(
    place,
    every,
    stats,
    strips,
    edge,
    dq_own,
    tiles_far,
    coarse_far,
    stash_far,
    merge_far,
    pick_far,
    out,
    w_coarse,
    stash,
    w_merge,
    pick,
    dq_ref,
    dk_ref,
    dv_ref,
    tiles,
    sems,
):
    pairs = (
        (tiles_far, tiles, 1),
        (coarse_far, w_coarse, 2),
        (stash_far, stash, 1),
        (merge_far, w_merge, 2),
        (pick_far, pick, 1),
    )
    copies = []
    for n, (source, target, pieces) in enumerate(pairs):
        copies += fetch(source, target, sems.at[n], pieces)
    for copy in copies:
        copy.start()
    row = place[2]
    others = (lax.rem(row + SLABS - 1, SLABS), lax.rem(row + 1, SLABS))
    taken = []
    for k, other in enumerate(others):
        both = jnp.concatenate(stat_rows(stats[other]) + (jnp.zeros((6, SLAB), F32),), axis=0)
        taken.append(
            lax.dot_general(
                both,
                strips[k].astype(F32),
                (((1,), (1,)), ((), ())),
                precision=lax.Precision.HIGHEST,
                preferred_element_type=F32,
            )
        )
    strip_lse, strip_stat = turn(
        jnp.concatenate([t[0:1] for t in taken], axis=1),
        jnp.concatenate([t[1:2] for t in taken], axis=1),
    )
    edge_k, edge_v = halves(edge[:, :128])
    edge_q, edge_g = halves(edge[SLAB:, 128:])
    for n in range(SLABS // 2):
        rows = slice(2 * n * SLAB, 2 * (n + 1) * SLAB)
        dq = query_side(every, rows, edge_q, edge_g, strip_lse, strip_stat)
        query = every[rows, 128:]
        both = [stat_rows(stats[2 * n + k]) for k in range(2)]
        lse = jnp.concatenate([pair[0] for pair in both], axis=1)
        stat = jnp.concatenate([pair[1] for pair in both], axis=1)
        probs = jnp.exp(dot(edge_k, query, 1, 1) - lse)
        slopes = (probs * (dot(edge_v, query, 1, 1) - stat)).astype(BF16)
        dk = dot(slopes, query, 1, 0)
        dv = dot(probs.astype(BF16), query, 1, 0)
        if n == 0:
            dq_ref[...] = dq
            dk_ref[...] = dk
            dv_ref[...] = dv
        else:
            dq_ref[...] += dq
            dk_ref[...] += dk
            dv_ref[...] += dv
    lanes = lax.broadcasted_iota(jnp.int32, (EDGE, 128), 1)
    keyval = jnp.where(lanes < HEAD, dk_ref[...] * (HEAD**-0.5), dv_ref[...]).astype(BF16)
    query = jnp.concatenate(
        [dq_own[...], (dq_ref[...] * (HEAD**-0.5)).astype(BF16)], axis=0
    )
    copies[0].wait()
    out[...] = dot(tiles[...], jnp.concatenate([keyval, query], axis=1), 1, 0).astype(BF16)
    for copy in copies[1:]:
        copy.wait()


def run_coarse_backward(place, every, stats, strips, edge, dq_own, *later):
    tiles = jnp.asarray(tile_pick(), BF16)
    return pl.pallas_call(
        coarse_backward,
        out_shape=[pltpu.HBM((H1 * EXT, 256), BF16)]
        + [pltpu.VMEM(array.shape, array.dtype) for array in later],
        in_specs=[pl.BlockSpec(memory_space=pltpu.SMEM)] + [whole()] * 5 + [far()] * 5,
        out_specs=[whole()] * 5,
        scratch_shapes=[
            pltpu.VMEM((2 * STRIP, 128), F32),
            pltpu.VMEM((EDGE, 128), F32),
            pltpu.VMEM((EDGE, 128), F32),
            pltpu.VMEM(tiles.shape, BF16),
            pltpu.SemaphoreType.DMA((5, 4)),
        ],
        compiler_params=vmem_params(16),
        cost_estimate=pl.CostEstimate(flops=3 * 10**9, bytes_accessed=2 * 10**6, transcendentals=4 * 10**6),
        name="coarse_backward",
    )(
        place,
        every,
        stats,
        strips,
        in_hbm(edge),
        in_hbm(dq_own),
        *[in_hbm(array) for array in (tiles,) + later],
    )


def block_pick():
    c, b = np.meshgrid(np.arange(H1), np.arange(64), indexing="ij")
    source = np.where(b < 48, 48 * c + b, 3 * D0 + 16 * c + b - 48).reshape(-1)
    pick = np.zeros((4 * D0, 4 * D0), np.float32)
    pick[source, np.arange(4 * D0)] = 1
    return pick


def merged_order(back):
    rows = lax.broadcasted_iota(jnp.int32, (BLOCK, BLOCK), 0)
    cols = lax.broadcasted_iota(jnp.int32, (BLOCK, BLOCK), 1)
    merged, grid = (cols, rows) if back else (rows, cols)
    a = merged // C4
    c = merged // 8 % MERGE
    j = merged % 8
    return (grid == a * C4 + j * MERGE + c).astype(F32).astype(BF16)


def backward_kernel(
    place,
    terms_coarse,
    own_fine,
    own_coarse,
    above,
    below,
    grads_left,
    grads_right,
    coarse,
    lse,
    gain_coarse,
    gain,
    w_qkv,
    w_out,
    w_coarse,
    stash,
    pick_block,
    w_merge,
    grad_tokens,
    terms,
    grad_fine,
    sp32,
    gh_ref,
    ga_ref,
    dq_ref,
    dk_ref,
    dv_ref,
    gt_ref,
    stack_ref,
    probs_ref,
):
    queries = stash.at[pl.ds(AT_Q, N4)]
    attended = stash.at[pl.ds(AT_ATT, N4)]
    keys_w = stash.at[pl.ds(AT_K, WROWS * C4)]
    values_w = stash.at[pl.ds(AT_V, WROWS * C4)]
    tokens_own = stash.at[pl.ds(AT_X, OWN)]
    row0 = place[0]
    col0 = place[1]
    wide = CCOLS + 2
    fine_rows, coarse_rows = grads_of(own_fine, own_coarse, above, below)
    side = [part[...].astype(F32) for part in (grads_left, grads_right)]
    for i, row in enumerate(fine_rows):
        outer = [part[4 * i : 4 * (i + 1)] for part in side]
        grad_fine[C4 * i : C4 * (i + 1)] = jnp.concatenate([outer[0], row, outer[1]], axis=0)
    grad_coarse = []
    for i, row in enumerate(coarse_rows):
        parts = []
        for g, piece in enumerate(row):
            at = 4 * R4 + 4 * i + g
            outer = [part[at : at + 1] for part in side]
            parts.append(jnp.concatenate([outer[0], piece, outer[1]], axis=0))
        grad_coarse.append(jnp.concatenate(parts, axis=1))
    grad_coarse = jnp.concatenate(grad_coarse, axis=0)
    parts = []
    for h in range(H1):
        block = terms_coarse[h].astype(F32)
        parts += [block[:, 128:192], block[:, :128]]
    heads = jnp.concatenate(parts, axis=1).astype(BF16)
    upstream = dot(heads, w_coarse[...], 1, 1) * gain_coarse[...]
    normed, inverse = norm_forward(coarse[...].astype(F32))
    back = norm_backward(upstream, normed, inverse)
    change = (grad_coarse + back).astype(BF16)
    for a in range(MERGE):
        sp32[a] = dot(change, w_merge[D1 * a : D1 * (a + 1)], 1, 1)
    window = window_bias(C4, -3)
    for b in range(BLOCKS):
        stacked = stack_heads(queries[BLOCK * b : BLOCK * (b + 1)].astype(F32)).astype(BF16)
        stack_ref[b] = stacked
        bias = all_heads(window + key_bias(C4, row0 - 7 + 4 * b, col0 - 4))
        scores = dot(keys_w[BLOCK * b : BLOCK * b + 10 * C4], stacked, 1, 1) + bias
        probs_ref[b] = jnp.exp(scores - lse[b : b + 1])
    to_merged = merged_order(False)
    to_grid = merged_order(True)
    for i in range(CROWS + 2):
        block = slice(BLOCK * i, BLOCK * (i + 1))
        rows = slice(wide * i, wide * (i + 1))
        spread = [
            sp32[a, rows, D0 * c : D0 * (c + 1)] for a in range(MERGE) for c in range(MERGE)
        ]
        total = dot(to_merged, grad_fine[block].astype(BF16), 1, 0) + jnp.concatenate(spread, axis=0)
        gh_ref[block] = dot(to_grid, total.astype(BF16), 1, 0).astype(BF16)
    ga_ref[...] = dot(gh_ref[...], w_out[...], 1, 1).astype(BF16)
    dk_ref[...] = jnp.zeros_like(dk_ref)
    dv_ref[...] = jnp.zeros_like(dv_ref)
    pick = (
        lax.broadcasted_iota(jnp.int32, (8, D0), 1) // HEAD
        == lax.broadcasted_iota(jnp.int32, (8, D0), 0)
    ).astype(F32).astype(BF16)
    for b in range(BLOCKS):
        at = slice(BLOCK * b, BLOCK * (b + 1))
        keep = slice(BLOCK * b, BLOCK * b + 10 * C4)
        grad = ga_ref[at].astype(F32)
        product = grad * attended[at].astype(F32)
        upper = product.astype(BF16)
        lower = (product - upper.astype(F32)).astype(BF16)
        sums = dot(pick, upper, 1, 1) + dot(pick, lower, 1, 1)
        stat = jnp.concatenate([sums[h : h + 1] for h in range(H0)], axis=1)
        stack_q = stack_ref[b]
        stack_g = stack_heads(grad).astype(BF16)
        key_block = keys_w[keep]
        probs = probs_ref[b]
        slopes = (probs * (dot(values_w[keep], stack_g, 1, 1) - stat)).astype(BF16)
        dk_ref[keep] += dot(slopes, stack_q, 1, 0)
        dv_ref[keep] += dot(probs.astype(BF16), stack_g, 1, 0)
        if 1 <= b <= 4:
            dq = unstack_heads(dot(slopes, key_block, 0, 0)) * (HEAD**-0.5)
            dq_ref[BLOCK * (b - 1) : BLOCK * b] = dq.astype(BF16)
    own = slice(7 * C4, 7 * C4 + OWN)
    grads = jnp.concatenate(
        [dq_ref[...], dk_ref[own].astype(BF16), dv_ref[own].astype(BF16)], axis=1
    )
    column = lax.broadcasted_iota(jnp.int32, (ROWS, C4, D0), 1).reshape(OWN, D0)
    in_tile = (column >= 4) & (column < 4 + COLS)
    normed, inverse = norm_forward(tokens_own[...].astype(F32))
    rounded = jnp.where(in_tile, normed * gain[...], 0.0).astype(BF16)
    term_qkv = dot(rounded, grads, 0, 0).astype(BF16)
    inner = slice(BLOCK, BLOCK + OWN)
    att = jnp.where(in_tile, attended[inner].astype(F32), 0.0).astype(BF16)
    term_out = dot(att, gh_ref[inner], 0, 0).astype(BF16)
    both = dot(jnp.concatenate([term_qkv, term_out], axis=1), pick_block[...], 1, 0)
    low = lax.broadcasted_iota(jnp.int32, (16, 128), 1) < 64
    for r in range(8):
        for m in range(8):
            first = both[32 * r : 32 * r + 16, 128 * m : 128 * (m + 1)]
            last = both[32 * r + 16 : 32 * (r + 1), 128 * m : 128 * (m + 1)]
            terms[16 * r + 2 * m] = jnp.where(low, first, pltpu.roll(last, 64, 1)).astype(BF16)
            terms[16 * r + 2 * m + 1] = jnp.where(low, pltpu.roll(first, 64, 1), last).astype(BF16)
    upstream = dot(grads, w_qkv[...], 1, 1) * gain[...]
    gt_ref[...] = gh_ref[inner].astype(F32) + norm_backward(upstream, normed, inverse)
    for pair in range(ROWS // 2):
        parts = [gt_ref[pl.ds(i * C4 + 4, COLS), :] for i in (2 * pair, 2 * pair + 1)]
        grad_tokens[2 * COLS * pair : 2 * COLS * (pair + 1)] = jnp.concatenate(
            parts, axis=0
        ).astype(BF16)


def run_backward(place, *operands):
    shapes = [((ROWS * COLS, D0), BF16), ((128, 16, 128), BF16)]
    return pl.pallas_call(
        backward_kernel,
        out_shape=[jax.ShapeDtypeStruct(s, d) for s, d in shapes],
        in_specs=[pl.BlockSpec(memory_space=pltpu.SMEM)] + [whole()] * 17,
        out_specs=[whole()] * 2,
        scratch_shapes=[
            pltpu.VMEM((N4, D0), F32),
            pltpu.VMEM((MERGE, EXT, D1), F32),
            pltpu.VMEM((N4, D0), BF16),
            pltpu.VMEM((N4, D0), BF16),
            pltpu.VMEM((OWN, D0), BF16),
            pltpu.VMEM((WROWS * C4, D0), F32),
            pltpu.VMEM((WROWS * C4, D0), F32),
            pltpu.VMEM((OWN, D0), F32),
            pltpu.VMEM((BLOCKS, H0 * BLOCK, D0), BF16),
            pltpu.VMEM((BLOCKS, 10 * C4, H0 * BLOCK), F32),
        ],
        compiler_params=vmem_params(20),
        cost_estimate=pl.CostEstimate(flops=5 * 10**9, bytes_accessed=2 * 10**7, transcendentals=10**6),
        name="backward_kernel",
    )(place, *operands)


def sum_terms(terms, out_qkv, out_out):
    total = jnp.sum(terms[...].astype(F32), axis=0)
    total = jnp.concatenate([total[:, :64], total[:, 64:]], axis=0)
    out_qkv[...] = total[:, :48]
    out_out[...] = total[:, 48:].T


def run_sum_terms(terms):
    return pl.pallas_call(
        sum_terms,
        out_shape=[jax.ShapeDtypeStruct((32, 48), F32), jax.ShapeDtypeStruct((16, 32), F32)],
        in_specs=[whole()],
        out_specs=[whole()] * 2,
        compiler_params=vmem_params(8),
        name="sum_terms",
    )(terms)


def ring(axis, step):
    devices = lax.axis_size(axis)
    return [(i, (i + step) % devices) for i in range(devices)]


def swap_edges(first, last, axis):
    before = lax.ppermute(last, axis, ring(axis, 1))
    after = lax.ppermute(first, axis, ring(axis, -1))
    return before, after


HALO = 8
TOKEN_ROWS = HALO * COLS
FINE_ROWS = 4 * COLS
FILL = 8
STRIP_ROWS = TOKEN_ROWS + FINE_ROWS + 4 * CCOLS + FILL


def row_strips(tokens, grad_fine, grad_coarse, first, last, flat, held, sems):
    fine_at = pl.ds(TOKEN_ROWS, FINE_ROWS)
    own = ROWS * COLS
    copies = [
        pltpu.make_async_copy(grad_coarse, held, sems.at[0]),
        pltpu.make_async_copy(
            tokens.at[pl.ds(0, TOKEN_ROWS)], first.at[pl.ds(0, TOKEN_ROWS)], sems.at[1]
        ),
        pltpu.make_async_copy(
            tokens.at[pl.ds(own - TOKEN_ROWS, TOKEN_ROWS)],
            last.at[pl.ds(0, TOKEN_ROWS)],
            sems.at[2],
        ),
        pltpu.make_async_copy(grad_fine.at[pl.ds(0, FINE_ROWS)], first.at[fine_at], sems.at[3]),
        pltpu.make_async_copy(
            grad_fine.at[pl.ds(own - FINE_ROWS, FINE_ROWS)], last.at[fine_at], sems.at[4]
        ),
    ]
    for copy in copies:
        copy.start()
    copies[0].wait()
    wide = held[...].astype(F32)
    rows = [wide[:, i, :] for i in range(CROWS)]
    flat[...] = jnp.concatenate(rows, axis=0).astype(BF16)
    for out, coarse in ((first, rows[0]), (last, rows[-1])):
        pieces = [coarse[:, D0 * g : D0 * (g + 1)] for g in range(4)]
        pieces.append(jnp.zeros((FILL, D0), F32))
        out[TOKEN_ROWS + FINE_ROWS :] = jnp.concatenate(pieces, axis=0).astype(BF16)
    for copy in copies[1:]:
        copy.wait()


def run_row_strips(tokens, grad_fine, grad_coarse):
    shapes = [(STRIP_ROWS, D0), (STRIP_ROWS, D0), (CROWS * CCOLS, D1)]
    operands = (tokens.reshape(-1, D0), grad_fine.reshape(-1, D0), grad_coarse.transpose(1, 0, 2))
    return pl.pallas_call(
        row_strips,
        out_shape=[jax.ShapeDtypeStruct(shape, BF16) for shape in shapes],
        in_specs=[far()] * 3,
        out_specs=[whole()] * 3,
        scratch_shapes=[
            pltpu.VMEM((CCOLS, CROWS, D1), BF16),
            pltpu.SemaphoreType.DMA((5,)),
        ],
        compiler_params=vmem_params(8),
        name="row_strips",
    )(*[in_hbm(operand) for operand in operands])


def own_columns(tokens, first, last):
    wide = tokens[...].astype(F32)
    rows = [wide[COLS * i : COLS * (i + 1)] for i in range(ROWS)]
    first[...] = jnp.concatenate([row[:HALO] for row in rows], axis=0).astype(BF16)
    last[...] = jnp.concatenate([row[-HALO:] for row in rows], axis=0).astype(BF16)


def run_own_columns(tokens):
    return pl.pallas_call(
        own_columns,
        out_shape=[jax.ShapeDtypeStruct((ROWS * HALO, D0), BF16)] * 2,
        in_specs=[whole()],
        out_specs=[whole()] * 2,
        compiler_params=vmem_params(8),
        name="own_columns",
    )(in_hbm(tokens.reshape(-1, D0)))


def column_strips(own_first, own_last, above, below, first, last):
    upper, lower = [part[:TOKEN_ROWS].astype(F32) for part in (above, below)]
    upper, lower = [
        [part[COLS * i : COLS * (i + 1)] for i in range(HALO)] for part in (upper, lower)
    ]
    for out, own, at in (
        (first, own_first, slice(0, HALO)),
        (last, own_last, slice(COLS - HALO, COLS)),
    ):
        rows = HALO * HALO
        out[:rows] = jnp.concatenate([row[at] for row in upper], axis=0).astype(BF16)
        out[rows:-rows] = own[...]
        out[-rows:] = jnp.concatenate([row[at] for row in lower], axis=0).astype(BF16)


def run_column_strips(own_first, own_last, above, below):
    return pl.pallas_call(
        column_strips,
        out_shape=[jax.ShapeDtypeStruct((R8 * HALO, D0), BF16)] * 2,
        in_specs=[whole()] * 4,
        out_specs=[whole()] * 2,
        compiler_params=vmem_params(8),
        name="column_strips",
    )(own_first, own_last, above, below)


def grads_of(own_fine, own_coarse, above, below):
    at = TOKEN_ROWS + FINE_ROWS
    fine = []
    coarse = []
    for outer in (above, below):
        outer_fine = outer[TOKEN_ROWS:at].astype(F32)
        outer_coarse = outer[at:].astype(F32)
        fine.append([outer_fine[COLS * i : COLS * (i + 1)] for i in range(4)])
        coarse.append([outer_coarse[CCOLS * g : CCOLS * (g + 1)] for g in range(4)])
    wide = own_fine[...].astype(F32)
    flat = own_coarse[...].astype(F32)
    fine_rows = fine[0] + [wide[COLS * i : COLS * (i + 1)] for i in range(ROWS)] + fine[1]
    own = [
        [flat[CCOLS * i : CCOLS * (i + 1), D0 * g : D0 * (g + 1)] for g in range(4)]
        for i in range(CROWS)
    ]
    return fine_rows, [coarse[0]] + own + [coarse[1]]


def grad_strips(own_fine, own_coarse, above, below, first, last):
    fine, coarse = grads_of(own_fine, own_coarse, above, below)
    left = [row[:4] for row in fine] + [piece[:1] for row in coarse for piece in row]
    right = [row[-4:] for row in fine] + [piece[-1:] for row in coarse for piece in row]
    left.append(jnp.zeros((FILL, D0), F32))
    right.append(jnp.zeros((FILL, D0), F32))
    first[...] = jnp.concatenate(left, axis=0).astype(BF16)
    last[...] = jnp.concatenate(right, axis=0).astype(BF16)


def run_grad_strips(own_fine, own_coarse, above, below):
    return pl.pallas_call(
        grad_strips,
        out_shape=[jax.ShapeDtypeStruct((R4 * 4 + EXT // 2 + FILL, D0), BF16)] * 2,
        in_specs=[whole()] * 4,
        out_specs=[whole()] * 2,
        compiler_params=vmem_params(8),
        name="grad_strips",
    )(own_fine, own_coarse, above, below)


def on_device(
    tokens,
    grad_fine,
    grad_coarse,
    fine_gain,
    fine_qkv,
    fine_out,
    merge_weight,
    coarse_gain,
    coarse_qkv,
    coarse_out,
):
    row = lax.axis_index("row")
    col = lax.axis_index("col")
    place = jnp.stack([row * ROWS, col * COLS, row]).astype(jnp.int32)
    first, last, grad_coarse = run_row_strips(tokens, grad_fine, grad_coarse)
    above, below = swap_edges(first, last, "row")
    columns = run_own_columns(tokens)
    left, right = swap_edges(*run_column_strips(*columns, above, below), "col")
    pieces = (tokens, above, below, left, right)
    grad_heads = jnp.dot(grad_coarse, coarse_out.T, preferred_element_type=F32).astype(BF16)
    packed = run_near(
        place,
        pieces,
        fine_gain,
        fine_qkv,
        fine_out,
        merge_weight,
        coarse_gain,
        coarse_qkv,
        grad_heads,
    )
    packed, grad_fine, grad_coarse, *pieces = lax.optimization_barrier(
        (packed, grad_fine, grad_coarse, *pieces)
    )
    every = lax.all_to_all(
        packed.reshape(8 * H1, CROWS * CCOLS, 256),
        ("row", "col"),
        split_axis=0,
        concat_axis=0,
        tiled=True,
    )
    grads = (grad_fine.reshape(-1, D0), grad_coarse, pieces[1], pieces[2])
    left, right = swap_edges(*run_grad_strips(*grads), "col")
    stash, lse, coarse = run_wide(place, pieces, fine_gain, fine_qkv, fine_out, merge_weight)
    every, left, right, stash, lse, coarse = lax.optimization_barrier(
        (every, left, right, stash, lse, coarse)
    )
    every = every.reshape(SLAB * SLABS, 256)
    edges = jnp.asarray(strip_pick(), BF16)
    own_stats = run_coarse_forward(place, every)
    stats = lax.all_to_all(own_stats, "row", split_axis=0, concat_axis=0, tiled=True)
    edge, dq_own = run_coarse_own(place, every, own_stats, edges)
    pick = jnp.asarray(block_pick(), BF16)
    tiles, near_coarse, stash, near_merge, pick = run_coarse_backward(
        place, every, stats, edges, edge, dq_own, coarse_qkv, stash, merge_weight, pick
    )
    tiles = tiles.reshape(H1, EXT, 256)
    terms = lax.all_to_all(tiles, "col", split_axis=0, concat_axis=0, tiled=True)
    grad_tokens, blocks = run_backward(
        place,
        terms,
        *grads,
        left,
        right,
        coarse,
        lse,
        coarse_gain.reshape(1, D1),
        fine_gain.reshape(1, D0),
        fine_qkv,
        fine_out,
        near_coarse,
        stash,
        pick,
        near_merge,
    )
    blocks = lax.all_to_all(blocks, ("row", "col"), split_axis=0, concat_axis=0, tiled=True)
    grad_qkv, grad_out = run_sum_terms(blocks)
    return grad_tokens.reshape(ROWS, COLS, D0), grad_qkv, grad_out.T


def solution(mesh):
    return jax.shard_map(
        on_device,
        mesh=mesh,
        in_specs=(P("row", "col", None),) * 3 + (P(),) * 7,
        out_specs=(P("row", "col", None), P("row", "col"), P("row", "col")),
        check_vma=False,
    )
```
